32 devices in a mesh: section: 2 (over x), dp: 4 (over z), tensor: 4 (over y, core).
Axes of the slice: x: 2, y: 2, z: 4, core: 2. Of those that a mesh axis runs over, the one named last changes fastest.
Arguments:
- norm_in: bfloat16 [2, 512, 8192], P('section', 'dp', 'tensor'), may hold values from -20 to 20
- query_grad: bfloat16 [2, 512, 4096], P('section', 'dp', 'tensor'), may hold values from -20 to 20
- attn_out: bfloat16 [2, 512, 4096], P('section', 'dp', 'tensor'), may hold values from -20 to 20
- handed: bfloat16 [2, 512, 8192], P('section', 'dp', 'tensor'), may hold values from -20 to 20
- sketch_q: bfloat16 [2, 64, 4096], P('section', None, 'tensor'), may hold values from -6 to 6
- sketch_o: bfloat16 [2, 64, 8192], P('section', None, 'tensor'), may hold values from -6 to 6
Outputs:
- lora_b_q: bfloat16 [2, 64, 8192], P('section', None, 'tensor')
- lora_a_q: float32 [2, 64, 4096], P('section', None, 'tensor')
- lora_b_o: bfloat16 [2, 64, 4096], P('section', None, 'tensor')
- lora_a_o: float32 [2, 64, 8192], P('section', None, 'tensor')
The draws below stay inside these ranges and needn't reach their ends.
All inputs are finite; a program needn't handle non-finite values.
Results may differ from the reference program's by a relative error of at most 0.03.
Values may be sent and summed in bfloat16 or wider, within the bound.
No kernel may reach another device: no remote copies, remote signals or barrier semaphores. Data moves between devices by JAX's collectives and lax.ppermute only.
A program may use at most 64 MiB of HBM per device.

```python
import math
import jax
import jax.numpy as jnp
from jax import lax

D = 8192
HQ = 4096
RANK = 64
POWER = 2
TOK_DEV = 128
TOKENS = 512
SECTIONS = 2
N_DP = 4


def scaled_field(key, full_shape):
    key_rows, key_noise = jax.random.split(key, 2)
    columns = full_shape[-1]
    col_scale = jnp.exp(jnp.arange(columns, dtype=jnp.float32) * (math.log(3.0) / (columns - 1)))
    row_scale = jnp.exp(jax.random.uniform(key_rows, full_shape[:-1] + (1,), minval=0.0, maxval=math.log(2.5)))
    noise = jnp.clip(jax.random.normal(key_noise, full_shape), -6.0, 6.0)
    return (0.3 * noise * row_scale * col_scale).astype(jnp.bfloat16)


def draw_norm_in(key, part):
    return scaled_field(jax.random.fold_in(key, 11), (SECTIONS, TOKENS, D))


def draw_query_grad(key, part):
    return scaled_field(jax.random.fold_in(key, 12), (SECTIONS, TOKENS, HQ))


def draw_attn_out(key, part):
    return scaled_field(jax.random.fold_in(key, 13), (SECTIONS, TOKENS, HQ))


def draw_handed(key, part):
    return scaled_field(jax.random.fold_in(key, 14), (SECTIONS, TOKENS, D))


def block_scale(rng, dims, pieces, low, top_value):
    def one(position, parts):
        steps = jax.random.uniform(jax.random.fold_in(jax.random.fold_in(rng, 6), position), (parts,), jnp.float32, low / len(pieces), top_value / len(pieces))
        return jnp.repeat(jnp.exp(steps), dims[position] // parts).reshape((-1,) + (1,) * (len(dims) - position - 1))

    gain = one(*pieces[0])
    for cut in pieces[1:]:
        gain = gain * one(*cut)
    return gain


def gaussian(key, extent, spread, bound, pieces=(), held_as=jnp.bfloat16):
    drawn = spread * jax.random.normal(key, extent, jnp.float32)
    if pieces:
        drawn = drawn * block_scale(key, extent, pieces, -0.22, 0.18)
    return jnp.clip(drawn, -bound, bound).astype(held_as)


def setup_inputs(seed: int = 0) -> dict:
    seeds = jax.random.split(jax.random.key(seed), 7)
    norm_in = draw_norm_in(jax.random.fold_in(seeds[6], 71), 0)
    query_grad = draw_query_grad(jax.random.fold_in(seeds[6], 71), 0)
    attn_out = draw_attn_out(jax.random.fold_in(seeds[6], 71), 0)
    handed = draw_handed(jax.random.fold_in(seeds[6], 71), 0)
    sketch_q = gaussian(seeds[4], (SECTIONS, RANK, HQ), 1.0, 6.0, ((0, 2), (2, 4)))
    sketch_o = gaussian(seeds[5], (SECTIONS, RANK, D), 1.0, 6.0, ((0, 2), (2, 4)))
    return {"norm_in": norm_in, "query_grad": query_grad, "attn_out": attn_out, "handed": handed, "sketch_q": sketch_q, "sketch_o": sketch_o}


precise = lax.Precision.HIGHEST

def orthonormal(row_block):
    gram_rows = jnp.dot(row_block.astype(jnp.float32), row_block.T.astype(jnp.float32), precision=precise, preferred_element_type=jnp.float32)
    low_factor = jnp.linalg.cholesky(gram_rows)
    solved = lax.linalg.triangular_solve(low_factor, row_block, left_side=True, lower=True)
    return solved.astype(jnp.bfloat16)

def factor(basis, matrix):
    return jnp.dot(basis.astype(jnp.float32), matrix.T.astype(jnp.float32), preferred_element_type=jnp.float32).astype(jnp.bfloat16)

def summed(token_rows, matrix):
    token_blocks = token_rows.reshape(RANK, N_DP, TOK_DEV).transpose(1, 0, 2)
    matrix_blocks = matrix.reshape(N_DP, TOK_DEV, matrix.shape[1])

    def block_product(two_parts):
        return jnp.dot(two_parts[0].astype(jnp.float32), two_parts[1].astype(jnp.float32), preferred_element_type=jnp.float32).astype(jnp.bfloat16)
    partial_value = lax.map(block_product, (token_blocks, matrix_blocks))
    return lax.optimization_barrier(jnp.sum(partial_value.astype(jnp.float32), axis=0))

def adapters(left, right, sketch):
    basis = orthonormal(summed(factor(sketch, right), left))
    for iteration in range(POWER):
        other = orthonormal(summed(factor(basis, left), right))
        basis = orthonormal(summed(factor(other, right), left))
    raw = summed(factor(basis, left), right)
    norm_scale = jnp.sqrt(jnp.mean(raw * raw) + 1e-06)
    return (basis * 16.0, raw / norm_scale)

def reference(norm_in, query_grad, attn_out, handed, sketch_q, sketch_o):
    upstream = jnp.concatenate([handed[1:], handed[:1]], axis=0)

    def per_section(section_items):
        norm_rows, query_rows, attn_rows, up_rows, sketch_a, sketch_b = section_items
        b_query, a_query = adapters(norm_rows, query_rows, sketch_a)
        b_output, a_output = adapters(attn_rows, up_rows, sketch_b)
        return (b_query, a_query, b_output, a_output)
    b_query, a_query, b_output, a_output = lax.map(per_section, (norm_in, query_grad, attn_out, upstream, sketch_q, sketch_o))
    return (b_query, a_query, b_output, a_output)
```

```python
import functools

import jax
import jax.numpy as jnp
from jax import lax
from jax.experimental import pallas as pl
from jax.experimental.pallas import tpu as pltpu
from jax.sharding import PartitionSpec as P

RANK = 64
POWER = 2
BLK = 128

precise = lax.Precision.HIGHEST
f32 = jnp.float32
bf16 = jnp.bfloat16
VMEM = pl.BlockSpec(memory_space=pltpu.VMEM)
SMEM = pl.BlockSpec(memory_space=pltpu.SMEM)


def from_behind(value, axis, steps):
    count = lax.axis_size(axis)
    pairs = [(source, (source + steps) % count) for source in range(count)]
    return lax.ppermute(value, axis, pairs)


def gram_of(row_block):
    return jnp.dot(row_block, row_block.T, precision=precise, preferred_element_type=f32)


def solve_rows(gram_rows, row_block):
    low_factor = jnp.linalg.cholesky(gram_rows)
    solved = lax.linalg.triangular_solve(low_factor, row_block, left_side=True, lower=True)
    return solved.astype(bf16)


def tokens_of(sketches, matrices):
    parts = [
        jnp.einsum("km,tm->kt", s, m, preferred_element_type=f32)
        for s, m in zip(sketches, matrices)
    ]
    return tuple(lax.psum(p.astype(bf16), "tensor").astype(bf16) for p in parts)


def partials(token_rows, matrices):
    return tuple(
        jnp.dot(r, m, preferred_element_type=f32) for r, m in zip(token_rows, matrices)
    )


def orthonormal(parts):
    rows = [lax.psum(p.astype(bf16), "dp").astype(f32) for p in parts]
    grams = [lax.psum(gram_of(r).astype(bf16), "tensor").astype(f32) for r in rows]
    return tuple(solve_rows(g, r) for g, r in zip(grams, rows))


def feature_space(norm_in, query_grad, attn_out, handed, sketch_q, sketch_o):
    upstream = from_behind(handed, "section", -1)
    lefts = (norm_in[0], attn_out[0])
    rights = (query_grad[0], upstream[0])
    basis = orthonormal(partials(tokens_of((sketch_q[0], sketch_o[0]), rights), lefts))
    for _ in range(POWER):
        other = orthonormal(partials(tokens_of(basis, lefts), rights))
        basis = orthonormal(partials(tokens_of(other, rights), lefts))
    final = partials(tokens_of(basis, lefts), rights)
    raws = [lax.psum(p.astype(bf16), "dp").astype(f32) for p in final]
    energies = lax.psum(tuple(jnp.sum(r * r) for r in raws), "tensor")
    count = lax.axis_size("tensor")
    adapters = [
        r / jnp.sqrt(e / (r.size * count) + 1e-06) for r, e in zip(raws, energies)
    ]
    return (
        (basis[0] * 16.0)[None],
        adapters[0][None],
        (basis[1] * 16.0)[None],
        adapters[1][None],
    )


def swap(value, axis, bit):
    count = lax.axis_size(axis)
    return lax.ppermute(value, axis, [(i, i ^ bit) for i in range(count)])


def routed(value, sizes, token_bit, tensor_bit, shifted):
    sections, dps, tensors = sizes
    pairs = []
    for s in range(sections):
        for z in range(dps):
            for t in range(tensors):
                to_t = t ^ tensor_bit
                to_s = (s - 1) % sections if shifted and to_t >= tensors // 2 else s
                to = (to_s * dps + (z ^ token_bit)) * tensors + to_t
                pairs.append(((s * dps + z) * tensors + t, to))
    return lax.ppermute(value, ("section", "dp", "tensor"), pairs)


def pack_kernel(dps, idx, norm, grad, attn, hand, sk_q, sk_o, *outs):
    z, out_half = idx[0], idx[1]
    big_w, small_w = norm.shape[1] // dps, grad.shape[1] // dps
    own_big, oth_big = outs[:dps], outs[dps : 2 * dps]
    own_small, oth_small = outs[2 * dps : 3 * dps], outs[3 * dps : 4 * dps]
    own_sk, oth_sk = outs[4 * dps :]
    for d in range(dps):
        at = z ^ d
        bigs = pl.ds(pl.multiple_of(at * big_w, big_w), big_w)
        smalls = pl.ds(pl.multiple_of(at * small_w, small_w), small_w)

        @pl.when(out_half == 0)
        def _():
            own_big[d][...] = norm[:, bigs]
            oth_big[d][...] = hand[:, bigs]
            own_small[d][...] = grad[:, smalls]
            oth_small[d][...] = attn[:, smalls]

        @pl.when(out_half == 1)
        def _():
            own_big[d][...] = hand[:, bigs]
            oth_big[d][...] = norm[:, bigs]
            own_small[d][...] = attn[:, smalls]
            oth_small[d][...] = grad[:, smalls]

    bigs = pl.ds(pl.multiple_of(z * big_w, big_w), big_w)
    smalls = pl.ds(pl.multiple_of(z * small_w, small_w), small_w)
    for_o, for_q = sk_o[:, bigs], sk_q[:, smalls]

    @pl.when(out_half == 0)
    def _():
        own_sk[:, :big_w] = jnp.zeros_like(for_o)
        own_sk[:, big_w:] = for_q
        oth_sk[:, :big_w] = for_o
        oth_sk[:, big_w:] = jnp.zeros_like(for_q)

    @pl.when(out_half == 1)
    def _():
        own_sk[:, :big_w] = for_o
        own_sk[:, big_w:] = jnp.zeros_like(for_q)
        oth_sk[:, :big_w] = jnp.zeros_like(for_o)
        oth_sk[:, big_w:] = for_q


def nt(a, b, precision=None):
    return lax.dot_general(
        a, b, (((1,), (1,)), ((), ())), precision=precision, preferred_element_type=f32
    )


def gram_kernel(dps, idx, *refs):
    z, core = idx[0], idx[2]
    own_big, oth_big = refs[:dps], refs[dps : 2 * dps]
    own_small, oth_small = refs[2 * dps : 3 * dps], refs[3 * dps : 4 * dps]
    own_sk, oth_sk = refs[4 * dps : 4 * dps + 2]
    big, small, keep, send, slots = refs[4 * dps + 2 :]
    big_w, small_w = own_big[0].shape[1], own_small[0].shape[1]
    rank = own_sk.shape[0]
    for d in range(dps):
        rows = pl.ds(pl.multiple_of((z ^ d) * BLK, BLK), BLK)
        big[rows, :big_w] = own_big[d][...]
        big[rows, big_w:] = oth_big[d][...]
        small[rows, :small_w] = own_small[d][...]
        small[rows, small_w:] = oth_small[d][...]
    half = slots.shape[1]
    at = 0
    for m in (big, small):
        for i in range(dps):
            row = nt(m[i * BLK : (i + 1) * BLK, :], m[: (i + 1) * BLK, :])
            for j in range(i + 1):
                slots[at // half, at % half] = row[:, j * BLK : (j + 1) * BLK].astype(bf16)
                at += 1
    first = (
        nt(own_sk[:, :big_w], big[:, :big_w])
        + nt(oth_sk[:, :big_w], big[:, big_w:])
        + nt(own_sk[:, big_w:], small[:, :small_w])
        + nt(oth_sk[:, big_w:], small[:, small_w:])
    ).astype(bf16)
    per = BLK // rank
    for i in range(dps):
        s = at + i // per
        r = (i % per) * rank
        slots[s // half, s % half, r : r + rank, :] = first[:, i * BLK : (i + 1) * BLK]
    for s in range(at + dps // per, 2 * half):
        slots[s // half, s % half] = jnp.zeros((BLK, BLK), bf16)
    keep[...] = slots[core]
    send[...] = slots[1 - core]


def add_pair_kernel(dps, idx, keep, got, *shares):
    z = idx[0]
    size = shares[0].shape[0]
    for d in range(dps):
        part = pl.ds((z ^ d) * size, size)
        shares[d][...] = (keep[part].astype(f32) + got[part].astype(f32)).astype(bf16)


def add_all_kernel(*refs):
    total = refs[0][...].astype(f32)
    for r in refs[1:-1]:
        total = total + r[...].astype(f32)
    refs[-1][...] = total.astype(bf16)


def inverse_factor(gram):
    n = gram.shape[0]
    rows = lax.broadcasted_iota(jnp.int32, (n, n), 0)
    cols = lax.broadcasted_iota(jnp.int32, (n, n), 1)
    eye = (rows == cols).astype(f32)
    work = jnp.concatenate([gram, eye], axis=1)
    slabs = [work[8 * s : 8 * s + 8, :] for s in range(n // 8)]
    sub = lax.broadcasted_iota(jnp.int32, (8, 2 * n), 0)
    for k in range(n):
        s0, r0 = divmod(k, 8)
        pivot_row = slabs[s0][r0 : r0 + 1, :]
        scaled = pivot_row * (1.0 / pivot_row[:, k : k + 1])
        for s in range(s0, n // 8):
            col = slabs[s][:, k : k + 1]
            new = slabs[s] - col * scaled
            slabs[s] = jnp.where(sub > r0, new, slabs[s]) if s == s0 else new
    work = jnp.concatenate(slabs, axis=0)
    pivots = jnp.sum(work[:, :n] * eye, axis=1, keepdims=True)
    return work[:, n:] * lax.rsqrt(pivots)


def times(rows, gram):
    high = rows.astype(bf16)
    low = (rows - high.astype(f32)).astype(bf16)
    return jnp.dot(high, gram, preferred_element_type=f32) + jnp.dot(
        low, gram, preferred_element_type=f32
    )


def chain_kernel(dps, counts, idx, *refs):
    z, out_half, core = idx[0], idx[1], idx[2]
    mine, theirs = refs[:dps], refs[dps : 2 * dps]
    big, small = refs[2 * dps : 2 * dps + 2]
    own_out, oth_out, slots, left, right = refs[2 * dps + 2 :]
    size = mine[0].shape[0]
    half = size * dps
    for d in range(dps):
        slots[pl.ds(core * half + (z ^ d) * size, size)] = mine[d][...]
        slots[pl.ds((1 - core) * half + (z ^ d) * size, size)] = theirs[d][...]
    tri = dps * (dps + 1) // 2
    for gram, base in ((left, out_half * tri), (right, (1 - out_half) * tri)):
        at = 0
        for i in range(dps):
            for j in range(i + 1):
                block = slots[base + at]
                gram[i * BLK : (i + 1) * BLK, j * BLK : (j + 1) * BLK] = block
                if j < i:
                    gram[j * BLK : (j + 1) * BLK, i * BLK : (i + 1) * BLK] = (
                        block.astype(f32).T.astype(bf16)
                    )
                at += 1
    per = BLK // RANK
    rows = jnp.concatenate(
        [
            slots[2 * tri + i // per, (i % per) * RANK : (i % per + 1) * RANK, :]
            for i in range(dps)
        ],
        axis=1,
    ).astype(f32)
    for step in range(2 * POWER + 1):
        gram = left if step % 2 == 0 else right
        ahead = times(rows, gram[...])
        low_inv = inverse_factor(nt(ahead, rows, precise))
        basis = rows
        rows = jnp.dot(low_inv, ahead, precision=precise, preferred_element_type=f32)
    basis = jnp.dot(low_inv, basis, precision=precise, preferred_element_type=f32)
    energy = jnp.sum(times(rows, right[...]) * rows)
    count = jnp.where(out_half == 1, counts[0], counts[1]).astype(f32)
    scale = lax.rsqrt(jnp.full((1, 1), energy, f32) / count + 1e-06)
    coef_b, coef_a = basis.astype(bf16), rows.astype(bf16)
    is_out = out_half == 1
    for_big = jnp.where(is_out, coef_a, coef_b)
    for_small = jnp.where(is_out, coef_b, coef_a)
    scale_big = jnp.where(is_out, scale, 16.0)
    scale_small = jnp.where(is_out, 16.0, scale)
    big_w, small_w = big.shape[1] // 2, small.shape[1] // 2
    for out, n in ((own_out, 0), (oth_out, 1)):
        out[:, :big_w] = (
            jnp.dot(for_big, big[:, n * big_w : (n + 1) * big_w], preferred_element_type=f32)
            * scale_big
        ).astype(bf16)
        out[:, big_w:] = (
            jnp.dot(
                for_small, small[:, n * small_w : (n + 1) * small_w], preferred_element_type=f32
            )
            * scale_small
        ).astype(bf16)


def place_kernel(dps, idx, *refs):
    z, out_half = idx[0], idx[1]
    own, oth = refs[:dps], refs[dps : 2 * dps]
    b_q, a_q, b_o, a_o = refs[2 * dps :]
    big_w, small_w = b_q.shape[1] // dps, a_q.shape[1] // dps
    for d in range(dps):
        bigs = pl.ds(pl.multiple_of((z ^ d) * big_w, big_w), big_w)
        smalls = pl.ds(pl.multiple_of((z ^ d) * small_w, small_w), small_w)
        for half, query, output in ((0, own[d], oth[d]), (1, oth[d], own[d])):

            @pl.when(out_half == half)
            def _():
                b_q[:, bigs] = query[:, :big_w]
                a_q[:, smalls] = query[:, big_w:].astype(f32)
                a_o[:, bigs] = output[:, :big_w].astype(f32)
                b_o[:, smalls] = output[:, big_w:]


def call(kernel, out_shapes, args, scratch=()):
    outs = pl.pallas_call(
        kernel,
        out_shape=out_shapes,
        in_specs=[SMEM] + [VMEM] * (len(args) - 1),
        out_specs=jax.tree.map(lambda _: VMEM, out_shapes),
        scratch_shapes=list(scratch),
        compiler_params=pltpu.CompilerParams(vmem_limit_bytes=48 * 2**20),
    )(*args)
    return list(outs)


def token_space(sizes, norm_in, query_grad, attn_out, handed, sketch_q, sketch_o):
    _, dps, tensors = sizes
    side = tensors // 2
    shape = lambda s, t=bf16: jax.ShapeDtypeStruct(s, t)
    z, t = lax.axis_index("dp"), lax.axis_index("tensor")
    idx = jnp.stack([z, t // side, t % side]).astype(jnp.int32)
    wide, narrow = norm_in.shape[2], query_grad.shape[2]
    big_w, small_w = wide // dps, narrow // dps

    packed = call(
        functools.partial(pack_kernel, dps),
        [shape((BLK, big_w))] * (2 * dps)
        + [shape((BLK, small_w))] * (2 * dps)
        + [shape((RANK, big_w + small_w))] * 2,
        (idx, norm_in[0], query_grad[0], attn_out[0], handed[0], sketch_q[0], sketch_o[0]),
    )
    own_big, oth_big = packed[:dps], packed[dps : 2 * dps]
    own_small, oth_small = packed[2 * dps : 3 * dps], packed[3 * dps : 4 * dps]
    own_sk, oth_sk = packed[4 * dps :]
    own_big = [routed(v, sizes, d, 0, True) for d, v in enumerate(own_big)]
    oth_big = [routed(v, sizes, d, side, True) for d, v in enumerate(oth_big)]
    own_small = own_small[:1] + [
        routed(v, sizes, d, 0, False) for d, v in enumerate(own_small) if d
    ]
    oth_small = [routed(v, sizes, d, side, False) for d, v in enumerate(oth_small)]
    oth_sk = swap(oth_sk, "tensor", side)

    tri = dps * (dps + 1) // 2
    share = pl.cdiv(2 * tri + dps * RANK // BLK, 2 * dps)
    half = share * dps
    tokens = dps * BLK
    big, small, keep, send = call(
        functools.partial(gram_kernel, dps),
        [
            shape((tokens, 2 * big_w)),
            shape((tokens, 2 * small_w)),
            shape((half, BLK, BLK)),
            shape((half, BLK, BLK)),
        ],
        (idx, *own_big, *oth_big, *own_small, *oth_small, own_sk, oth_sk),
        [pltpu.VMEM((2, half, BLK, BLK), bf16)],
    )
    got = swap(send, "tensor", 1)
    shares = call(
        functools.partial(add_pair_kernel, dps),
        [shape((share, BLK, BLK))] * dps,
        (idx, keep, got),
    )
    shares = shares[:1] + [swap(v, "dp", d) for d, v in enumerate(shares) if d]
    total = pl.pallas_call(
        add_all_kernel,
        out_shape=shape((share, BLK, BLK)),
        in_specs=[VMEM] * dps,
        out_specs=VMEM,
    )(*shares)
    mine = [total] + [swap(total, "dp", d) for d in range(1, dps)]
    theirs = [swap(v, "tensor", 1) for v in mine]

    counts = (RANK * wide * tensors, RANK * narrow * tensors)
    own_out, oth_out = call(
        functools.partial(chain_kernel, dps, counts),
        [shape((RANK, big_w + small_w))] * 2,
        (idx, *mine, *theirs, big, small),
        [
            pltpu.VMEM((2 * half, BLK, BLK), bf16),
            pltpu.VMEM((tokens, tokens), bf16),
            pltpu.VMEM((tokens, tokens), bf16),
        ],
    )
    oth_out = swap(oth_out, "tensor", side)
    own = [own_out] + [swap(own_out, "dp", d) for d in range(1, dps)]
    oth = [oth_out] + [swap(oth_out, "dp", d) for d in range(1, dps)]
    outs = call(
        functools.partial(place_kernel, dps),
        [
            shape((RANK, wide)),
            shape((RANK, narrow), f32),
            shape((RANK, narrow)),
            shape((RANK, wide), f32),
        ],
        (idx, *own, *oth),
    )
    return tuple(o[None] for o in outs)


def solution(mesh):
    sizes = tuple(mesh.shape[axis] for axis in ("section", "dp", "tensor"))
    _, dps, tensors = sizes

    def body(norm_in, query_grad, attn_out, handed, sketch_q, sketch_o):
        args = (norm_in, query_grad, attn_out, handed, sketch_q, sketch_o)
        fits = (
            dps in (2, 4)
            and tensors == 4
            and norm_in.shape[1] == BLK
            and sketch_q.shape[1] == RANK
            and norm_in.shape[2] == handed.shape[2]
            and query_grad.shape[2] == attn_out.shape[2]
            and query_grad.shape[2] % (dps * 128) == 0
            and norm_in.shape[2] % (dps * 128) == 0
        )
        return token_space(sizes, *args) if fits else feature_space(*args)

    return jax.shard_map(
        body,
        mesh=mesh,
        in_specs=(P("section", "dp", "tensor"),) * 4 + (P("section", None, "tensor"),) * 2,
        out_specs=(P("section", None, "tensor"),) * 4,
        check_vma=False,
    )
```

```python
import functools

import jax
import jax.numpy as jnp
from jax import lax
from jax.experimental import pallas as pl
from jax.experimental.pallas import tpu as pltpu
from jax.sharding import PartitionSpec as P

RANK = 64
POWER = 2
BLK = 128

precise = lax.Precision.HIGHEST
f32 = jnp.float32
bf16 = jnp.bfloat16
VMEM = pl.BlockSpec(memory_space=pltpu.VMEM)
SMEM = pl.BlockSpec(memory_space=pltpu.SMEM)


def from_behind(value, axis, steps):
    count = lax.axis_size(axis)
    pairs = [(source, (source + steps) % count) for source in range(count)]
    return lax.ppermute(value, axis, pairs)


def gram_of(row_block):
    return jnp.dot(row_block, row_block.T, precision=precise, preferred_element_type=f32)


def solve_rows(gram_rows, row_block):
    low_factor = jnp.linalg.cholesky(gram_rows)
    solved = lax.linalg.triangular_solve(low_factor, row_block, left_side=True, lower=True)
    return solved.astype(bf16)


def tokens_of(sketches, matrices):
    parts = [
        jnp.einsum("km,tm->kt", s, m, preferred_element_type=f32)
        for s, m in zip(sketches, matrices)
    ]
    return tuple(lax.psum(p.astype(bf16), "tensor").astype(bf16) for p in parts)


def partials(token_rows, matrices):
    return tuple(
        jnp.dot(r, m, preferred_element_type=f32) for r, m in zip(token_rows, matrices)
    )


def orthonormal(parts):
    rows = [lax.psum(p.astype(bf16), "dp").astype(f32) for p in parts]
    grams = [lax.psum(gram_of(r).astype(bf16), "tensor").astype(f32) for r in rows]
    return tuple(solve_rows(g, r) for g, r in zip(grams, rows))


def feature_space(norm_in, query_grad, attn_out, handed, sketch_q, sketch_o):
    upstream = from_behind(handed, "section", -1)
    lefts = (norm_in[0], attn_out[0])
    rights = (query_grad[0], upstream[0])
    basis = orthonormal(partials(tokens_of((sketch_q[0], sketch_o[0]), rights), lefts))
    for _ in range(POWER):
        other = orthonormal(partials(tokens_of(basis, lefts), rights))
        basis = orthonormal(partials(tokens_of(other, rights), lefts))
    final = partials(tokens_of(basis, lefts), rights)
    raws = [lax.psum(p.astype(bf16), "dp").astype(f32) for p in final]
    energies = lax.psum(tuple(jnp.sum(r * r) for r in raws), "tensor")
    count = lax.axis_size("tensor")
    adapters = [
        r / jnp.sqrt(e / (r.size * count) + 1e-06) for r, e in zip(raws, energies)
    ]
    return (
        (basis[0] * 16.0)[None],
        adapters[0][None],
        (basis[1] * 16.0)[None],
        adapters[1][None],
    )


def swap(value, axis, bit):
    count = lax.axis_size(axis)
    return lax.ppermute(value, axis, [(i, i ^ bit) for i in range(count)])


def routed(value, sizes, token_bit, tensor_bit, shifted):
    sections, dps, tensors = sizes
    pairs = []
    for s in range(sections):
        for z in range(dps):
            for t in range(tensors):
                to_t = t ^ tensor_bit
                to_s = (s - 1) % sections if shifted and to_t >= tensors // 2 else s
                to = (to_s * dps + (z ^ token_bit)) * tensors + to_t
                pairs.append(((s * dps + z) * tensors + t, to))
    return lax.ppermute(value, ("section", "dp", "tensor"), pairs)


def pack_kernel(dps, idx, norm, grad, attn, hand, sk_q, sk_o, *refs):
    z, out_half = idx[0], idx[1]
    outs, sems = refs[:-1], refs[-1]
    big_w, small_w = outs[0].shape[1], outs[2 * dps].shape[1]
    own_sk, oth_sk = outs[4 * dps :]

    def window(ref, width, at):
        return ref.at[:, pl.ds(pl.multiple_of(at * width, width), width)]

    def move(own_wide, oth_wide, own_thin, oth_thin, sk_wide, sk_thin):
        pairs = []
        for n, (ref, width) in enumerate(
            ((own_wide, big_w), (oth_wide, big_w), (own_thin, small_w), (oth_thin, small_w))
        ):
            pairs += [(window(ref, width, z ^ d), outs[n * dps + d]) for d in range(dps)]
        pairs.append((window(sk_o, big_w, z), sk_wide.at[:, :big_w]))
        pairs.append((window(sk_q, small_w, z), sk_thin.at[:, big_w:]))
        copies = [
            pltpu.make_async_copy(src, dst, sems.at[n]) for n, (src, dst) in enumerate(pairs)
        ]
        for c in copies:
            c.start()
        sk_wide[:, big_w:] = jnp.zeros((sk_wide.shape[0], small_w), bf16)
        sk_thin[:, :big_w] = jnp.zeros((sk_thin.shape[0], big_w), bf16)
        for c in copies:
            c.wait()

    @pl.when(out_half == 0)
    def _():
        move(norm, hand, grad, attn, oth_sk, own_sk)

    @pl.when(out_half == 1)
    def _():
        move(hand, norm, attn, grad, own_sk, oth_sk)


def nt(a, b, precision=None):
    return lax.dot_general(
        a, b, (((1,), (1,)), ((), ())), precision=precision, preferred_element_type=f32
    )


def gram_kernel(dps, idx, *refs):
    z, core = idx[0], idx[2]
    own_big, oth_big = refs[:dps], refs[dps : 2 * dps]
    own_small, oth_small = refs[2 * dps : 3 * dps], refs[3 * dps : 4 * dps]
    own_sk, oth_sk = refs[4 * dps : 4 * dps + 2]
    big, small, keep, send, slots = refs[4 * dps + 2 :]
    big_w, small_w = own_big[0].shape[1], own_small[0].shape[1]
    rank = own_sk.shape[0]
    for d in range(dps):
        rows = pl.ds(pl.multiple_of((z ^ d) * BLK, BLK), BLK)
        big[rows, :big_w] = own_big[d][...]
        big[rows, big_w:] = oth_big[d][...]
        small[rows, :small_w] = own_small[d][...]
        small[rows, small_w:] = oth_small[d][...]
    half = slots.shape[1]
    at = 0
    for m in (big, small):
        for i in range(dps):
            row = nt(m[i * BLK : (i + 1) * BLK, :], m[: (i + 1) * BLK, :])
            for j in range(i + 1):
                slots[at // half, at % half] = row[:, j * BLK : (j + 1) * BLK].astype(bf16)
                at += 1
    first = (
        nt(own_sk[:, :big_w], big[:, :big_w])
        + nt(oth_sk[:, :big_w], big[:, big_w:])
        + nt(own_sk[:, big_w:], small[:, :small_w])
        + nt(oth_sk[:, big_w:], small[:, small_w:])
    ).astype(bf16)
    per = BLK // rank
    for i in range(dps):
        s = at + i // per
        r = (i % per) * rank
        slots[s // half, s % half, r : r + rank, :] = first[:, i * BLK : (i + 1) * BLK]
    for s in range(at + dps // per, 2 * half):
        slots[s // half, s % half] = jnp.zeros((BLK, BLK), bf16)
    keep[...] = slots[core]
    send[...] = slots[1 - core]


def add_pair_kernel(dps, idx, keep, got, *shares):
    z = idx[0]
    size = shares[0].shape[0]
    for d in range(dps):
        part = pl.ds((z ^ d) * size, size)
        shares[d][...] = (keep[part].astype(f32) + got[part].astype(f32)).astype(bf16)


def add_all_kernel(*refs):
    total = refs[0][...].astype(f32)
    for r in refs[1:-1]:
        total = total + r[...].astype(f32)
    refs[-1][...] = total.astype(bf16)


def inverse_factor(gram):
    n, nb = gram.shape[0], 8
    rows = lax.broadcasted_iota(jnp.int32, (n, n), 0)
    cols = lax.broadcasted_iota(jnp.int32, (n, n), 1)
    work = jnp.concatenate([(rows == cols).astype(f32), gram], axis=1)
    count = n // nb
    slabs = [work[nb * s : nb * s + nb, :] for s in range(count)]
    sub = lax.broadcasted_iota(jnp.int32, (nb, 2 * n), 0)

    def lane(x, k):
        return jnp.broadcast_to(x[:, n + k : n + k + 1], (nb, 2 * n))

    def row(x, i):
        return jnp.broadcast_to(x[i : i + 1, :], (nb, 2 * n))

    done = []
    for b in range(count):
        cols_of = [lane(slabs[b], nb * b + j) for j in range(nb)]
        pivot_rows = [row(slabs[b], i) for i in range(nb)]
        splat = [[row(cols_of[j], i) for j in range(i + 1)] for i in range(nb)]
        below = {s: [lane(slabs[s], nb * b + j) for j in range(nb)] for s in range(b + 1, count)}
        out = None
        for k in range(nb):
            inv = 1.0 / splat[k][k]
            at = pivot_rows[k]
            final = at * lax.rsqrt(splat[k][k])
            out = final if out is None else jnp.where(sub == k, final, out)
            for i in range(k + 1, nb):
                mult = splat[i][k] * inv
                for j in range(k + 1, i + 1):
                    splat[i][j] = splat[i][j] - mult * splat[j][k]
                pivot_rows[i] = pivot_rows[i] - mult * at
            for s in range(b + 1, count):
                mult = below[s][k] * inv
                for j in range(k + 1, nb):
                    below[s][j] = below[s][j] - mult * splat[j][k]
                slabs[s] = slabs[s] - mult * at
        done.append(out)
    return jnp.concatenate(done, axis=0)[:, :n]


def split(x):
    high = x.astype(bf16)
    return high, (x - high.astype(f32)).astype(bf16)


def times(rows, gram):
    n = rows.shape[0]
    both = jnp.dot(jnp.concatenate(split(rows), axis=0), gram, preferred_element_type=f32)
    return both[:n] + both[n:]


def product(a, b):
    (ah, al), (bh, bl) = split(a), split(b)
    return jnp.dot(
        jnp.concatenate([ah, ah, al], axis=1),
        jnp.concatenate([bh, bl, bh], axis=0),
        preferred_element_type=f32,
    )


def product_nt(a, b):
    (ah, al), (bh, bl) = split(a), split(b)
    return nt(jnp.concatenate([ah, ah, al], axis=1), jnp.concatenate([bh, bl, bh], axis=1))


def chain_kernel(dps, counts, idx, *refs):
    z, out_half, core = idx[0], idx[1], idx[2]
    mine, theirs = refs[:dps], refs[dps : 2 * dps]
    big, small = refs[2 * dps : 2 * dps + 2]
    own_out, oth_out, slots, left, right = refs[2 * dps + 2 :]
    size = mine[0].shape[0]
    half = size * dps
    for d in range(dps):
        slots[pl.ds(core * half + (z ^ d) * size, size)] = mine[d][...]
        slots[pl.ds((1 - core) * half + (z ^ d) * size, size)] = theirs[d][...]
    tri = dps * (dps + 1) // 2
    for gram, base in ((left, out_half * tri), (right, (1 - out_half) * tri)):
        at = 0
        for i in range(dps):
            for j in range(i + 1):
                block = slots[base + at]
                gram[i * BLK : (i + 1) * BLK, j * BLK : (j + 1) * BLK] = block
                if j < i:
                    gram[j * BLK : (j + 1) * BLK, i * BLK : (i + 1) * BLK] = (
                        block.astype(f32).T.astype(bf16)
                    )
                at += 1
    per = BLK // RANK
    rows = jnp.concatenate(
        [
            slots[2 * tri + i // per, (i % per) * RANK : (i % per + 1) * RANK, :]
            for i in range(dps)
        ],
        axis=1,
    ).astype(f32)
    ahead = times(rows, left[...])
    gram = product_nt(ahead, rows)
    for step in range(2 * POWER):
        following = (right if step % 2 == 0 else left)[...]
        beyond = times(ahead, following)
        inner = product_nt(beyond, ahead)
        low_inv = inverse_factor(gram)
        rows = product(low_inv, ahead)
        if step < 2 * POWER - 1:
            gram = product_nt(product(low_inv, inner), low_inv)
            ahead = product(low_inv, beyond)
        else:
            ahead = times(rows, following)
            gram = product_nt(ahead, rows)
    low_inv = inverse_factor(gram)
    basis = product(low_inv, rows)
    rows = product(low_inv, ahead)
    energy = jnp.sum(times(rows, right[...]) * rows)
    count = jnp.where(out_half == 1, counts[0], counts[1]).astype(f32)
    scale = lax.rsqrt(jnp.full((1, 1), energy, f32) / count + 1e-06)
    coef_b, coef_a = basis.astype(bf16), rows.astype(bf16)
    is_out = out_half == 1
    for_big = jnp.where(is_out, coef_a, coef_b)
    for_small = jnp.where(is_out, coef_b, coef_a)
    scale_big = jnp.where(is_out, scale, 16.0)
    scale_small = jnp.where(is_out, 16.0, scale)
    big_w, small_w = big.shape[1] // 2, small.shape[1] // 2
    for out, n in ((own_out, 0), (oth_out, 1)):
        out[:, :big_w] = (
            jnp.dot(for_big, big[:, n * big_w : (n + 1) * big_w], preferred_element_type=f32)
            * scale_big
        ).astype(bf16)
        out[:, big_w:] = (
            jnp.dot(
                for_small, small[:, n * small_w : (n + 1) * small_w], preferred_element_type=f32
            )
            * scale_small
        ).astype(bf16)


def place_kernel(dps, idx, *refs):
    z, out_half = idx[0], idx[1]
    own, oth = refs[:dps], refs[dps : 2 * dps]
    b_q, a_q, b_o, a_o = refs[2 * dps :]
    big_w, small_w = b_q.shape[1] // dps, a_q.shape[1] // dps
    for d in range(dps):
        bigs = pl.ds(pl.multiple_of((z ^ d) * big_w, big_w), big_w)
        smalls = pl.ds(pl.multiple_of((z ^ d) * small_w, small_w), small_w)
        for half, query, output in ((0, own[d], oth[d]), (1, oth[d], own[d])):

            @pl.when(out_half == half)
            def _():
                b_q[:, bigs] = query[:, :big_w]
                a_q[:, smalls] = query[:, big_w:].astype(f32)
                a_o[:, bigs] = output[:, :big_w].astype(f32)
                b_o[:, smalls] = output[:, big_w:]


def call(kernel, out_shapes, args, scratch=(), space=VMEM):
    outs = pl.pallas_call(
        kernel,
        out_shape=out_shapes,
        in_specs=[SMEM] + [space] * (len(args) - 1),
        out_specs=jax.tree.map(lambda _: VMEM, out_shapes),
        scratch_shapes=list(scratch),
        compiler_params=pltpu.CompilerParams(vmem_limit_bytes=48 * 2**20),
    )(*args)
    return list(outs)


def token_space(sizes, norm_in, query_grad, attn_out, handed, sketch_q, sketch_o):
    _, dps, tensors = sizes
    side = tensors // 2
    shape = lambda s, t=bf16: jax.ShapeDtypeStruct(s, t)
    z, t = lax.axis_index("dp"), lax.axis_index("tensor")
    idx = jnp.stack([z, t // side, t % side]).astype(jnp.int32)
    wide, narrow = norm_in.shape[2], query_grad.shape[2]
    big_w, small_w = wide // dps, narrow // dps

    packed = call(
        functools.partial(pack_kernel, dps),
        [shape((BLK, big_w))] * (2 * dps)
        + [shape((BLK, small_w))] * (2 * dps)
        + [shape((RANK, big_w + small_w))] * 2,
        (idx, norm_in[0], query_grad[0], attn_out[0], handed[0], sketch_q[0], sketch_o[0]),
        [pltpu.SemaphoreType.DMA((4 * dps + 2,))],
        pl.BlockSpec(memory_space=pl.ANY),
    )
    own_big, oth_big = packed[:dps], packed[dps : 2 * dps]
    own_small, oth_small = packed[2 * dps : 3 * dps], packed[3 * dps : 4 * dps]
    own_sk, oth_sk = packed[4 * dps :]
    own_big = [routed(v, sizes, d, 0, True) for d, v in enumerate(own_big)]
    oth_big = [routed(v, sizes, d, side, True) for d, v in enumerate(oth_big)]
    own_small = own_small[:1] + [
        routed(v, sizes, d, 0, False) for d, v in enumerate(own_small) if d
    ]
    oth_small = [routed(v, sizes, d, side, False) for d, v in enumerate(oth_small)]
    oth_sk = swap(oth_sk, "tensor", side)

    tri = dps * (dps + 1) // 2
    share = pl.cdiv(2 * tri + dps * RANK // BLK, 2 * dps)
    half = share * dps
    tokens = dps * BLK
    big, small, keep, send = call(
        functools.partial(gram_kernel, dps),
        [
            shape((tokens, 2 * big_w)),
            shape((tokens, 2 * small_w)),
            shape((half, BLK, BLK)),
            shape((half, BLK, BLK)),
        ],
        (idx, *own_big, *oth_big, *own_small, *oth_small, own_sk, oth_sk),
        [pltpu.VMEM((2, half, BLK, BLK), bf16)],
    )
    got = swap(send, "tensor", 1)
    shares = call(
        functools.partial(add_pair_kernel, dps),
        [shape((share, BLK, BLK))] * dps,
        (idx, keep, got),
    )
    shares = shares[:1] + [swap(v, "dp", d) for d, v in enumerate(shares) if d]
    total = pl.pallas_call(
        add_all_kernel,
        out_shape=shape((share, BLK, BLK)),
        in_specs=[VMEM] * dps,
        out_specs=VMEM,
    )(*shares)
    mine = [total] + [swap(total, "dp", d) for d in range(1, dps)]
    theirs = [swap(v, "tensor", 1) for v in mine]

    counts = (RANK * wide * tensors, RANK * narrow * tensors)
    own_out, oth_out = call(
        functools.partial(chain_kernel, dps, counts),
        [shape((RANK, big_w + small_w))] * 2,
        (idx, *mine, *theirs, big, small),
        [
            pltpu.VMEM((2 * half, BLK, BLK), bf16),
            pltpu.VMEM((tokens, tokens), bf16),
            pltpu.VMEM((tokens, tokens), bf16),
        ],
    )
    oth_out = swap(oth_out, "tensor", side)
    own = [own_out] + [swap(own_out, "dp", d) for d in range(1, dps)]
    oth = [oth_out] + [swap(oth_out, "dp", d) for d in range(1, dps)]
    outs = call(
        functools.partial(place_kernel, dps),
        [
            shape((RANK, wide)),
            shape((RANK, narrow), f32),
            shape((RANK, narrow)),
            shape((RANK, wide), f32),
        ],
        (idx, *own, *oth),
    )
    return tuple(o[None] for o in outs)


def solution(mesh):
    sizes = tuple(mesh.shape[axis] for axis in ("section", "dp", "tensor"))
    _, dps, tensors = sizes

    def body(norm_in, query_grad, attn_out, handed, sketch_q, sketch_o):
        args = (norm_in, query_grad, attn_out, handed, sketch_q, sketch_o)
        fits = (
            dps in (2, 4)
            and tensors == 4
            and norm_in.shape[1] == BLK
            and sketch_q.shape[1] == RANK
            and norm_in.shape[2] == handed.shape[2]
            and query_grad.shape[2] == attn_out.shape[2]
            and query_grad.shape[2] % (dps * 128) == 0
            and norm_in.shape[2] % (dps * 128) == 0
        )
        return token_space(sizes, *args) if fits else feature_space(*args)

    return jax.shard_map(
        body,
        mesh=mesh,
        in_specs=(P("section", "dp", "tensor"),) * 4 + (P("section", None, "tensor"),) * 2,
        out_specs=(P("section", None, "tensor"),) * 4,
        check_vma=False,
    )
```

```python
import functools

import jax
import jax.numpy as jnp
from jax import lax
from jax.experimental import pallas as pl
from jax.experimental.pallas import tpu as pltpu
from jax.sharding import PartitionSpec as P

RANK = 64
POWER = 2
BLK = 128

precise = lax.Precision.HIGHEST
f32 = jnp.float32
bf16 = jnp.bfloat16
VMEM = pl.BlockSpec(memory_space=pltpu.VMEM)
SMEM = pl.BlockSpec(memory_space=pltpu.SMEM)


def from_behind(value, axis, steps):
    count = lax.axis_size(axis)
    pairs = [(source, (source + steps) % count) for source in range(count)]
    return lax.ppermute(value, axis, pairs)


def gram_of(row_block):
    return jnp.dot(row_block, row_block.T, precision=precise, preferred_element_type=f32)


def solve_rows(gram_rows, row_block):
    low_factor = jnp.linalg.cholesky(gram_rows)
    solved = lax.linalg.triangular_solve(low_factor, row_block, left_side=True, lower=True)
    return solved.astype(bf16)


def tokens_of(sketches, matrices):
    parts = [
        jnp.einsum("km,tm->kt", s, m, preferred_element_type=f32)
        for s, m in zip(sketches, matrices)
    ]
    return tuple(lax.psum(p.astype(bf16), "tensor").astype(bf16) for p in parts)


def partials(token_rows, matrices):
    return tuple(
        jnp.dot(r, m, preferred_element_type=f32) for r, m in zip(token_rows, matrices)
    )


def orthonormal(parts):
    rows = [lax.psum(p.astype(bf16), "dp").astype(f32) for p in parts]
    grams = [lax.psum(gram_of(r).astype(bf16), "tensor").astype(f32) for r in rows]
    return tuple(solve_rows(g, r) for g, r in zip(grams, rows))


def feature_space(norm_in, query_grad, attn_out, handed, sketch_q, sketch_o):
    upstream = from_behind(handed, "section", -1)
    lefts = (norm_in[0], attn_out[0])
    rights = (query_grad[0], upstream[0])
    basis = orthonormal(partials(tokens_of((sketch_q[0], sketch_o[0]), rights), lefts))
    for _ in range(POWER):
        other = orthonormal(partials(tokens_of(basis, lefts), rights))
        basis = orthonormal(partials(tokens_of(other, rights), lefts))
    final = partials(tokens_of(basis, lefts), rights)
    raws = [lax.psum(p.astype(bf16), "dp").astype(f32) for p in final]
    energies = lax.psum(tuple(jnp.sum(r * r) for r in raws), "tensor")
    count = lax.axis_size("tensor")
    adapters = [
        r / jnp.sqrt(e / (r.size * count) + 1e-06) for r, e in zip(raws, energies)
    ]
    return (
        (basis[0] * 16.0)[None],
        adapters[0][None],
        (basis[1] * 16.0)[None],
        adapters[1][None],
    )


def swap(value, axis, bit):
    count = lax.axis_size(axis)
    return lax.ppermute(value, axis, [(i, i ^ bit) for i in range(count)])


def routed(value, sizes, token_bit, shifted):
    sections, dps, tensors = sizes
    side = tensors // 2
    pairs = []
    for s in range(sections):
        for z in range(dps):
            for t in range(tensors):
                to_t = t ^ side if t % side else t
                to_s = (s - 1) % sections if shifted and to_t >= side else s
                to = (to_s * dps + (z ^ token_bit)) * tensors + to_t
                pairs.append(((s * dps + z) * tensors + t, to))
    return lax.ppermute(value, ("section", "dp", "tensor"), pairs)


def window(ref, width, at):
    return ref.at[:, pl.ds(pl.multiple_of(at * width, width), width)]


def move(pairs, sems):
    copies = [pltpu.make_async_copy(src, dst, sems.at[n]) for n, (src, dst) in enumerate(pairs)]
    for c in copies:
        c.start()
    for c in copies:
        c.wait()


def give_kernel(dps, idx, norm, grad, attn, hand, sk_q, sk_o, give, sems):
    z, kind = idx[0], idx[3]
    wide, narrow = norm.shape[1], grad.shape[1]
    big_w, small_w = wide // dps, narrow // dps
    rows = RANK // dps

    def sketch(ref, width, start):
        part = ref.at[:, pl.ds(pl.multiple_of(z * width, width), width)]
        return [
            (
                part.at[i * rows : (i + 1) * rows],
                give.at[BLK:, i * (big_w + small_w) + start : i * (big_w + small_w) + start + width],
            )
            for i in range(dps)
        ]

    give[BLK:, :] = jnp.zeros((rows, wide + narrow), bf16)

    @pl.when(kind == 0)
    def _():
        pairs = [(hand, give.at[:BLK, :wide]), (attn, give.at[:BLK, wide:])]
        move(pairs + sketch(sk_o, big_w, 0), sems)

    @pl.when(kind == 1)
    def _():
        pairs = [(norm, give.at[:BLK, :wide]), (grad, give.at[:BLK, wide:])]
        move(pairs + sketch(sk_q, small_w, big_w), sems)


def merge_kernel(dps, idx, norm, grad, attn, hand, sk_q, sk_o, got, *refs):
    z, kind = idx[0], idx[3]
    bigs, smalls, sems = refs[:dps], refs[dps : 2 * dps], refs[-1]
    big_w, small_w = bigs[0].shape[1] // 2, smalls[0].shape[1] // 2
    wide, rows = norm.shape[1], RANK // dps

    def keep(wide_ref, thin_ref, extra):
        pairs = [extra]
        for d in range(dps):
            pairs.append((window(wide_ref, big_w, z ^ d), bigs[d].at[:, :big_w]))
            pairs.append((window(thin_ref, small_w, z ^ d), smalls[d].at[:BLK, :small_w]))
        copies = [
            pltpu.make_async_copy(src, dst, sems.at[n]) for n, (src, dst) in enumerate(pairs)
        ]
        for c in copies:
            c.start()
        fill()
        for c in copies:
            c.wait()

    def fill():
        for d in range(dps):
            at = pl.multiple_of((z ^ d) * big_w, big_w)
            bigs[d][:, big_w:] = got[:BLK, pl.ds(at, big_w)]
            at = pl.multiple_of(wide + (z ^ d) * small_w, small_w)
            smalls[d][:BLK, small_w:] = got[:BLK, pl.ds(at, small_w)]
        for i in range(dps):
            at = i * (big_w + small_w)
            below = slice(BLK + RANK + i * rows, BLK + RANK + (i + 1) * rows)
            smalls[0][below, :] = got[BLK:, at : at + big_w]
            below = slice(BLK + 2 * RANK + i * rows, BLK + 2 * RANK + (i + 1) * rows)
            smalls[0][below, small_w:] = got[BLK:, at + big_w : at + big_w + small_w]

    @pl.when(kind == 0)
    def _():
        smalls[0][BLK : BLK + RANK, :] = jnp.zeros((RANK, big_w), bf16)
        dst = smalls[0].at[BLK + 2 * RANK :, :small_w]
        keep(norm, grad, (window(sk_q, small_w, z), dst))

    @pl.when(kind == 1)
    def _():
        smalls[0][BLK + 2 * RANK :, :small_w] = jnp.zeros((RANK, small_w), bf16)
        dst = smalls[0].at[BLK : BLK + RANK, :]
        keep(hand, attn, (window(sk_o, big_w, z), dst))


def nt(a, b, precision=None):
    return lax.dot_general(
        a, b, (((1,), (1,)), ((), ())), precision=precision, preferred_element_type=f32
    )


def packed_rows(dps):
    per_gram = (dps * (dps - 1) // 2 + dps // 2) * BLK
    used = 2 * per_gram + dps * RANK + 16
    return per_gram, pl.cdiv(used, 4 * 16) * 4 * 16


def gram_kernel(dps, idx, *refs):
    z, core = idx[0], idx[2]
    bigs, smalls = refs[:dps], refs[dps : 2 * dps]
    big, small, keep, send, flat = refs[2 * dps :]
    half_w = big.shape[1] // 2
    for d in range(dps):
        rows = pl.ds(pl.multiple_of((z ^ d) * BLK, BLK), BLK)
        big[rows, :] = bigs[d][...]
        small[rows, :] = smalls[d][:BLK, :]
    per_gram, total = packed_rows(dps)
    r = lax.broadcasted_iota(jnp.int32, (BLK, BLK), 0)
    c = lax.broadcasted_iota(jnp.int32, (BLK, BLK), 1)
    at, diagonals = 0, []

    def put(value):
        nonlocal at
        flat[at : at + value.shape[0], :] = value.astype(bf16)
        at += value.shape[0]

    for m in (big, small):
        on = []
        for i in range(dps):
            row = nt(m[i * BLK : (i + 1) * BLK, :], m[: (i + 1) * BLK, :])
            for j in range(i):
                put(row[:, j * BLK : (j + 1) * BLK])
            on.append(row[:, i * BLK :])
        for i in range(0, dps, 2):
            put(jnp.where(r > c, on[i], on[i + 1]))
        diagonals += [jnp.sum(jnp.where(r == c, v, 0.0), axis=0, keepdims=True) for v in on]
        diagonals.append(jnp.zeros((8 - dps, BLK), f32))
    sk = smalls[0]
    first = (
        nt(sk[BLK : BLK + RANK, :], big[:, :half_w])
        + nt(sk[BLK + RANK : BLK + 2 * RANK, :], big[:, half_w:])
        + nt(sk[BLK + 2 * RANK :, :], small[...])
    )
    for i in range(dps):
        put(first[:, i * BLK : (i + 1) * BLK])
    put(jnp.concatenate(diagonals, axis=0))
    put(jnp.zeros((total - at, BLK), f32))
    half = total // 2
    keep[...] = flat[pl.ds(pl.multiple_of(core * half, 16), half), :]
    send[...] = flat[pl.ds(pl.multiple_of((1 - core) * half, 16), half), :]


def add_halves_kernel(idx, mine, got, keep, send):
    size, bit = keep.shape[0], idx[0] % 2
    for out, which in ((keep, bit), (send, 1 - bit)):
        part = pl.ds(pl.multiple_of(which * size, 16), size)
        out[...] = (mine[part, :].astype(f32) + got[part, :].astype(f32)).astype(bf16)


def add_kernel(mine, got, out):
    out[...] = (mine[...].astype(f32) + got[...].astype(f32)).astype(bf16)


def inverse_factor(gram):
    n, nb = gram.shape[0], 8
    rows = lax.broadcasted_iota(jnp.int32, (n, n), 0)
    cols = lax.broadcasted_iota(jnp.int32, (n, n), 1)
    work = jnp.concatenate([(rows == cols).astype(f32), gram], axis=1)
    count = n // nb
    slabs = [work[nb * s : nb * s + nb, :] for s in range(count)]
    sub = lax.broadcasted_iota(jnp.int32, (nb, 2 * n), 0)

    def lane(x, k):
        return jnp.broadcast_to(x[:, n + k : n + k + 1], (nb, 2 * n))

    def row(x, i):
        return jnp.broadcast_to(x[i : i + 1, :], (nb, 2 * n))

    done = []
    for b in range(count):
        cols_of = [lane(slabs[b], nb * b + j) for j in range(nb)]
        pivot_rows = [row(slabs[b], i) for i in range(nb)]
        splat = [[row(cols_of[j], i) for j in range(i + 1)] for i in range(nb)]
        below = {s: [lane(slabs[s], nb * b + j) for j in range(nb)] for s in range(b + 1, count)}
        out = None
        for k in range(nb):
            inv = 1.0 / splat[k][k]
            at = pivot_rows[k]
            final = at * lax.rsqrt(splat[k][k])
            out = final if out is None else jnp.where(sub == k, final, out)
            for i in range(k + 1, nb):
                mult = splat[i][k] * inv
                for j in range(k + 1, i + 1):
                    splat[i][j] = splat[i][j] - mult * splat[j][k]
                pivot_rows[i] = pivot_rows[i] - mult * at
            for s in range(b + 1, count):
                mult = below[s][k] * inv
                for j in range(k + 1, nb):
                    below[s][j] = below[s][j] - mult * splat[j][k]
                slabs[s] = slabs[s] - mult * at
        done.append(out)
    return jnp.concatenate(done, axis=0)[:, :n]


def split(x):
    high = x.astype(bf16)
    return high, (x - high.astype(f32)).astype(bf16)


def times(rows, gram):
    n = rows.shape[0]
    both = jnp.dot(jnp.concatenate(split(rows), axis=0), gram, preferred_element_type=f32)
    return both[:n] + both[n:]


def product(a, b):
    (ah, al), (bh, bl) = split(a), split(b)
    return jnp.dot(
        jnp.concatenate([ah, ah, al], axis=1),
        jnp.concatenate([bh, bl, bh], axis=0),
        preferred_element_type=f32,
    )


def product_nt(a, b):
    (ah, al), (bh, bl) = split(a), split(b)
    return nt(jnp.concatenate([ah, ah, al], axis=1), jnp.concatenate([bh, bl, bh], axis=1))


def chain_kernel(dps, counts, idx, *refs):
    z, out_half, core = idx[0], idx[1], idx[2]
    quarters, big, small, out, flat, left, right = refs[:4], *refs[4:]
    size, bit = quarters[0].shape[0], z % 2
    for n, ref in enumerate(quarters):
        which = 2 * (core ^ (n // 2)) + (bit ^ (n % 2))
        flat[pl.ds(pl.multiple_of(which * size, 16), size), :] = ref[...]
    per_gram, _ = packed_rows(dps)
    r = lax.broadcasted_iota(jnp.int32, (BLK, BLK), 0)
    c = lax.broadcasted_iota(jnp.int32, (BLK, BLK), 1)
    start = 2 * per_gram
    rows = jnp.concatenate(
        [flat[start + i * RANK : start + (i + 1) * RANK, :] for i in range(dps)], axis=1
    ).astype(f32)
    start += dps * RANK
    diagonals = flat[start : start + 16, :].astype(f32)
    is_out = out_half == 1
    for gram, which in ((left, out_half), (right, 1 - out_half)):
        base = which * per_gram

        def block(n):
            return flat[pl.ds(pl.multiple_of(base + n * BLK, BLK), BLK), :].astype(f32)

        def put(i, j, value):
            gram[i * BLK : (i + 1) * BLK, j * BLK : (j + 1) * BLK] = value.astype(bf16)

        n = 0
        for i in range(dps):
            for j in range(i):
                value = block(n)
                put(i, j, value)
                put(j, i, value.T)
                n += 1
        diag = jnp.where(which == 1, diagonals[8:, :], diagonals[:8, :])
        for i in range(0, dps, 2):
            value = block(n)
            turned = value.T
            put(i, i, jnp.where(r > c, value, jnp.where(r == c, diag[i : i + 1, :], turned)))
            put(
                i + 1,
                i + 1,
                jnp.where(r < c, value, jnp.where(r == c, diag[i + 1 : i + 2, :], turned)),
            )
            n += 1
    ahead = times(rows, left[...])
    gram = product_nt(ahead, rows)
    for step in range(2 * POWER):
        following = (right if step % 2 == 0 else left)[...]
        beyond = times(ahead, following)
        inner = product_nt(beyond, ahead)
        low_inv = inverse_factor(gram)
        rows = product(low_inv, ahead)
        if step < 2 * POWER - 1:
            gram = product_nt(product(low_inv, inner), low_inv)
            ahead = product(low_inv, beyond)
        else:
            ahead = times(rows, following)
            gram = product_nt(ahead, rows)
    low_inv = inverse_factor(gram)
    basis = product(low_inv, rows)
    rows = product(low_inv, ahead)
    energy = jnp.sum(times(rows, right[...]) * rows)
    count = jnp.where(out_half == 1, counts[0], counts[1]).astype(f32)
    scale = lax.rsqrt(jnp.full((1, 1), energy, f32) / count + 1e-06)
    coef_b, coef_a = basis.astype(bf16), rows.astype(bf16)
    for_big = jnp.where(is_out, coef_a, coef_b)
    for_small = jnp.where(is_out, coef_b, coef_a)
    scale_big = jnp.where(is_out, scale, 16.0)
    scale_small = jnp.where(is_out, 16.0, scale)
    big_w, small_w = big.shape[1] // 2, small.shape[1] // 2
    made_big = (jnp.dot(for_big, big[...], preferred_element_type=f32) * scale_big).astype(bf16)
    made_small = (jnp.dot(for_small, small[...], preferred_element_type=f32) * scale_small).astype(
        bf16
    )
    for n in range(2):
        part = slice(n * RANK, (n + 1) * RANK)
        out[part, :big_w] = made_big[:, n * big_w : (n + 1) * big_w]
        out[part, big_w:] = made_small[:, n * small_w : (n + 1) * small_w]


def place_kernel(dps, idx, *refs):
    z, kind = idx[0], idx[3]
    mine, theirs = refs[:dps], refs[dps : 2 * dps]
    b_q, a_q, b_o, a_o = refs[2 * dps :]
    big_w, small_w = b_q.shape[1] // dps, a_q.shape[1] // dps
    for d in range(dps):
        bigs = pl.ds(pl.multiple_of((z ^ d) * big_w, big_w), big_w)
        smalls = pl.ds(pl.multiple_of((z ^ d) * small_w, small_w), small_w)
        here, there = mine[d].at[:RANK], theirs[d].at[RANK:]
        for which, query, output in ((0, here, there), (1, there, here)):

            @pl.when(kind == which)
            def _():
                b_q[:, bigs] = query[:, :big_w]
                a_q[:, smalls] = query[:, big_w:].astype(f32)
                a_o[:, bigs] = output[:, :big_w].astype(f32)
                b_o[:, smalls] = output[:, big_w:]


def call(kernel, out_shapes, args, scratch=(), spaces=()):
    spaces = [SMEM] + [VMEM] * (len(args) - 1) if not spaces else spaces
    return pl.pallas_call(
        kernel,
        out_shape=out_shapes,
        in_specs=spaces,
        out_specs=jax.tree.map(lambda _: VMEM, out_shapes),
        scratch_shapes=list(scratch),
        compiler_params=pltpu.CompilerParams(vmem_limit_bytes=48 * 2**20),
    )(*args)


def token_space(sizes, norm_in, query_grad, attn_out, handed, sketch_q, sketch_o):
    _, dps, tensors = sizes
    side = tensors // 2

    def shape(*dims, dtype=bf16):
        return jax.ShapeDtypeStruct(dims, dtype)

    z, t = lax.axis_index("dp"), lax.axis_index("tensor")
    half, core = t // side, t % side
    idx = jnp.stack([z, half, core, half ^ core]).astype(jnp.int32)
    wide, narrow = norm_in.shape[2], query_grad.shape[2]
    big_w, small_w = wide // dps, narrow // dps
    tokens = dps * BLK
    args = (norm_in[0], query_grad[0], attn_out[0], handed[0], sketch_q[0], sketch_o[0])
    in_hbm = [SMEM] + [pl.BlockSpec(memory_space=pltpu.HBM)] * len(args)

    give = call(
        functools.partial(give_kernel, dps),
        shape(BLK + RANK // dps, wide + narrow),
        (idx, *args),
        [pltpu.SemaphoreType.DMA((2 + dps,))],
        in_hbm,
    )
    got = swap(give, "tensor", 1)
    packed = call(
        functools.partial(merge_kernel, dps),
        [shape(BLK, 2 * big_w)] * dps
        + [shape(BLK + 3 * RANK, 2 * small_w)]
        + [shape(BLK, 2 * small_w)] * (dps - 1),
        (idx, *args, got),
        [pltpu.SemaphoreType.DMA((2 * dps + 1,))],
        in_hbm + [VMEM],
    )
    bigs = [routed(v, sizes, d, True) for d, v in enumerate(packed[:dps])]
    smalls = [routed(v, sizes, d, False) for d, v in enumerate(packed[dps:])]

    _, total = packed_rows(dps)
    big, small, keep, send = call(
        functools.partial(gram_kernel, dps),
        [
            shape(tokens, 2 * big_w),
            shape(tokens, 2 * small_w),
            shape(total // 2, BLK),
            shape(total // 2, BLK),
        ],
        (idx, *bigs, *smalls),
        [pltpu.VMEM((total, BLK), bf16)],
    )
    quarter = shape(total // 4, BLK)
    keep, send = call(add_halves_kernel, [quarter] * 2, (idx, keep, swap(send, "tensor", 1)))
    for bit, value in ((1, send), (2, None)):
        value = swap(keep if value is None else value, "dp", bit)
        keep = call(add_kernel, quarter, (keep, value), (), [VMEM] * 2)
    beside = swap(keep, "dp", 1)
    quarters = (keep, beside, swap(keep, "tensor", 1), swap(beside, "tensor", 1))

    counts = (RANK * wide * tensors, RANK * narrow * tensors)
    out = call(
        functools.partial(chain_kernel, dps, counts),
        shape(2 * RANK, big_w + small_w),
        (idx, *quarters, big, small),
        [
            pltpu.VMEM((total, BLK), bf16),
            pltpu.VMEM((tokens, tokens), bf16),
            pltpu.VMEM((tokens, tokens), bf16),
        ],
    )
    mine = [routed(out, sizes, d, False) for d in range(3)]
    mine.append(swap(mine[2], "dp", 1))
    theirs = [swap(v, "tensor", 1) for v in mine]
    outs = call(
        functools.partial(place_kernel, dps),
        [
            shape(RANK, wide),
            shape(RANK, narrow, dtype=f32),
            shape(RANK, narrow),
            shape(RANK, wide, dtype=f32),
        ],
        (idx, *mine, *theirs),
    )
    return tuple(o[None] for o in outs)


def solution(mesh):
    sizes = tuple(mesh.shape[axis] for axis in ("section", "dp", "tensor"))
    _, dps, tensors = sizes

    def body(norm_in, query_grad, attn_out, handed, sketch_q, sketch_o):
        args = (norm_in, query_grad, attn_out, handed, sketch_q, sketch_o)
        fits = (
            dps == 4
            and tensors == 4
            and norm_in.shape[1] == BLK
            and sketch_q.shape[1] == RANK
            and norm_in.shape[2] == handed.shape[2]
            and query_grad.shape[2] == attn_out.shape[2]
            and norm_in.shape[2] == 2 * query_grad.shape[2]
            and query_grad.shape[2] % (dps * 128) == 0
        )
        return token_space(sizes, *args) if fits else feature_space(*args)

    return jax.shard_map(
        body,
        mesh=mesh,
        in_specs=(P("section", "dp", "tensor"),) * 4 + (P("section", None, "tensor"),) * 2,
        out_specs=(P("section", None, "tensor"),) * 4,
        check_vma=False,
    )
```

```python
import functools

import jax
import jax.numpy as jnp
from jax import lax
from jax.experimental import pallas as pl
from jax.experimental.pallas import tpu as pltpu
from jax.sharding import PartitionSpec as P

RANK = 64
POWER = 2
BLK = 128
FAR_FIRST = (2, 3, 1, 0)

precise = lax.Precision.HIGHEST
f32 = jnp.float32
bf16 = jnp.bfloat16
VMEM = pl.BlockSpec(memory_space=pltpu.VMEM)
SMEM = pl.BlockSpec(memory_space=pltpu.SMEM)


def from_behind(value, axis, steps):
    count = lax.axis_size(axis)
    pairs = [(source, (source + steps) % count) for source in range(count)]
    return lax.ppermute(value, axis, pairs)


def gram_of(row_block):
    return jnp.dot(row_block, row_block.T, precision=precise, preferred_element_type=f32)


def solve_rows(gram_rows, row_block):
    low_factor = jnp.linalg.cholesky(gram_rows)
    solved = lax.linalg.triangular_solve(low_factor, row_block, left_side=True, lower=True)
    return solved.astype(bf16)


def tokens_of(sketches, matrices):
    parts = [
        jnp.einsum("km,tm->kt", s, m, preferred_element_type=f32)
        for s, m in zip(sketches, matrices)
    ]
    return tuple(lax.psum(p.astype(bf16), "tensor").astype(bf16) for p in parts)


def partials(token_rows, matrices):
    return tuple(
        jnp.dot(r, m, preferred_element_type=f32) for r, m in zip(token_rows, matrices)
    )


def orthonormal(parts):
    rows = [lax.psum(p.astype(bf16), "dp").astype(f32) for p in parts]
    grams = [lax.psum(gram_of(r).astype(bf16), "tensor").astype(f32) for r in rows]
    return tuple(solve_rows(g, r) for g, r in zip(grams, rows))


def feature_space(norm_in, query_grad, attn_out, handed, sketch_q, sketch_o):
    upstream = from_behind(handed, "section", -1)
    lefts = (norm_in[0], attn_out[0])
    rights = (query_grad[0], upstream[0])
    basis = orthonormal(partials(tokens_of((sketch_q[0], sketch_o[0]), rights), lefts))
    for _ in range(POWER):
        other = orthonormal(partials(tokens_of(basis, lefts), rights))
        basis = orthonormal(partials(tokens_of(other, rights), lefts))
    final = partials(tokens_of(basis, lefts), rights)
    raws = [lax.psum(p.astype(bf16), "dp").astype(f32) for p in final]
    energies = lax.psum(tuple(jnp.sum(r * r) for r in raws), "tensor")
    count = lax.axis_size("tensor")
    adapters = [
        r / jnp.sqrt(e / (r.size * count) + 1e-06) for r, e in zip(raws, energies)
    ]
    return (
        (basis[0] * 16.0)[None],
        adapters[0][None],
        (basis[1] * 16.0)[None],
        adapters[1][None],
    )


def swap(value, axis, bit):
    count = lax.axis_size(axis)
    return lax.ppermute(value, axis, [(i, i ^ bit) for i in range(count)])


def routed(value, sizes, token_bit, shifted):
    sections, dps, tensors = sizes
    side = tensors // 2
    pairs = []
    for s in range(sections):
        for z in range(dps):
            for t in range(tensors):
                to_t = t ^ side if t % side else t
                to_s = (s - 1) % sections if shifted and to_t >= side else s
                to = (to_s * dps + (z ^ token_bit)) * tensors + to_t
                pairs.append(((s * dps + z) * tensors + t, to))
    return lax.ppermute(value, ("section", "dp", "tensor"), pairs)


def window(ref, width, at):
    return ref.at[:, pl.ds(pl.multiple_of(at * width, width), width)]


def move(pairs, sems):
    copies = [pltpu.make_async_copy(src, dst, sems.at[n]) for n, (src, dst) in enumerate(pairs)]
    for c in copies:
        c.start()
    for c in copies:
        c.wait()


def give_kernel(dps, idx, norm, grad, attn, hand, sk_q, sk_o, give, sems):
    z, kind = idx[0], idx[3]
    wide, narrow = norm.shape[1], grad.shape[1]
    big_w, small_w = wide // dps, narrow // dps
    rows = RANK // dps

    def sketch(ref, width, start):
        part = ref.at[:, pl.ds(pl.multiple_of(z * width, width), width)]
        return [
            (
                part.at[i * rows : (i + 1) * rows],
                give.at[BLK:, i * (big_w + small_w) + start : i * (big_w + small_w) + start + width],
            )
            for i in range(dps)
        ]

    give[BLK:, :] = jnp.zeros((rows, wide + narrow), bf16)

    @pl.when(kind == 0)
    def _():
        pairs = [(hand, give.at[:BLK, :wide]), (attn, give.at[:BLK, wide:])]
        move(pairs + sketch(sk_o, big_w, 0), sems)

    @pl.when(kind == 1)
    def _():
        pairs = [(norm, give.at[:BLK, :wide]), (grad, give.at[:BLK, wide:])]
        move(pairs + sketch(sk_q, small_w, big_w), sems)


def merge_kernel(dps, idx, norm, grad, attn, hand, sk_q, sk_o, got, *refs):
    z, kind = idx[0], idx[3]
    bigs, smalls, sems = refs[:dps], refs[dps : 2 * dps], refs[-1]
    big_w, small_w = bigs[0].shape[1] // 2, smalls[0].shape[1] // 2
    wide, rows = norm.shape[1], RANK // dps

    def keep(wide_ref, thin_ref, extra):
        pairs = [extra]
        for d in range(dps):
            pairs.append((window(wide_ref, big_w, z ^ d), bigs[d].at[:, :big_w]))
            pairs.append((window(thin_ref, small_w, z ^ d), smalls[d].at[:BLK, :small_w]))
        copies = [
            pltpu.make_async_copy(src, dst, sems.at[n]) for n, (src, dst) in enumerate(pairs)
        ]
        for c in copies:
            c.start()
        fill()
        for c in copies:
            c.wait()

    def fill():
        for d in range(dps):
            at = pl.multiple_of((z ^ d) * big_w, big_w)
            bigs[d][:, big_w:] = got[:BLK, pl.ds(at, big_w)]
            at = pl.multiple_of(wide + (z ^ d) * small_w, small_w)
            smalls[d][:BLK, small_w:] = got[:BLK, pl.ds(at, small_w)]
        for i in range(dps):
            at = i * (big_w + small_w)
            below = slice(BLK + RANK + i * rows, BLK + RANK + (i + 1) * rows)
            smalls[0][below, :] = got[BLK:, at : at + big_w]
            below = slice(BLK + 2 * RANK + i * rows, BLK + 2 * RANK + (i + 1) * rows)
            smalls[0][below, small_w:] = got[BLK:, at + big_w : at + big_w + small_w]

    @pl.when(kind == 0)
    def _():
        smalls[0][BLK : BLK + RANK, :] = jnp.zeros((RANK, big_w), bf16)
        dst = smalls[0].at[BLK + 2 * RANK :, :small_w]
        keep(norm, grad, (window(sk_q, small_w, z), dst))

    @pl.when(kind == 1)
    def _():
        smalls[0][BLK + 2 * RANK :, :small_w] = jnp.zeros((RANK, small_w), bf16)
        dst = smalls[0].at[BLK : BLK + RANK, :]
        keep(hand, attn, (window(sk_o, big_w, z), dst))


def nt(a, b, precision=None):
    return lax.dot_general(
        a, b, (((1,), (1,)), ((), ())), precision=precision, preferred_element_type=f32
    )


def packed_rows(dps):
    per_gram = (dps * (dps - 1) // 2 + dps // 2) * BLK
    thin = pl.cdiv(per_gram + 16, 32) * 32
    rest = per_gram + dps * RANK + 16
    wide = pl.cdiv(thin + rest, 64) * 64 - thin
    return per_gram, thin, wide


def pack_gram(m, flat, dps):
    r = lax.broadcasted_iota(jnp.int32, (BLK, BLK), 0)
    c = lax.broadcasted_iota(jnp.int32, (BLK, BLK), 1)
    at, on = 0, []
    for i in range(dps):
        row = nt(m[i * BLK : (i + 1) * BLK, :], m[: (i + 1) * BLK, :])
        for j in range(i):
            flat[at : at + BLK, :] = row[:, j * BLK : (j + 1) * BLK].astype(bf16)
            at += BLK
        on.append(row[:, i * BLK :])
    for i in range(0, dps, 2):
        flat[at : at + BLK, :] = jnp.where(r > c, on[i], on[i + 1]).astype(bf16)
        at += BLK
    diagonals = [jnp.sum(jnp.where(r == c, v, 0.0), axis=0, keepdims=True) for v in on]
    diagonals.append(jnp.zeros((16 - dps, BLK), f32))
    return at, jnp.concatenate(diagonals, axis=0).astype(bf16)


def hand_out(core, flat, keep, send):
    half = flat.shape[0] // 2
    keep[...] = flat[pl.ds(pl.multiple_of(core * half, 16), half), :]
    send[...] = flat[pl.ds(pl.multiple_of((1 - core) * half, 16), half), :]


def thin_gram_kernel(dps, idx, *refs):
    z, core = idx[0], idx[2]
    smalls, small, keep, send, flat = refs[:dps], *refs[dps:]
    for d, ref in zip(FAR_FIRST, smalls):
        small[pl.ds(pl.multiple_of((z ^ d) * BLK, BLK), BLK), :] = ref[:BLK, :]
    at, diagonals = pack_gram(small, flat, dps)
    flat[at:, :] = jnp.zeros((flat.shape[0] - at, BLK), bf16)
    flat[at : at + 16, :] = diagonals
    hand_out(core, flat, keep, send)


def wide_gram_kernel(dps, idx, *refs):
    z, core = idx[0], idx[2]
    bigs, small, sk, big, keep, send, flat = refs[:dps], *refs[dps:]
    half_w = big.shape[1] // 2
    for d, ref in zip(FAR_FIRST, bigs):
        big[pl.ds(pl.multiple_of((z ^ d) * BLK, BLK), BLK), :] = ref[...]
    at, diagonals = pack_gram(big, flat, dps)
    first = (
        nt(sk[BLK : BLK + RANK, :], big[:, :half_w])
        + nt(sk[BLK + RANK : BLK + 2 * RANK, :], big[:, half_w:])
        + nt(sk[BLK + 2 * RANK :, :], small[...])
    ).astype(bf16)
    for i in range(dps):
        flat[at : at + RANK, :] = first[:, i * BLK : (i + 1) * BLK]
        at += RANK
    flat[at:, :] = jnp.zeros((flat.shape[0] - at, BLK), bf16)
    flat[at : at + 16, :] = diagonals
    hand_out(core, flat, keep, send)


def add_halves_kernel(idx, thin_mine, thin_got, wide_mine, wide_got, keep, send, both):
    size, bit, split_at = keep.shape[0], idx[0] % 2, thin_mine.shape[0]
    both[:split_at, :] = (thin_mine[...].astype(f32) + thin_got[...].astype(f32)).astype(bf16)
    both[split_at:, :] = (wide_mine[...].astype(f32) + wide_got[...].astype(f32)).astype(bf16)
    for out, which in ((keep, bit), (send, 1 - bit)):
        out[...] = both[pl.ds(pl.multiple_of(which * size, 16), size), :]


def add_kernel(mine, got, out):
    out[...] = (mine[...].astype(f32) + got[...].astype(f32)).astype(bf16)


def inverse_factor(gram):
    n, nb = gram.shape[0], 8
    rows = lax.broadcasted_iota(jnp.int32, (n, n), 0)
    cols = lax.broadcasted_iota(jnp.int32, (n, n), 1)
    work = jnp.concatenate([(rows == cols).astype(f32), gram], axis=1)
    count = n // nb
    slabs = [work[nb * s : nb * s + nb, :] for s in range(count)]
    sub = lax.broadcasted_iota(jnp.int32, (nb, 2 * n), 0)

    def lane(x, k):
        return jnp.broadcast_to(x[:, n + k : n + k + 1], (nb, 2 * n))

    def row(x, i):
        return jnp.broadcast_to(x[i : i + 1, :], (nb, 2 * n))

    done = []
    for b in range(count):
        cols_of = [lane(slabs[b], nb * b + j) for j in range(nb)]
        pivot_rows = [row(slabs[b], i) for i in range(nb)]
        splat = [[row(cols_of[j], i) for j in range(i + 1)] for i in range(nb)]
        below = {s: [lane(slabs[s], nb * b + j) for j in range(nb)] for s in range(b + 1, count)}
        out = None
        for k in range(nb):
            inv = 1.0 / splat[k][k]
            at = pivot_rows[k]
            final = at * lax.rsqrt(splat[k][k])
            out = final if out is None else jnp.where(sub == k, final, out)
            for i in range(k + 1, nb):
                mult = splat[i][k] * inv
                for j in range(k + 1, i + 1):
                    splat[i][j] = splat[i][j] - mult * splat[j][k]
                pivot_rows[i] = pivot_rows[i] - mult * at
            for s in range(b + 1, count):
                mult = below[s][k] * inv
                for j in range(k + 1, nb):
                    below[s][j] = below[s][j] - mult * splat[j][k]
                slabs[s] = slabs[s] - mult * at
        done.append(out)
    return jnp.concatenate(done, axis=0)[:, :n]


def split(x):
    high = x.astype(bf16)
    return high, (x - high.astype(f32)).astype(bf16)


def times(rows, gram):
    n = rows.shape[0]
    both = jnp.dot(jnp.concatenate(split(rows), axis=0), gram, preferred_element_type=f32)
    return both[:n] + both[n:]


def product(a, b):
    (ah, al), (bh, bl) = split(a), split(b)
    return jnp.dot(
        jnp.concatenate([ah, ah, al], axis=1),
        jnp.concatenate([bh, bl, bh], axis=0),
        preferred_element_type=f32,
    )


def product_nt(a, b):
    (ah, al), (bh, bl) = split(a), split(b)
    return nt(jnp.concatenate([ah, ah, al], axis=1), jnp.concatenate([bh, bl, bh], axis=1))


def chain_kernel(dps, counts, idx, *refs):
    z, out_half, core = idx[0], idx[1], idx[2]
    quarters, big, small, out, flat, thin, wide, left, right = refs[:4], *refs[4:]
    size, bit = quarters[0].shape[0], z % 2
    for n, ref in enumerate(quarters):
        which = 2 * (core ^ (n // 2)) + (bit ^ (n % 2))
        flat[pl.ds(pl.multiple_of(which * size, 16), size), :] = ref[...]
    per_gram, thin_rows, wide_rows = packed_rows(dps)
    for n in range(2):
        at, split_at = n * 2 * size, n * 2 * size + thin_rows // 2
        thin[n * (thin_rows // 2) : (n + 1) * (thin_rows // 2), :] = flat[at:split_at, :]
        wide[n * (wide_rows // 2) : (n + 1) * (wide_rows // 2), :] = flat[split_at : at + 2 * size, :]
    r = lax.broadcasted_iota(jnp.int32, (BLK, BLK), 0)
    c = lax.broadcasted_iota(jnp.int32, (BLK, BLK), 1)
    rows = jnp.concatenate(
        [wide[per_gram + i * RANK : per_gram + (i + 1) * RANK, :] for i in range(dps)], axis=1
    ).astype(f32)
    wide_diag = wide[per_gram + dps * RANK : per_gram + dps * RANK + 16, :].astype(f32)
    thin_diag = thin[per_gram : per_gram + 16, :].astype(f32)
    is_out = out_half == 1
    for gram, is_wide in ((left, out_half == 0), (right, is_out)):

        def block(n):
            part = slice(n * BLK, (n + 1) * BLK)
            return jnp.where(is_wide, wide[part, :].astype(f32), thin[part, :].astype(f32))

        def put(i, j, value):
            gram[i * BLK : (i + 1) * BLK, j * BLK : (j + 1) * BLK] = value.astype(bf16)

        n = 0
        for i in range(dps):
            for j in range(i):
                value = block(n)
                put(i, j, value)
                put(j, i, value.T)
                n += 1
        diag = jnp.where(is_wide, wide_diag, thin_diag)
        for i in range(0, dps, 2):
            value = block(n)
            turned = value.T
            put(i, i, jnp.where(r > c, value, jnp.where(r == c, diag[i : i + 1, :], turned)))
            put(
                i + 1,
                i + 1,
                jnp.where(r < c, value, jnp.where(r == c, diag[i + 1 : i + 2, :], turned)),
            )
            n += 1
    ahead = times(rows, left[...])
    gram = product_nt(ahead, rows)
    for step in range(2 * POWER):
        following = (right if step % 2 == 0 else left)[...]
        beyond = times(ahead, following)
        inner = product_nt(beyond, ahead)
        low_inv = inverse_factor(gram)
        rows = product(low_inv, ahead)
        if step < 2 * POWER - 1:
            gram = product_nt(product(low_inv, inner), low_inv)
            ahead = product(low_inv, beyond)
        else:
            ahead = times(rows, following)
            gram = product_nt(ahead, rows)
    low_inv = inverse_factor(gram)
    basis = product(low_inv, rows)
    rows = product(low_inv, ahead)
    energy = jnp.sum(times(rows, right[...]) * rows)
    count = jnp.where(out_half == 1, counts[0], counts[1]).astype(f32)
    scale = lax.rsqrt(jnp.full((1, 1), energy, f32) / count + 1e-06)
    coef_b, coef_a = basis.astype(bf16), rows.astype(bf16)
    for_big = jnp.where(is_out, coef_a, coef_b)
    for_small = jnp.where(is_out, coef_b, coef_a)
    scale_big = jnp.where(is_out, scale, 16.0)
    scale_small = jnp.where(is_out, 16.0, scale)
    big_w, small_w = big.shape[1] // 2, small.shape[1] // 2
    made_big = (jnp.dot(for_big, big[...], preferred_element_type=f32) * scale_big).astype(bf16)
    made_small = (jnp.dot(for_small, small[...], preferred_element_type=f32) * scale_small).astype(
        bf16
    )
    for n in range(2):
        part = slice(n * RANK, (n + 1) * RANK)
        out[part, :big_w] = made_big[:, n * big_w : (n + 1) * big_w]
        out[part, big_w:] = made_small[:, n * small_w : (n + 1) * small_w]


def place_kernel(dps, idx, *refs):
    z, kind = idx[0], idx[3]
    mine, theirs = refs[:dps], refs[dps : 2 * dps]
    b_q, a_q, b_o, a_o = refs[2 * dps :]
    big_w, small_w = b_q.shape[1] // dps, a_q.shape[1] // dps
    for d in range(dps):
        bigs = pl.ds(pl.multiple_of((z ^ d) * big_w, big_w), big_w)
        smalls = pl.ds(pl.multiple_of((z ^ d) * small_w, small_w), small_w)
        here, there = mine[d].at[:RANK], theirs[d].at[RANK:]
        for which, query, output in ((0, here, there), (1, there, here)):

            @pl.when(kind == which)
            def _():
                b_q[:, bigs] = query[:, :big_w]
                a_q[:, smalls] = query[:, big_w:].astype(f32)
                a_o[:, bigs] = output[:, :big_w].astype(f32)
                b_o[:, smalls] = output[:, big_w:]


def call(kernel, out_shapes, args, scratch=(), spaces=()):
    spaces = [SMEM] + [VMEM] * (len(args) - 1) if not spaces else spaces
    return pl.pallas_call(
        kernel,
        out_shape=out_shapes,
        in_specs=spaces,
        out_specs=jax.tree.map(lambda _: VMEM, out_shapes),
        scratch_shapes=list(scratch),
        compiler_params=pltpu.CompilerParams(vmem_limit_bytes=48 * 2**20),
    )(*args)


def token_space(sizes, norm_in, query_grad, attn_out, handed, sketch_q, sketch_o):
    _, dps, tensors = sizes
    side = tensors // 2

    def shape(*dims, dtype=bf16):
        return jax.ShapeDtypeStruct(dims, dtype)

    z, t = lax.axis_index("dp"), lax.axis_index("tensor")
    half, core = t // side, t % side
    idx = jnp.stack([z, half, core, half ^ core]).astype(jnp.int32)
    wide, narrow = norm_in.shape[2], query_grad.shape[2]
    big_w, small_w = wide // dps, narrow // dps
    tokens = dps * BLK
    args = tuple(
        pltpu.with_memory_space_constraint(v[0], pltpu.HBM)
        for v in (norm_in, query_grad, attn_out, handed, sketch_q, sketch_o)
    )
    in_hbm = [SMEM] + [pl.BlockSpec(memory_space=pltpu.HBM)] * len(args)

    give = call(
        functools.partial(give_kernel, dps),
        shape(BLK + RANK // dps, wide + narrow),
        (idx, *args),
        [pltpu.SemaphoreType.DMA((2 + dps,))],
        in_hbm,
    )
    got = swap(give, "tensor", 1)
    packed = call(
        functools.partial(merge_kernel, dps),
        [shape(BLK, 2 * big_w)] * dps
        + [shape(BLK + 3 * RANK, 2 * small_w)]
        + [shape(BLK, 2 * small_w)] * (dps - 1),
        (idx, *args, got),
        [pltpu.SemaphoreType.DMA((2 * dps + 1,))],
        in_hbm + [VMEM],
    )
    smalls = [routed(packed[dps + d], sizes, d, False) for d in FAR_FIRST]
    bigs = [routed(packed[d], sizes, d, True) for d in FAR_FIRST[:2]]

    _, thin_rows, wide_rows = packed_rows(dps)

    def gram(kernel, m, rows, operands):
        m, keep, send = call(
            functools.partial(kernel, dps),
            [m, shape(rows // 2, BLK), shape(rows // 2, BLK)],
            (idx, *operands),
            [pltpu.VMEM((rows, BLK), bf16)],
        )
        return m, keep, swap(send, "tensor", 1)

    small, *thin = gram(thin_gram_kernel, shape(tokens, 2 * small_w), thin_rows, smalls)
    near = lax.optimization_barrier((packed[1], packed[0], thin[0]))
    thin[0] = near[2]
    bigs += [routed(v, sizes, d, True) for v, d in zip(near, FAR_FIRST[2:])]
    bigs[0], thin[1] = lax.optimization_barrier((bigs[0], thin[1]))
    big, *rest = gram(
        wide_gram_kernel, shape(tokens, 2 * big_w), wide_rows, (*bigs, small, smalls[-1])
    )
    total = thin_rows + wide_rows
    quarter = shape(total // 4, BLK)
    keep, send = call(
        add_halves_kernel,
        [quarter] * 2,
        (idx, *thin, *rest),
        [pltpu.VMEM((total // 2, BLK), bf16)],
    )
    for bit, value in ((1, send), (2, None)):
        value = swap(keep if value is None else value, "dp", bit)
        keep = call(add_kernel, quarter, (keep, value), (), [VMEM] * 2)
    beside = swap(keep, "dp", 1)
    quarters = (keep, beside, swap(keep, "tensor", 1), swap(beside, "tensor", 1))

    counts = (RANK * wide * tensors, RANK * narrow * tensors)
    out = call(
        functools.partial(chain_kernel, dps, counts),
        shape(2 * RANK, big_w + small_w),
        (idx, *quarters, big, small),
        [
            pltpu.VMEM((total, BLK), bf16),
            pltpu.VMEM((thin_rows, BLK), bf16),
            pltpu.VMEM((wide_rows, BLK), bf16),
            pltpu.VMEM((tokens, tokens), bf16),
            pltpu.VMEM((tokens, tokens), bf16),
        ],
    )
    mine = [routed(out, sizes, d, False) for d in range(3)]
    mine.append(swap(mine[2], "dp", 1))
    theirs = [swap(v, "tensor", 1) for v in mine]
    outs = call(
        functools.partial(place_kernel, dps),
        [
            shape(RANK, wide),
            shape(RANK, narrow, dtype=f32),
            shape(RANK, narrow),
            shape(RANK, wide, dtype=f32),
        ],
        (idx, *mine, *theirs),
    )
    return tuple(o[None] for o in outs)


def solution(mesh):
    sizes = tuple(mesh.shape[axis] for axis in ("section", "dp", "tensor"))
    _, dps, tensors = sizes

    def body(norm_in, query_grad, attn_out, handed, sketch_q, sketch_o):
        args = (norm_in, query_grad, attn_out, handed, sketch_q, sketch_o)
        fits = (
            dps == 4
            and tensors == 4
            and norm_in.shape[1] == BLK
            and sketch_q.shape[1] == RANK
            and norm_in.shape[2] == handed.shape[2]
            and query_grad.shape[2] == attn_out.shape[2]
            and norm_in.shape[2] == 2 * query_grad.shape[2]
            and query_grad.shape[2] % (dps * 128) == 0
        )
        return token_space(sizes, *args) if fits else feature_space(*args)

    return jax.shard_map(
        body,
        mesh=mesh,
        in_specs=(P("section", "dp", "tensor"),) * 4 + (P("section", None, "tensor"),) * 2,
        out_specs=(P("section", None, "tensor"),) * 4,
        check_vma=False,
    )
```

```python
import functools

import jax
import jax.numpy as jnp
from jax import lax
from jax.experimental import pallas as pl
from jax.experimental.pallas import tpu as pltpu
from jax.sharding import PartitionSpec as P

RANK = 64
POWER = 2
BLK = 128
FAR_FIRST = (2, 3, 1, 0)

precise = lax.Precision.HIGHEST
f32 = jnp.float32
bf16 = jnp.bfloat16
VMEM = pl.BlockSpec(memory_space=pltpu.VMEM)
SMEM = pl.BlockSpec(memory_space=pltpu.SMEM)


def from_behind(value, axis, steps):
    count = lax.axis_size(axis)
    pairs = [(source, (source + steps) % count) for source in range(count)]
    return lax.ppermute(value, axis, pairs)


def gram_of(row_block):
    return jnp.dot(row_block, row_block.T, precision=precise, preferred_element_type=f32)


def solve_rows(gram_rows, row_block):
    low_factor = jnp.linalg.cholesky(gram_rows)
    solved = lax.linalg.triangular_solve(low_factor, row_block, left_side=True, lower=True)
    return solved.astype(bf16)


def tokens_of(sketches, matrices):
    parts = [
        jnp.einsum("km,tm->kt", s, m, preferred_element_type=f32)
        for s, m in zip(sketches, matrices)
    ]
    return tuple(lax.psum(p.astype(bf16), "tensor").astype(bf16) for p in parts)


def partials(token_rows, matrices):
    return tuple(
        jnp.dot(r, m, preferred_element_type=f32) for r, m in zip(token_rows, matrices)
    )


def orthonormal(parts):
    rows = [lax.psum(p.astype(bf16), "dp").astype(f32) for p in parts]
    grams = [lax.psum(gram_of(r).astype(bf16), "tensor").astype(f32) for r in rows]
    return tuple(solve_rows(g, r) for g, r in zip(grams, rows))


def feature_space(norm_in, query_grad, attn_out, handed, sketch_q, sketch_o):
    upstream = from_behind(handed, "section", -1)
    lefts = (norm_in[0], attn_out[0])
    rights = (query_grad[0], upstream[0])
    basis = orthonormal(partials(tokens_of((sketch_q[0], sketch_o[0]), rights), lefts))
    for _ in range(POWER):
        other = orthonormal(partials(tokens_of(basis, lefts), rights))
        basis = orthonormal(partials(tokens_of(other, rights), lefts))
    final = partials(tokens_of(basis, lefts), rights)
    raws = [lax.psum(p.astype(bf16), "dp").astype(f32) for p in final]
    energies = lax.psum(tuple(jnp.sum(r * r) for r in raws), "tensor")
    count = lax.axis_size("tensor")
    adapters = [
        r / jnp.sqrt(e / (r.size * count) + 1e-06) for r, e in zip(raws, energies)
    ]
    return (
        (basis[0] * 16.0)[None],
        adapters[0][None],
        (basis[1] * 16.0)[None],
        adapters[1][None],
    )


def swap(value, axis, bit):
    count = lax.axis_size(axis)
    return lax.ppermute(value, axis, [(i, i ^ bit) for i in range(count)])


def routed(value, sizes, token_bit, shifted):
    sections, dps, tensors = sizes
    side = tensors // 2
    pairs = []
    for s in range(sections):
        for z in range(dps):
            for t in range(tensors):
                to_t = t ^ side if t % side else t
                to_s = (s - 1) % sections if shifted and to_t >= side else s
                to = (to_s * dps + (z ^ token_bit)) * tensors + to_t
                pairs.append(((s * dps + z) * tensors + t, to))
    return lax.ppermute(value, ("section", "dp", "tensor"), pairs)


def window(ref, width, at):
    return ref.at[:, pl.ds(pl.multiple_of(at * width, width), width)]


def move(pairs, sems):
    copies = [pltpu.make_async_copy(src, dst, sems.at[n]) for n, (src, dst) in enumerate(pairs)]
    for c in copies:
        c.start()
    for c in copies:
        c.wait()


def give_kernel(dps, idx, norm, grad, attn, hand, sk_q, sk_o, give, sems):
    z, kind = idx[0], idx[3]
    wide, narrow = norm.shape[1], grad.shape[1]
    big_w, small_w = wide // dps, narrow // dps
    rows = RANK // dps

    def sketch(ref, width, start):
        part = ref.at[:, pl.ds(pl.multiple_of(z * width, width), width)]
        return [
            (
                part.at[i * rows : (i + 1) * rows],
                give.at[BLK:, i * (big_w + small_w) + start : i * (big_w + small_w) + start + width],
            )
            for i in range(dps)
        ]

    give[BLK:, :] = jnp.zeros((rows, wide + narrow), bf16)

    @pl.when(kind == 0)
    def _():
        pairs = [(hand, give.at[:BLK, :wide]), (attn, give.at[:BLK, wide:])]
        move(pairs + sketch(sk_o, big_w, 0), sems)

    @pl.when(kind == 1)
    def _():
        pairs = [(norm, give.at[:BLK, :wide]), (grad, give.at[:BLK, wide:])]
        move(pairs + sketch(sk_q, small_w, big_w), sems)


def merge_kernel(dps, idx, norm, grad, attn, hand, sk_q, sk_o, got, *refs):
    z, kind = idx[0], idx[3]
    bigs, smalls, sems = refs[:dps], refs[dps : 2 * dps], refs[-1]
    big_w, small_w = bigs[0].shape[1] // 2, smalls[0].shape[1] // 2
    wide, rows = norm.shape[1], RANK // dps

    def keep(wide_ref, thin_ref, extra):
        pairs = [extra]
        for d in range(dps):
            pairs.append((window(wide_ref, big_w, z ^ d), bigs[d].at[:, :big_w]))
            pairs.append((window(thin_ref, small_w, z ^ d), smalls[d].at[:BLK, :small_w]))
        copies = [
            pltpu.make_async_copy(src, dst, sems.at[n]) for n, (src, dst) in enumerate(pairs)
        ]
        for c in copies:
            c.start()
        fill()
        for c in copies:
            c.wait()

    def fill():
        for d in range(dps):
            at = pl.multiple_of((z ^ d) * big_w, big_w)
            bigs[d][:, big_w:] = got[:BLK, pl.ds(at, big_w)]
            at = pl.multiple_of(wide + (z ^ d) * small_w, small_w)
            smalls[d][:BLK, small_w:] = got[:BLK, pl.ds(at, small_w)]
        for i in range(dps):
            at = i * (big_w + small_w)
            below = slice(BLK + RANK + i * rows, BLK + RANK + (i + 1) * rows)
            smalls[0][below, :] = got[BLK:, at : at + big_w]
            below = slice(BLK + 2 * RANK + i * rows, BLK + 2 * RANK + (i + 1) * rows)
            smalls[0][below, small_w:] = got[BLK:, at + big_w : at + big_w + small_w]

    @pl.when(kind == 0)
    def _():
        smalls[0][BLK : BLK + RANK, :] = jnp.zeros((RANK, big_w), bf16)
        dst = smalls[0].at[BLK + 2 * RANK :, :small_w]
        keep(norm, grad, (window(sk_q, small_w, z), dst))

    @pl.when(kind == 1)
    def _():
        smalls[0][BLK + 2 * RANK :, :small_w] = jnp.zeros((RANK, small_w), bf16)
        dst = smalls[0].at[BLK : BLK + RANK, :]
        keep(hand, attn, (window(sk_o, big_w, z), dst))


def nt(a, b, precision=None):
    return lax.dot_general(
        a, b, (((1,), (1,)), ((), ())), precision=precision, preferred_element_type=f32
    )


def packed_rows(dps):
    per_gram = (dps * (dps - 1) // 2 + dps // 2) * BLK
    thin = pl.cdiv(per_gram + 16, 32) * 32
    rest = per_gram + dps * RANK + 16
    wide = pl.cdiv(thin + rest, 64) * 64 - thin
    return per_gram, thin, wide


def pack_gram(m, flat, dps):
    r = lax.broadcasted_iota(jnp.int32, (BLK, BLK), 0)
    c = lax.broadcasted_iota(jnp.int32, (BLK, BLK), 1)
    at, on = 0, []
    for i in range(dps):
        row = nt(m[i * BLK : (i + 1) * BLK, :], m[: (i + 1) * BLK, :])
        for j in range(i):
            flat[at : at + BLK, :] = row[:, j * BLK : (j + 1) * BLK].astype(bf16)
            at += BLK
        on.append(row[:, i * BLK :])
    for i in range(0, dps, 2):
        flat[at : at + BLK, :] = jnp.where(r > c, on[i], on[i + 1]).astype(bf16)
        at += BLK
    diagonals = [jnp.sum(jnp.where(r == c, v, 0.0), axis=0, keepdims=True) for v in on]
    diagonals.append(jnp.zeros((16 - dps, BLK), f32))
    return at, jnp.concatenate(diagonals, axis=0).astype(bf16)


def hand_out(core, flat, keep, send):
    half = flat.shape[0] // 2
    keep[...] = flat[pl.ds(pl.multiple_of(core * half, 16), half), :]
    send[...] = flat[pl.ds(pl.multiple_of((1 - core) * half, 16), half), :]


def thin_gram_kernel(dps, idx, *refs):
    z, core = idx[0], idx[2]
    smalls, small, keep, send, flat = refs[:dps], *refs[dps:]
    for d, ref in zip(FAR_FIRST, smalls):
        small[pl.ds(pl.multiple_of((z ^ d) * BLK, BLK), BLK), :] = ref[:BLK, :]
    at, diagonals = pack_gram(small, flat, dps)
    flat[at:, :] = jnp.zeros((flat.shape[0] - at, BLK), bf16)
    flat[at : at + 16, :] = diagonals
    hand_out(core, flat, keep, send)


def wide_gram_kernel(dps, idx, *refs):
    z, core = idx[0], idx[2]
    bigs, small, sk, big, keep, send, flat = refs[:dps], *refs[dps:]
    half_w = big.shape[1] // 2
    for d, ref in zip(FAR_FIRST, bigs):
        big[pl.ds(pl.multiple_of((z ^ d) * BLK, BLK), BLK), :] = ref[...]
    at, diagonals = pack_gram(big, flat, dps)
    first = (
        nt(sk[BLK : BLK + RANK, :], big[:, :half_w])
        + nt(sk[BLK + RANK : BLK + 2 * RANK, :], big[:, half_w:])
        + nt(sk[BLK + 2 * RANK :, :], small[...])
    ).astype(bf16)
    for i in range(dps):
        flat[at : at + RANK, :] = first[:, i * BLK : (i + 1) * BLK]
        at += RANK
    flat[at:, :] = jnp.zeros((flat.shape[0] - at, BLK), bf16)
    flat[at : at + 16, :] = diagonals
    hand_out(core, flat, keep, send)


def add_halves_kernel(idx, thin_mine, thin_got, wide_mine, wide_got, keep, send, both):
    size, bit, split_at = keep.shape[0], idx[0] % 2, thin_mine.shape[0]
    both[:split_at, :] = (thin_mine[...].astype(f32) + thin_got[...].astype(f32)).astype(bf16)
    both[split_at:, :] = (wide_mine[...].astype(f32) + wide_got[...].astype(f32)).astype(bf16)
    for out, which in ((keep, bit), (send, 1 - bit)):
        out[...] = both[pl.ds(pl.multiple_of(which * size, 16), size), :]


def add_kernel(mine, got, out):
    out[...] = (mine[...].astype(f32) + got[...].astype(f32)).astype(bf16)


def inverse_factor(gram):
    n, nb = gram.shape[0], 8
    rows = lax.broadcasted_iota(jnp.int32, (n, n), 0)
    cols = lax.broadcasted_iota(jnp.int32, (n, n), 1)
    work = jnp.concatenate([(rows == cols).astype(f32), gram], axis=1)
    count = n // nb
    slabs = [work[nb * s : nb * s + nb, :] for s in range(count)]
    sub = lax.broadcasted_iota(jnp.int32, (nb, 2 * n), 0)

    def lane(x, k):
        return jnp.broadcast_to(x[:, n + k : n + k + 1], (nb, 2 * n))

    def row(x, i):
        return jnp.broadcast_to(x[i : i + 1, :], (nb, 2 * n))

    done = []
    for b in range(count):
        cols_of = [lane(slabs[b], nb * b + j) for j in range(nb)]
        pivot_rows = [row(slabs[b], i) for i in range(nb)]
        splat = [[row(cols_of[j], i) for j in range(i + 1)] for i in range(nb)]
        below = {s: [lane(slabs[s], nb * b + j) for j in range(nb)] for s in range(b + 1, count)}
        out = None
        for k in range(nb):
            inv = 1.0 / splat[k][k]
            at = pivot_rows[k]
            final = at * lax.rsqrt(splat[k][k])
            out = final if out is None else jnp.where(sub == k, final, out)
            for i in range(k + 1, nb):
                mult = splat[i][k] * inv
                for j in range(k + 1, i + 1):
                    splat[i][j] = splat[i][j] - mult * splat[j][k]
                pivot_rows[i] = pivot_rows[i] - mult * at
            for s in range(b + 1, count):
                mult = below[s][k] * inv
                for j in range(k + 1, nb):
                    below[s][j] = below[s][j] - mult * splat[j][k]
                slabs[s] = slabs[s] - mult * at
        done.append(out)
    return jnp.concatenate(done, axis=0)[:, :n]


def split(x):
    high = x.astype(bf16)
    return high, (x - high.astype(f32)).astype(bf16)


def times(rows, gram):
    n = rows.shape[0]
    both = jnp.dot(jnp.concatenate(split(rows), axis=0), gram, preferred_element_type=f32)
    return both[:n] + both[n:]


def product(a, b):
    (ah, al), (bh, bl) = split(a), split(b)
    return jnp.dot(
        jnp.concatenate([ah, ah, al], axis=1),
        jnp.concatenate([bh, bl, bh], axis=0),
        preferred_element_type=f32,
    )


def product_nt(a, b):
    (ah, al), (bh, bl) = split(a), split(b)
    return nt(jnp.concatenate([ah, ah, al], axis=1), jnp.concatenate([bh, bl, bh], axis=1))


def chain_kernel(dps, counts, idx, *refs):
    z, out_half, core = idx[0], idx[1], idx[2]
    quarters, big, small, out, flat, thin, wide, left, right = refs[:4], *refs[4:]
    size, bit = quarters[0].shape[0], z % 2
    for n, ref in enumerate(quarters):
        which = 2 * (core ^ (n // 2)) + (bit ^ (n % 2))
        flat[pl.ds(pl.multiple_of(which * size, 16), size), :] = ref[...]
    per_gram, thin_rows, wide_rows = packed_rows(dps)
    for n in range(2):
        at, split_at = n * 2 * size, n * 2 * size + thin_rows // 2
        thin[n * (thin_rows // 2) : (n + 1) * (thin_rows // 2), :] = flat[at:split_at, :]
        wide[n * (wide_rows // 2) : (n + 1) * (wide_rows // 2), :] = flat[split_at : at + 2 * size, :]
    r = lax.broadcasted_iota(jnp.int32, (BLK, BLK), 0)
    c = lax.broadcasted_iota(jnp.int32, (BLK, BLK), 1)
    rows = jnp.concatenate(
        [wide[per_gram + i * RANK : per_gram + (i + 1) * RANK, :] for i in range(dps)], axis=1
    ).astype(f32)
    wide_diag = wide[per_gram + dps * RANK : per_gram + dps * RANK + 16, :].astype(f32)
    thin_diag = thin[per_gram : per_gram + 16, :].astype(f32)
    is_out = out_half == 1
    for gram, is_wide in ((left, out_half == 0), (right, is_out)):

        def block(n):
            part = slice(n * BLK, (n + 1) * BLK)
            return jnp.where(is_wide, wide[part, :].astype(f32), thin[part, :].astype(f32))

        def put(i, j, value):
            gram[i * BLK : (i + 1) * BLK, j * BLK : (j + 1) * BLK] = value.astype(bf16)

        n = 0
        for i in range(dps):
            for j in range(i):
                value = block(n)
                put(i, j, value)
                put(j, i, value.T)
                n += 1
        diag = jnp.where(is_wide, wide_diag, thin_diag)
        for i in range(0, dps, 2):
            value = block(n)
            turned = value.T
            put(i, i, jnp.where(r > c, value, jnp.where(r == c, diag[i : i + 1, :], turned)))
            put(
                i + 1,
                i + 1,
                jnp.where(r < c, value, jnp.where(r == c, diag[i + 1 : i + 2, :], turned)),
            )
            n += 1
    ahead = times(rows, left[...])
    gram = product_nt(ahead, rows)
    for step in range(2 * POWER):
        following = (right if step % 2 == 0 else left)[...]
        beyond = times(ahead, following)
        inner = product_nt(beyond, ahead)
        low_inv = inverse_factor(gram)
        rows = product(low_inv, ahead)
        if step < 2 * POWER - 1:
            gram = product_nt(product(low_inv, inner), low_inv)
            ahead = product(low_inv, beyond)
        else:
            ahead = times(rows, following)
            gram = product_nt(ahead, rows)
    low_inv = inverse_factor(gram)
    basis = product(low_inv, rows)
    rows = product(low_inv, ahead)
    energy = jnp.sum(times(rows, right[...]) * rows)
    count = jnp.where(out_half == 1, counts[0], counts[1]).astype(f32)
    scale = lax.rsqrt(jnp.full((1, 1), energy, f32) / count + 1e-06)
    coef_b, coef_a = basis.astype(bf16), rows.astype(bf16)
    for_big = jnp.where(is_out, coef_a, coef_b)
    for_small = jnp.where(is_out, coef_b, coef_a)
    scale_big = jnp.where(is_out, scale, 16.0)
    scale_small = jnp.where(is_out, 16.0, scale)
    big_w, small_w = big.shape[1] // 2, small.shape[1] // 2
    made_big = (jnp.dot(for_big, big[...], preferred_element_type=f32) * scale_big).astype(bf16)
    made_small = (jnp.dot(for_small, small[...], preferred_element_type=f32) * scale_small).astype(
        bf16
    )
    for n in range(2):
        part = slice(n * RANK, (n + 1) * RANK)
        out[part, :big_w] = made_big[:, n * big_w : (n + 1) * big_w]
        out[part, big_w:] = made_small[:, n * small_w : (n + 1) * small_w]


def place_kernel(dps, idx, *refs):
    z, kind = idx[0], idx[3]
    mine, theirs = refs[:dps], refs[dps : 2 * dps]
    b_q, a_q, b_o, a_o = refs[2 * dps :]
    big_w, small_w = b_q.shape[1] // dps, a_q.shape[1] // dps
    for d in range(dps):
        bigs = pl.ds(pl.multiple_of((z ^ d) * big_w, big_w), big_w)
        smalls = pl.ds(pl.multiple_of((z ^ d) * small_w, small_w), small_w)
        here, there = mine[d].at[:RANK], theirs[d].at[RANK:]
        for which, query, output in ((0, here, there), (1, there, here)):

            @pl.when(kind == which)
            def _():
                b_q[:, bigs] = query[:, :big_w]
                a_q[:, smalls] = query[:, big_w:].astype(f32)
                a_o[:, bigs] = output[:, :big_w].astype(f32)
                b_o[:, smalls] = output[:, big_w:]


def call(kernel, out_shapes, args, scratch=(), spaces=()):
    spaces = [SMEM] + [VMEM] * (len(args) - 1) if not spaces else spaces
    return pl.pallas_call(
        kernel,
        out_shape=out_shapes,
        in_specs=spaces,
        out_specs=jax.tree.map(lambda _: VMEM, out_shapes),
        scratch_shapes=list(scratch),
        compiler_params=pltpu.CompilerParams(vmem_limit_bytes=48 * 2**20),
    )(*args)


def token_space(sizes, norm_in, query_grad, attn_out, handed, sketch_q, sketch_o):
    _, dps, tensors = sizes
    side = tensors // 2

    def shape(*dims, dtype=bf16):
        return jax.ShapeDtypeStruct(dims, dtype)

    z, t = lax.axis_index("dp"), lax.axis_index("tensor")
    half, core = t // side, t % side
    idx = jnp.stack([z, half, core, half ^ core]).astype(jnp.int32)
    wide, narrow = norm_in.shape[2], query_grad.shape[2]
    big_w, small_w = wide // dps, narrow // dps
    tokens = dps * BLK
    args = tuple(
        pltpu.with_memory_space_constraint(v[0], pltpu.HBM)
        for v in (norm_in, query_grad, attn_out, handed, sketch_q, sketch_o)
    )
    in_hbm = [SMEM] + [pl.BlockSpec(memory_space=pltpu.HBM)] * len(args)

    give = call(
        functools.partial(give_kernel, dps),
        shape(BLK + RANK // dps, wide + narrow),
        (idx, *args),
        [pltpu.SemaphoreType.DMA((2 + dps,))],
        in_hbm,
    )
    got = swap(give, "tensor", 1)
    packed = call(
        functools.partial(merge_kernel, dps),
        [shape(BLK, 2 * big_w)] * dps
        + [shape(BLK + 3 * RANK, 2 * small_w)]
        + [shape(BLK, 2 * small_w)] * (dps - 1),
        (idx, *args, got),
        [pltpu.SemaphoreType.DMA((2 * dps + 1,))],
        in_hbm + [VMEM],
    )
    smalls = [routed(packed[dps + d], sizes, d, False) for d in FAR_FIRST]
    bigs = [routed(packed[d], sizes, d, True) for d in FAR_FIRST[:-1]]

    _, thin_rows, wide_rows = packed_rows(dps)

    def gram(kernel, m, rows, operands):
        m, keep, send = call(
            functools.partial(kernel, dps),
            [m, shape(rows // 2, BLK), shape(rows // 2, BLK)],
            (idx, *operands),
            [pltpu.VMEM((rows, BLK), bf16)],
        )
        return m, keep, swap(send, "tensor", 1)

    small, *thin = gram(thin_gram_kernel, shape(tokens, 2 * small_w), thin_rows, smalls)
    last, thin[0] = lax.optimization_barrier((packed[0], thin[0]))
    bigs.append(routed(last, sizes, 0, True))
    bigs[0], thin[1] = lax.optimization_barrier((bigs[0], thin[1]))
    big, *rest = gram(
        wide_gram_kernel, shape(tokens, 2 * big_w), wide_rows, (*bigs, small, smalls[-1])
    )
    total = thin_rows + wide_rows
    quarter = shape(total // 4, BLK)
    keep, send = call(
        add_halves_kernel,
        [quarter] * 2,
        (idx, *thin, *rest),
        [pltpu.VMEM((total // 2, BLK), bf16)],
    )
    for bit, value in ((1, send), (2, None)):
        value = swap(keep if value is None else value, "dp", bit)
        keep = call(add_kernel, quarter, (keep, value), (), [VMEM] * 2)
    beside = swap(keep, "dp", 1)
    quarters = (keep, beside, swap(keep, "tensor", 1), swap(beside, "tensor", 1))

    counts = (RANK * wide * tensors, RANK * narrow * tensors)
    out = call(
        functools.partial(chain_kernel, dps, counts),
        shape(2 * RANK, big_w + small_w),
        (idx, *quarters, big, small),
        [
            pltpu.VMEM((total, BLK), bf16),
            pltpu.VMEM((thin_rows, BLK), bf16),
            pltpu.VMEM((wide_rows, BLK), bf16),
            pltpu.VMEM((tokens, tokens), bf16),
            pltpu.VMEM((tokens, tokens), bf16),
        ],
    )
    mine = [routed(out, sizes, d, False) for d in range(3)]
    mine.append(swap(mine[2], "dp", 1))
    theirs = [swap(v, "tensor", 1) for v in mine]
    outs = call(
        functools.partial(place_kernel, dps),
        [
            shape(RANK, wide),
            shape(RANK, narrow, dtype=f32),
            shape(RANK, narrow),
            shape(RANK, wide, dtype=f32),
        ],
        (idx, *mine, *theirs),
    )
    return tuple(o[None] for o in outs)


def solution(mesh):
    sizes = tuple(mesh.shape[axis] for axis in ("section", "dp", "tensor"))
    _, dps, tensors = sizes

    def body(norm_in, query_grad, attn_out, handed, sketch_q, sketch_o):
        args = (norm_in, query_grad, attn_out, handed, sketch_q, sketch_o)
        fits = (
            dps == 4
            and tensors == 4
            and norm_in.shape[1] == BLK
            and sketch_q.shape[1] == RANK
            and norm_in.shape[2] == handed.shape[2]
            and query_grad.shape[2] == attn_out.shape[2]
            and norm_in.shape[2] == 2 * query_grad.shape[2]
            and query_grad.shape[2] % (dps * 128) == 0
        )
        return token_space(sizes, *args) if fits else feature_space(*args)

    return jax.shard_map(
        body,
        mesh=mesh,
        in_specs=(P("section", "dp", "tensor"),) * 4 + (P("section", None, "tensor"),) * 2,
        out_specs=(P("section", None, "tensor"),) * 4,
        check_vma=False,
    )
```

```python
import functools

import jax
import jax.numpy as jnp
from jax import lax
from jax.experimental import pallas as pl
from jax.experimental.pallas import tpu as pltpu
from jax.sharding import PartitionSpec as P

RANK = 64
POWER = 2
BLK = 128
FAR_FIRST = (2, 3, 1, 0)

precise = lax.Precision.HIGHEST
f32 = jnp.float32
bf16 = jnp.bfloat16
VMEM = pl.BlockSpec(memory_space=pltpu.VMEM)
SMEM = pl.BlockSpec(memory_space=pltpu.SMEM)


def from_behind(value, axis, steps):
    count = lax.axis_size(axis)
    pairs = [(source, (source + steps) % count) for source in range(count)]
    return lax.ppermute(value, axis, pairs)


def gram_of(row_block):
    return jnp.dot(row_block, row_block.T, precision=precise, preferred_element_type=f32)


def solve_rows(gram_rows, row_block):
    low_factor = jnp.linalg.cholesky(gram_rows)
    solved = lax.linalg.triangular_solve(low_factor, row_block, left_side=True, lower=True)
    return solved.astype(bf16)


def tokens_of(sketches, matrices):
    parts = [
        jnp.einsum("km,tm->kt", s, m, preferred_element_type=f32)
        for s, m in zip(sketches, matrices)
    ]
    return tuple(lax.psum(p.astype(bf16), "tensor").astype(bf16) for p in parts)


def partials(token_rows, matrices):
    return tuple(
        jnp.dot(r, m, preferred_element_type=f32) for r, m in zip(token_rows, matrices)
    )


def orthonormal(parts):
    rows = [lax.psum(p.astype(bf16), "dp").astype(f32) for p in parts]
    grams = [lax.psum(gram_of(r).astype(bf16), "tensor").astype(f32) for r in rows]
    return tuple(solve_rows(g, r) for g, r in zip(grams, rows))


def feature_space(norm_in, query_grad, attn_out, handed, sketch_q, sketch_o):
    upstream = from_behind(handed, "section", -1)
    lefts = (norm_in[0], attn_out[0])
    rights = (query_grad[0], upstream[0])
    basis = orthonormal(partials(tokens_of((sketch_q[0], sketch_o[0]), rights), lefts))
    for _ in range(POWER):
        other = orthonormal(partials(tokens_of(basis, lefts), rights))
        basis = orthonormal(partials(tokens_of(other, rights), lefts))
    final = partials(tokens_of(basis, lefts), rights)
    raws = [lax.psum(p.astype(bf16), "dp").astype(f32) for p in final]
    energies = lax.psum(tuple(jnp.sum(r * r) for r in raws), "tensor")
    count = lax.axis_size("tensor")
    adapters = [
        r / jnp.sqrt(e / (r.size * count) + 1e-06) for r, e in zip(raws, energies)
    ]
    return (
        (basis[0] * 16.0)[None],
        adapters[0][None],
        (basis[1] * 16.0)[None],
        adapters[1][None],
    )


def swap(value, axis, bit):
    count = lax.axis_size(axis)
    return lax.ppermute(value, axis, [(i, i ^ bit) for i in range(count)])


def routed(value, sizes, token_bit, shifted):
    sections, dps, tensors = sizes
    side = tensors // 2
    pairs = []
    for s in range(sections):
        for z in range(dps):
            for t in range(tensors):
                to_t = t ^ side if t % side else t
                to_s = (s - 1) % sections if shifted and to_t >= side else s
                to = (to_s * dps + (z ^ token_bit)) * tensors + to_t
                pairs.append(((s * dps + z) * tensors + t, to))
    return lax.ppermute(value, ("section", "dp", "tensor"), pairs)


def window(ref, width, at):
    return ref.at[:, pl.ds(pl.multiple_of(at * width, width), width)]


def move(pairs, sems):
    copies = [pltpu.make_async_copy(src, dst, sems.at[n]) for n, (src, dst) in enumerate(pairs)]
    for c in copies:
        c.start()
    for c in copies:
        c.wait()


def give_kernel(dps, idx, norm, grad, attn, hand, sk_q, sk_o, give, sems):
    z, kind = idx[0], idx[3]
    wide, narrow = norm.shape[1], grad.shape[1]
    big_w, small_w = wide // dps, narrow // dps
    rows = RANK // dps

    def sketch(ref, width, start):
        part = ref.at[:, pl.ds(pl.multiple_of(z * width, width), width)]
        return [
            (
                part.at[i * rows : (i + 1) * rows],
                give.at[BLK:, i * (big_w + small_w) + start : i * (big_w + small_w) + start + width],
            )
            for i in range(dps)
        ]

    give[BLK:, :] = jnp.zeros((rows, wide + narrow), bf16)

    @pl.when(kind == 0)
    def _():
        pairs = [(hand, give.at[:BLK, :wide]), (attn, give.at[:BLK, wide:])]
        move(pairs + sketch(sk_o, big_w, 0), sems)

    @pl.when(kind == 1)
    def _():
        pairs = [(norm, give.at[:BLK, :wide]), (grad, give.at[:BLK, wide:])]
        move(pairs + sketch(sk_q, small_w, big_w), sems)


def merge_kernel(dps, kind, fill, pairs, sems):
    for which in (0, 1):

        @pl.when(kind == which)
        def _():
            copies = [
                pltpu.make_async_copy(src, dst, sems.at[n])
                for n, (src, dst) in enumerate(pairs[which])
            ]
            for c in copies:
                c.start()
            fill(which)
            for c in copies:
                c.wait()


def merge_thin_kernel(dps, idx, grad, attn, got, *refs):
    z, kind, smalls, sems = idx[0], idx[3], refs[:dps], refs[-1]
    small_w = smalls[0].shape[1] // 2
    wide = got.shape[1] - grad.shape[1]

    def fill(_):
        for d in range(dps):
            at = pl.multiple_of(wide + (z ^ d) * small_w, small_w)
            smalls[d][:, small_w:] = got[:BLK, pl.ds(at, small_w)]

    def keep(ref):
        return [
            (window(ref, small_w, z ^ d), smalls[d].at[:, :small_w]) for d in range(dps)
        ]

    merge_kernel(dps, kind, fill, (keep(grad), keep(attn)), sems)


def merge_wide_kernel(dps, idx, norm, hand, sk_q, sk_o, got, *refs):
    z, kind, bigs, sk, sems = idx[0], idx[3], refs[:dps], refs[dps], refs[-1]
    big_w, small_w = bigs[0].shape[1] // 2, sk.shape[1] // 2
    rows = RANK // dps

    def fill(which):
        for d in range(dps):
            at = pl.multiple_of((z ^ d) * big_w, big_w)
            bigs[d][:, big_w:] = got[:BLK, pl.ds(at, big_w)]
        for i in range(dps):
            at = i * (big_w + small_w)
            sk[RANK + i * rows : RANK + (i + 1) * rows, :] = got[BLK:, at : at + big_w]
            below = slice(2 * RANK + i * rows, 2 * RANK + (i + 1) * rows)
            sk[below, small_w:] = got[BLK:, at + big_w : at + big_w + small_w]
        if which == 0:
            sk[:RANK, :] = jnp.zeros((RANK, big_w), bf16)
        else:
            sk[2 * RANK :, :small_w] = jnp.zeros((RANK, small_w), bf16)

    def keep(ref, sketch):
        return [sketch] + [
            (window(ref, big_w, z ^ d), bigs[d].at[:, :big_w]) for d in range(dps)
        ]

    pairs = (
        keep(norm, (window(sk_q, small_w, z), sk.at[2 * RANK :, :small_w])),
        keep(hand, (window(sk_o, big_w, z), sk.at[:RANK, :])),
    )
    merge_kernel(dps, kind, fill, pairs, sems)


def nt(a, b, precision=None):
    return lax.dot_general(
        a, b, (((1,), (1,)), ((), ())), precision=precision, preferred_element_type=f32
    )


def packed_rows(dps):
    per_gram = (dps * (dps - 1) // 2 + dps // 2) * BLK
    thin = pl.cdiv(per_gram + 16, 32) * 32
    rest = per_gram + dps * RANK + 16
    wide = pl.cdiv(thin + rest, 64) * 64 - thin
    return per_gram, thin, wide


def pack_gram(m, flat, dps):
    r = lax.broadcasted_iota(jnp.int32, (BLK, BLK), 0)
    c = lax.broadcasted_iota(jnp.int32, (BLK, BLK), 1)
    at, on = 0, []
    for i in range(dps):
        row = nt(m[i * BLK : (i + 1) * BLK, :], m[: (i + 1) * BLK, :])
        for j in range(i):
            flat[at : at + BLK, :] = row[:, j * BLK : (j + 1) * BLK].astype(bf16)
            at += BLK
        on.append(row[:, i * BLK :])
    for i in range(0, dps, 2):
        flat[at : at + BLK, :] = jnp.where(r > c, on[i], on[i + 1]).astype(bf16)
        at += BLK
    diagonals = [jnp.sum(jnp.where(r == c, v, 0.0), axis=0, keepdims=True) for v in on]
    diagonals.append(jnp.zeros((16 - dps, BLK), f32))
    return at, jnp.concatenate(diagonals, axis=0).astype(bf16)


def hand_out(core, flat, keep, send):
    half = flat.shape[0] // 2
    keep[...] = flat[pl.ds(pl.multiple_of(core * half, 16), half), :]
    send[...] = flat[pl.ds(pl.multiple_of((1 - core) * half, 16), half), :]


def thin_gram_kernel(dps, idx, *refs):
    z, core = idx[0], idx[2]
    smalls, small, keep, send, flat = refs[:dps], *refs[dps:]
    for d, ref in zip(FAR_FIRST, smalls):
        small[pl.ds(pl.multiple_of((z ^ d) * BLK, BLK), BLK), :] = ref[...]
    at, diagonals = pack_gram(small, flat, dps)
    flat[at:, :] = jnp.zeros((flat.shape[0] - at, BLK), bf16)
    flat[at : at + 16, :] = diagonals
    hand_out(core, flat, keep, send)


def wide_gram_kernel(dps, idx, *refs):
    z, core = idx[0], idx[2]
    bigs, small, sk, big, keep, send, flat = refs[:dps], *refs[dps:]
    half_w = big.shape[1] // 2
    for d, ref in zip(FAR_FIRST, bigs):
        big[pl.ds(pl.multiple_of((z ^ d) * BLK, BLK), BLK), :] = ref[...]
    at, diagonals = pack_gram(big, flat, dps)
    first = (
        nt(sk[:RANK, :], big[:, :half_w])
        + nt(sk[RANK : 2 * RANK, :], big[:, half_w:])
        + nt(sk[2 * RANK :, :], small[...])
    ).astype(bf16)
    for i in range(dps):
        flat[at : at + RANK, :] = first[:, i * BLK : (i + 1) * BLK]
        at += RANK
    flat[at:, :] = jnp.zeros((flat.shape[0] - at, BLK), bf16)
    flat[at : at + 16, :] = diagonals
    hand_out(core, flat, keep, send)


def add_halves_kernel(idx, thin_mine, thin_got, wide_mine, wide_got, keep, send, both):
    size, bit, split_at = keep.shape[0], idx[0] % 2, thin_mine.shape[0]
    both[:split_at, :] = (thin_mine[...].astype(f32) + thin_got[...].astype(f32)).astype(bf16)
    both[split_at:, :] = (wide_mine[...].astype(f32) + wide_got[...].astype(f32)).astype(bf16)
    for out, which in ((keep, bit), (send, 1 - bit)):
        out[...] = both[pl.ds(pl.multiple_of(which * size, 16), size), :]


def add_kernel(mine, got, out):
    out[...] = (mine[...].astype(f32) + got[...].astype(f32)).astype(bf16)


def inverse_factor(gram, spread):
    n, nb = gram.shape[0], 8
    rows = lax.broadcasted_iota(jnp.int32, (n, n), 0)
    cols = lax.broadcasted_iota(jnp.int32, (n, n), 1)
    work = jnp.concatenate([(rows == cols).astype(f32), gram], axis=1)
    count = n // nb
    slabs = [work[nb * s : nb * s + nb, :] for s in range(count)]
    sub = lax.broadcasted_iota(jnp.int32, (nb, 2 * n), 0)

    def lane(x, k):
        return jnp.broadcast_to(x[:, n + k : n + k + 1], (nb, 2 * n))

    def row(at):
        return jnp.broadcast_to(spread[at : at + 1, :], (nb, 2 * n))

    done = []
    for b in range(count):
        base = b * nb * (nb + 1)
        spread[base : base + nb, :] = slabs[b]
        for j in range(nb):
            at = base + nb * (j + 1)
            spread[at : at + nb, :] = lane(slabs[b], nb * b + j)
        pivot_rows = [row(base + i) for i in range(nb)]
        splat = [[row(base + nb * (j + 1) + i) for j in range(i + 1)] for i in range(nb)]
        below = {s: [lane(slabs[s], nb * b + j) for j in range(nb)] for s in range(b + 1, count)}
        out = None
        for k in range(nb):
            inv = 1.0 / splat[k][k]
            at = pivot_rows[k]
            final = at * lax.rsqrt(splat[k][k])
            out = final if out is None else jnp.where(sub == k, final, out)
            for i in range(k + 1, nb):
                mult = splat[i][k] * inv
                for j in range(k + 1, i + 1):
                    splat[i][j] = splat[i][j] - mult * splat[j][k]
                pivot_rows[i] = pivot_rows[i] - mult * at
            for s in range(b + 1, count):
                mult = below[s][k] * inv
                for j in range(k + 1, nb):
                    below[s][j] = below[s][j] - mult * splat[j][k]
                slabs[s] = slabs[s] - mult * at
        done.append(out)
    return jnp.concatenate(done, axis=0)[:, :n]


def split(x):
    high = x.astype(bf16)
    return high, (x - high.astype(f32)).astype(bf16)


def times(rows, gram):
    n = rows.shape[0]
    both = jnp.dot(jnp.concatenate(split(rows), axis=0), gram, preferred_element_type=f32)
    return both[:n] + both[n:]


def product(a, b):
    (ah, al), (bh, bl) = split(a), split(b)
    return jnp.dot(
        jnp.concatenate([ah, ah, al], axis=1),
        jnp.concatenate([bh, bl, bh], axis=0),
        preferred_element_type=f32,
    )


def product_nt(a, b):
    (ah, al), (bh, bl) = split(a), split(b)
    return nt(jnp.concatenate([ah, ah, al], axis=1), jnp.concatenate([bh, bl, bh], axis=1))


def chain_kernel(dps, counts, idx, *refs):
    z, out_half, core = idx[0], idx[1], idx[2]
    quarters, big, small, out, stays, leaves, flat, thin, wide, left, right, spread = (
        refs[:4],
        *refs[4:],
    )
    size, bit = quarters[0].shape[0], z % 2
    for n, ref in enumerate(quarters):
        which = 2 * (core ^ (n // 2)) + (bit ^ (n % 2))
        flat[pl.ds(pl.multiple_of(which * size, 16), size), :] = ref[...]
    per_gram, thin_rows, wide_rows = packed_rows(dps)
    for n in range(2):
        at, split_at = n * 2 * size, n * 2 * size + thin_rows // 2
        thin[n * (thin_rows // 2) : (n + 1) * (thin_rows // 2), :] = flat[at:split_at, :]
        wide[n * (wide_rows // 2) : (n + 1) * (wide_rows // 2), :] = flat[split_at : at + 2 * size, :]
    r = lax.broadcasted_iota(jnp.int32, (BLK, BLK), 0)
    c = lax.broadcasted_iota(jnp.int32, (BLK, BLK), 1)
    rows = jnp.concatenate(
        [wide[per_gram + i * RANK : per_gram + (i + 1) * RANK, :] for i in range(dps)], axis=1
    ).astype(f32)
    wide_diag = wide[per_gram + dps * RANK : per_gram + dps * RANK + 16, :].astype(f32)
    thin_diag = thin[per_gram : per_gram + 16, :].astype(f32)
    is_out = out_half == 1
    for gram, is_wide in ((left, out_half == 0), (right, is_out)):

        def block(n):
            part = slice(n * BLK, (n + 1) * BLK)
            return jnp.where(is_wide, wide[part, :].astype(f32), thin[part, :].astype(f32))

        def put(i, j, value):
            gram[i * BLK : (i + 1) * BLK, j * BLK : (j + 1) * BLK] = value.astype(bf16)

        n = 0
        for i in range(dps):
            for j in range(i):
                value = block(n)
                put(i, j, value)
                put(j, i, value.T)
                n += 1
        diag = jnp.where(is_wide, wide_diag, thin_diag)
        for i in range(0, dps, 2):
            value = block(n)
            turned = value.T
            put(i, i, jnp.where(r > c, value, jnp.where(r == c, diag[i : i + 1, :], turned)))
            put(
                i + 1,
                i + 1,
                jnp.where(r < c, value, jnp.where(r == c, diag[i + 1 : i + 2, :], turned)),
            )
            n += 1
    ahead = times(rows, left[...])
    gram = product_nt(ahead, rows)
    for step in range(2 * POWER):
        following = (right if step % 2 == 0 else left)[...]
        beyond = times(ahead, following)
        inner = product_nt(beyond, ahead)
        low_inv = inverse_factor(gram, spread)
        rows = product(low_inv, ahead)
        if step < 2 * POWER - 1:
            gram = product_nt(product(low_inv, inner), low_inv)
            ahead = product(low_inv, beyond)
        else:
            ahead = times(rows, following)
            gram = product_nt(ahead, rows)
    low_inv = inverse_factor(gram, spread)
    basis = product(low_inv, rows)
    rows = product(low_inv, ahead)
    energy = jnp.sum(times(rows, right[...]) * rows)
    count = jnp.where(out_half == 1, counts[0], counts[1]).astype(f32)
    scale = lax.rsqrt(jnp.full((1, 1), energy, f32) / count + 1e-06)
    coef_b, coef_a = basis.astype(bf16), rows.astype(bf16)
    for_big = jnp.where(is_out, coef_a, coef_b)
    for_small = jnp.where(is_out, coef_b, coef_a)
    scale_big = jnp.where(is_out, scale, 16.0)
    scale_small = jnp.where(is_out, 16.0, scale)
    big_w, small_w = big.shape[1] // 2, small.shape[1] // 2
    made_big = (jnp.dot(for_big, big[...], preferred_element_type=f32) * scale_big).astype(bf16)
    made_small = (jnp.dot(for_small, small[...], preferred_element_type=f32) * scale_small).astype(
        bf16
    )
    for n, half in enumerate((stays, leaves)):
        half[:, :big_w] = made_big[:, n * big_w : (n + 1) * big_w]
        half[:, big_w:] = made_small[:, n * small_w : (n + 1) * small_w]
        out[n * RANK : (n + 1) * RANK, :] = half[...]


def place_kernel(dps, idx, *refs):
    z, kind = idx[0], idx[3]
    mine, theirs = refs[:dps], refs[dps : 2 * dps]
    b_q, a_q, b_o, a_o = refs[2 * dps :]
    big_w, small_w = b_q.shape[1] // dps, a_q.shape[1] // dps
    for d in range(dps):
        bigs = pl.ds(pl.multiple_of((z ^ d) * big_w, big_w), big_w)
        smalls = pl.ds(pl.multiple_of((z ^ d) * small_w, small_w), small_w)
        here, there = mine[d].at[:RANK], theirs[d].at[theirs[d].shape[0] - RANK :]
        for which, query, output in ((0, here, there), (1, there, here)):

            @pl.when(kind == which)
            def _():
                b_q[:, bigs] = query[:, :big_w]
                a_q[:, smalls] = query[:, big_w:].astype(f32)
                a_o[:, bigs] = output[:, :big_w].astype(f32)
                b_o[:, smalls] = output[:, big_w:]


def call(kernel, out_shapes, args, scratch=(), spaces=()):
    spaces = [SMEM] + [VMEM] * (len(args) - 1) if not spaces else spaces
    return pl.pallas_call(
        kernel,
        out_shape=out_shapes,
        in_specs=spaces,
        out_specs=jax.tree.map(lambda _: VMEM, out_shapes),
        scratch_shapes=list(scratch),
        compiler_params=pltpu.CompilerParams(vmem_limit_bytes=48 * 2**20),
    )(*args)


def token_space(sizes, norm_in, query_grad, attn_out, handed, sketch_q, sketch_o):
    _, dps, tensors = sizes
    side = tensors // 2

    def shape(*dims, dtype=bf16):
        return jax.ShapeDtypeStruct(dims, dtype)

    z, t = lax.axis_index("dp"), lax.axis_index("tensor")
    half, core = t // side, t % side
    idx = jnp.stack([z, half, core, half ^ core]).astype(jnp.int32)
    wide, narrow = norm_in.shape[2], query_grad.shape[2]
    big_w, small_w = wide // dps, narrow // dps
    tokens = dps * BLK
    hbm = pl.BlockSpec(memory_space=pltpu.HBM)
    norm, grad, attn, hand, sk_q, sk_o = (
        pltpu.with_memory_space_constraint(v[0], pltpu.HBM)
        for v in (norm_in, query_grad, attn_out, handed, sketch_q, sketch_o)
    )

    give = call(
        functools.partial(give_kernel, dps),
        shape(BLK + RANK // dps, wide + narrow),
        (idx, norm, grad, attn, hand, sk_q, sk_o),
        [pltpu.SemaphoreType.DMA((2 + dps,))],
        [SMEM] + [hbm] * 6,
    )
    got = swap(give, "tensor", 1)
    smalls = call(
        functools.partial(merge_thin_kernel, dps),
        [shape(BLK, 2 * small_w)] * dps,
        (idx, grad, attn, got),
        [pltpu.SemaphoreType.DMA((dps,))],
        [SMEM, hbm, hbm, VMEM],
    )
    packed = call(
        functools.partial(merge_wide_kernel, dps),
        [shape(BLK, 2 * big_w)] * dps + [shape(3 * RANK, 2 * small_w)],
        (idx, norm, hand, sk_q, sk_o, got),
        [pltpu.SemaphoreType.DMA((dps + 1,))],
        [SMEM, hbm, hbm, hbm, hbm, VMEM],
    )
    smalls = [routed(smalls[d], sizes, d, False) for d in FAR_FIRST]
    bigs = [routed(packed[d], sizes, d, True) for d in FAR_FIRST[:-1]]
    sketch = routed(packed[dps], sizes, 0, False)

    _, thin_rows, wide_rows = packed_rows(dps)

    def gram(kernel, m, rows, operands):
        m, keep, send = call(
            functools.partial(kernel, dps),
            [m, shape(rows // 2, BLK), shape(rows // 2, BLK)],
            (idx, *operands),
            [pltpu.VMEM((rows, BLK), bf16)],
        )
        return m, keep, swap(send, "tensor", 1)

    small, *thin = gram(thin_gram_kernel, shape(tokens, 2 * small_w), thin_rows, smalls)
    last, thin[0] = lax.optimization_barrier((packed[0], thin[0]))
    bigs.append(routed(last, sizes, 0, True))
    bigs[0], thin[1] = lax.optimization_barrier((bigs[0], thin[1]))
    big, *rest = gram(
        wide_gram_kernel, shape(tokens, 2 * big_w), wide_rows, (*bigs, small, sketch)
    )
    total = thin_rows + wide_rows
    quarter = shape(total // 4, BLK)
    keep, send = call(
        add_halves_kernel,
        [quarter] * 2,
        (idx, *thin, *rest),
        [pltpu.VMEM((total // 2, BLK), bf16)],
    )
    for bit, value in ((1, send), (2, None)):
        value = swap(keep if value is None else value, "dp", bit)
        keep = call(add_kernel, quarter, (keep, value), (), [VMEM] * 2)
    beside = swap(keep, "dp", 1)
    quarters = (keep, beside, swap(keep, "tensor", 1), swap(beside, "tensor", 1))

    counts = (RANK * wide * tensors, RANK * narrow * tensors)
    whole, stays, leaves = call(
        functools.partial(chain_kernel, dps, counts),
        [shape(2 * RANK, big_w + small_w)] + [shape(RANK, big_w + small_w)] * 2,
        (idx, *quarters, big, small),
        [
            pltpu.VMEM((total, BLK), bf16),
            pltpu.VMEM((thin_rows, BLK), bf16),
            pltpu.VMEM((wide_rows, BLK), bf16),
            pltpu.VMEM((tokens, tokens), bf16),
            pltpu.VMEM((tokens, tokens), bf16),
            pltpu.VMEM((9 * RANK, 2 * RANK), f32),
        ],
    )
    leaves, stays = routed(leaves, sizes, 2, False), routed(stays, sizes, 2, False)
    near, here = routed(whole, sizes, 1, False), routed(whole, sizes, 0, False)
    leaves_on, stays_on = swap(leaves, "dp", 1), swap(stays, "dp", 1)
    mine = (here, near, stays, stays_on)
    theirs = [swap(v, "tensor", 1) for v in (here, near, leaves, leaves_on)]
    outs = call(
        functools.partial(place_kernel, dps),
        [
            shape(RANK, wide),
            shape(RANK, narrow, dtype=f32),
            shape(RANK, narrow),
            shape(RANK, wide, dtype=f32),
        ],
        (idx, *mine, *theirs),
    )
    return tuple(o[None] for o in outs)


def solution(mesh):
    sizes = tuple(mesh.shape[axis] for axis in ("section", "dp", "tensor"))
    _, dps, tensors = sizes

    def body(norm_in, query_grad, attn_out, handed, sketch_q, sketch_o):
        args = (norm_in, query_grad, attn_out, handed, sketch_q, sketch_o)
        fits = (
            dps == 4
            and tensors == 4
            and norm_in.shape[1] == BLK
            and sketch_q.shape[1] == RANK
            and norm_in.shape[2] == handed.shape[2]
            and query_grad.shape[2] == attn_out.shape[2]
            and norm_in.shape[2] == 2 * query_grad.shape[2]
            and query_grad.shape[2] % (dps * 128) == 0
        )
        return token_space(sizes, *args) if fits else feature_space(*args)

    return jax.shard_map(
        body,
        mesh=mesh,
        in_specs=(P("section", "dp", "tensor"),) * 4 + (P("section", None, "tensor"),) * 2,
        out_specs=(P("section", None, "tensor"),) * 4,
        check_vma=False,
    )
```

```python
import functools

import jax
import jax.numpy as jnp
from jax import lax
from jax.experimental import pallas as pl
from jax.experimental.pallas import tpu as pltpu
from jax.sharding import PartitionSpec as P

RANK = 64
POWER = 2
BLK = 128
THIN_ORDER = (2, 3, 1, 0)
WIDE_ORDER = (2, 1, 0, 3)

precise = lax.Precision.HIGHEST
f32 = jnp.float32
bf16 = jnp.bfloat16
VMEM = pl.BlockSpec(memory_space=pltpu.VMEM)
SMEM = pl.BlockSpec(memory_space=pltpu.SMEM)


def from_behind(value, axis, steps):
    count = lax.axis_size(axis)
    pairs = [(source, (source + steps) % count) for source in range(count)]
    return lax.ppermute(value, axis, pairs)


def gram_of(row_block):
    return jnp.dot(row_block, row_block.T, precision=precise, preferred_element_type=f32)


def solve_rows(gram_rows, row_block):
    low_factor = jnp.linalg.cholesky(gram_rows)
    solved = lax.linalg.triangular_solve(low_factor, row_block, left_side=True, lower=True)
    return solved.astype(bf16)


def tokens_of(sketches, matrices):
    parts = [
        jnp.einsum("km,tm->kt", s, m, preferred_element_type=f32)
        for s, m in zip(sketches, matrices)
    ]
    return tuple(lax.psum(p.astype(bf16), "tensor").astype(bf16) for p in parts)


def partials(token_rows, matrices):
    return tuple(
        jnp.dot(r, m, preferred_element_type=f32) for r, m in zip(token_rows, matrices)
    )


def orthonormal(parts):
    rows = [lax.psum(p.astype(bf16), "dp").astype(f32) for p in parts]
    grams = [lax.psum(gram_of(r).astype(bf16), "tensor").astype(f32) for r in rows]
    return tuple(solve_rows(g, r) for g, r in zip(grams, rows))


def feature_space(norm_in, query_grad, attn_out, handed, sketch_q, sketch_o):
    upstream = from_behind(handed, "section", -1)
    lefts = (norm_in[0], attn_out[0])
    rights = (query_grad[0], upstream[0])
    basis = orthonormal(partials(tokens_of((sketch_q[0], sketch_o[0]), rights), lefts))
    for _ in range(POWER):
        other = orthonormal(partials(tokens_of(basis, lefts), rights))
        basis = orthonormal(partials(tokens_of(other, rights), lefts))
    final = partials(tokens_of(basis, lefts), rights)
    raws = [lax.psum(p.astype(bf16), "dp").astype(f32) for p in final]
    energies = lax.psum(tuple(jnp.sum(r * r) for r in raws), "tensor")
    count = lax.axis_size("tensor")
    adapters = [
        r / jnp.sqrt(e / (r.size * count) + 1e-06) for r, e in zip(raws, energies)
    ]
    return (
        (basis[0] * 16.0)[None],
        adapters[0][None],
        (basis[1] * 16.0)[None],
        adapters[1][None],
    )


def swap(value, axis, bit):
    count = lax.axis_size(axis)
    return lax.ppermute(value, axis, [(i, i ^ bit) for i in range(count)])


def routed(value, sizes, token_bit, shifted):
    sections, dps, tensors = sizes
    side = tensors // 2
    pairs = []
    for s in range(sections):
        for z in range(dps):
            for t in range(tensors):
                to_t = t ^ side if t % side else t
                to_s = (s - 1) % sections if shifted and to_t >= side else s
                to = (to_s * dps + (z ^ token_bit)) * tensors + to_t
                pairs.append(((s * dps + z) * tensors + t, to))
    return lax.ppermute(value, ("section", "dp", "tensor"), pairs)


def window(ref, width, at):
    return ref.at[:, pl.ds(pl.multiple_of(at * width, width), width)]


def move(pairs, sems):
    copies = [pltpu.make_async_copy(src, dst, sems.at[n]) for n, (src, dst) in enumerate(pairs)]
    for c in copies:
        c.start()
    for c in copies:
        c.wait()


def give_kernel(dps, idx, norm, grad, attn, hand, sk_q, sk_o, give, sems):
    z, kind = idx[0], idx[3]
    wide, narrow = norm.shape[1], grad.shape[1]
    big_w, small_w = wide // dps, narrow // dps
    rows = RANK // dps

    def sketch(ref, width, start):
        part = ref.at[:, pl.ds(pl.multiple_of(z * width, width), width)]
        return [
            (
                part.at[i * rows : (i + 1) * rows],
                give.at[BLK:, i * (big_w + small_w) + start : i * (big_w + small_w) + start + width],
            )
            for i in range(dps)
        ]

    give[BLK:, :] = jnp.zeros((rows, wide + narrow), bf16)

    @pl.when(kind == 0)
    def _():
        pairs = [(hand, give.at[:BLK, :wide]), (attn, give.at[:BLK, wide:])]
        move(pairs + sketch(sk_o, big_w, 0), sems)

    @pl.when(kind == 1)
    def _():
        pairs = [(norm, give.at[:BLK, :wide]), (grad, give.at[:BLK, wide:])]
        move(pairs + sketch(sk_q, small_w, big_w), sems)


def merge_kernel(dps, kind, fill, pairs, sems):
    for which in (0, 1):

        @pl.when(kind == which)
        def _():
            copies = [
                pltpu.make_async_copy(src, dst, sems.at[n])
                for n, (src, dst) in enumerate(pairs[which])
            ]
            for c in copies:
                c.start()
            fill(which)
            for c in copies:
                c.wait()


def merge_thin_kernel(dps, idx, grad, attn, got, *refs):
    z, kind, smalls, sems = idx[0], idx[3], refs[:dps], refs[-1]
    small_w = smalls[0].shape[1] // 2
    wide = got.shape[1] - grad.shape[1]

    def fill(_):
        for d in range(dps):
            at = pl.multiple_of(wide + (z ^ d) * small_w, small_w)
            smalls[d][:, small_w:] = got[:BLK, pl.ds(at, small_w)]

    def keep(ref):
        return [
            (window(ref, small_w, z ^ d), smalls[d].at[:, :small_w]) for d in range(dps)
        ]

    merge_kernel(dps, kind, fill, (keep(grad), keep(attn)), sems)


def merge_wide_kernel(dps, idx, norm, hand, sk_q, sk_o, got, *refs):
    z, kind, bigs, sk, sems = idx[0], idx[3], refs[:dps], refs[dps], refs[-1]
    big_w, small_w = bigs[0].shape[1] // 2, sk.shape[1] // 2
    rows = RANK // dps

    def fill(which):
        for d in range(dps):
            at = pl.multiple_of((z ^ d) * big_w, big_w)
            bigs[d][:, big_w:] = got[:BLK, pl.ds(at, big_w)]
        for i in range(dps):
            at = i * (big_w + small_w)
            sk[RANK + i * rows : RANK + (i + 1) * rows, :] = got[BLK:, at : at + big_w]
            below = slice(2 * RANK + i * rows, 2 * RANK + (i + 1) * rows)
            sk[below, small_w:] = got[BLK:, at + big_w : at + big_w + small_w]
        if which == 0:
            sk[:RANK, :] = jnp.zeros((RANK, big_w), bf16)
        else:
            sk[2 * RANK :, :small_w] = jnp.zeros((RANK, small_w), bf16)

    def keep(ref, sketch):
        return [sketch] + [
            (window(ref, big_w, z ^ d), bigs[d].at[:, :big_w]) for d in range(dps)
        ]

    pairs = (
        keep(norm, (window(sk_q, small_w, z), sk.at[2 * RANK :, :small_w])),
        keep(hand, (window(sk_o, big_w, z), sk.at[:RANK, :])),
    )
    merge_kernel(dps, kind, fill, pairs, sems)


def nt(a, b, precision=None):
    return lax.dot_general(
        a, b, (((1,), (1,)), ((), ())), precision=precision, preferred_element_type=f32
    )


def packed_rows(dps):
    per_gram = (dps * (dps - 1) // 2 + dps // 2) * BLK
    thin = pl.cdiv(per_gram + 16, 32) * 32
    rest = per_gram + dps * RANK + 16
    wide = pl.cdiv(thin + rest, 64) * 64 - thin
    return per_gram, thin, wide


def pack_gram(m, flat, dps):
    r = lax.broadcasted_iota(jnp.int32, (BLK, BLK), 0)
    c = lax.broadcasted_iota(jnp.int32, (BLK, BLK), 1)
    at, on = 0, []
    for i in range(dps):
        row = nt(m[i * BLK : (i + 1) * BLK, :], m[: (i + 1) * BLK, :])
        for j in range(i):
            flat[at : at + BLK, :] = row[:, j * BLK : (j + 1) * BLK].astype(bf16)
            at += BLK
        on.append(row[:, i * BLK :])
    for i in range(0, dps, 2):
        flat[at : at + BLK, :] = jnp.where(r > c, on[i], on[i + 1]).astype(bf16)
        at += BLK
    diagonals = [jnp.sum(jnp.where(r == c, v, 0.0), axis=0, keepdims=True) for v in on]
    diagonals.append(jnp.zeros((16 - dps, BLK), f32))
    return at, jnp.concatenate(diagonals, axis=0).astype(bf16)


def hand_out(core, flat, keep, send):
    half = flat.shape[0] // 2
    keep[...] = flat[pl.ds(pl.multiple_of(core * half, 16), half), :]
    send[...] = flat[pl.ds(pl.multiple_of((1 - core) * half, 16), half), :]


def thin_gram_kernel(dps, idx, *refs):
    z, core = idx[0], idx[2]
    smalls, small, keep, send, flat = refs[:dps], *refs[dps:]
    for d, ref in zip(THIN_ORDER, smalls):
        small[pl.ds(pl.multiple_of((z ^ d) * BLK, BLK), BLK), :] = ref[...]
    at, diagonals = pack_gram(small, flat, dps)
    flat[at:, :] = jnp.zeros((flat.shape[0] - at, BLK), bf16)
    flat[at : at + 16, :] = diagonals
    hand_out(core, flat, keep, send)


def wide_gram_kernel(dps, idx, *refs):
    z, core = idx[0], idx[2]
    sk, bigs, small, big, keep, send, flat = refs[0], refs[1 : dps + 1], *refs[dps + 1 :]
    half_w = big.shape[1] // 2
    for d, ref in zip(WIDE_ORDER, bigs):
        big[pl.ds(pl.multiple_of((z ^ d) * BLK, BLK), BLK), :] = ref[...]
    at, diagonals = pack_gram(big, flat, dps)
    first = (
        nt(sk[:RANK, :], big[:, :half_w])
        + nt(sk[RANK : 2 * RANK, :], big[:, half_w:])
        + nt(sk[2 * RANK :, :], small[...])
    ).astype(bf16)
    for i in range(dps):
        flat[at : at + RANK, :] = first[:, i * BLK : (i + 1) * BLK]
        at += RANK
    flat[at:, :] = jnp.zeros((flat.shape[0] - at, BLK), bf16)
    flat[at : at + 16, :] = diagonals
    hand_out(core, flat, keep, send)


def add_halves_kernel(idx, thin_mine, thin_got, wide_mine, wide_got, keep, send, both):
    size, bit, split_at = keep.shape[0], idx[0] % 2, thin_mine.shape[0]
    both[:split_at, :] = (thin_mine[...].astype(f32) + thin_got[...].astype(f32)).astype(bf16)
    both[split_at:, :] = (wide_mine[...].astype(f32) + wide_got[...].astype(f32)).astype(bf16)
    for out, which in ((keep, bit), (send, 1 - bit)):
        out[...] = both[pl.ds(pl.multiple_of(which * size, 16), size), :]


def add_kernel(mine, got, out):
    out[...] = (mine[...].astype(f32) + got[...].astype(f32)).astype(bf16)


def inverse_factor(gram, spread):
    n, nb = gram.shape[0], 8
    rows = lax.broadcasted_iota(jnp.int32, (n, n), 0)
    cols = lax.broadcasted_iota(jnp.int32, (n, n), 1)
    work = jnp.concatenate([(rows == cols).astype(f32), gram], axis=1)
    count = n // nb
    slabs = [work[nb * s : nb * s + nb, :] for s in range(count)]
    sub = lax.broadcasted_iota(jnp.int32, (nb, 2 * n), 0)

    def lane(x, k):
        return jnp.broadcast_to(x[:, n + k : n + k + 1], (nb, 2 * n))

    def row(at):
        return jnp.broadcast_to(spread[at : at + 1, :], (nb, 2 * n))

    done = []
    for b in range(count):
        base = b * nb * (nb + 1)
        spread[base : base + nb, :] = slabs[b]
        for j in range(nb):
            at = base + nb * (j + 1)
            spread[at : at + nb, :] = lane(slabs[b], nb * b + j)
        pivot_rows = [row(base + i) for i in range(nb)]
        splat = [[row(base + nb * (j + 1) + i) for j in range(i + 1)] for i in range(nb)]
        below = {s: [lane(slabs[s], nb * b + j) for j in range(nb)] for s in range(b + 1, count)}
        out = None
        for k in range(nb):
            inv = 1.0 / splat[k][k]
            at = pivot_rows[k]
            final = at * lax.rsqrt(splat[k][k])
            out = final if out is None else jnp.where(sub == k, final, out)
            for i in range(k + 1, nb):
                mult = splat[i][k] * inv
                for j in range(k + 1, i + 1):
                    splat[i][j] = splat[i][j] - mult * splat[j][k]
                pivot_rows[i] = pivot_rows[i] - mult * at
            for s in range(b + 1, count):
                mult = below[s][k] * inv
                for j in range(k + 1, nb):
                    below[s][j] = below[s][j] - mult * splat[j][k]
                slabs[s] = slabs[s] - mult * at
        done.append(out)
    return jnp.concatenate(done, axis=0)[:, :n]


def split(x):
    high = x.astype(bf16)
    return high, (x - high.astype(f32)).astype(bf16)


def times(rows, gram):
    n = rows.shape[0]
    both = jnp.dot(jnp.concatenate(split(rows), axis=0), gram, preferred_element_type=f32)
    return both[:n] + both[n:]


def product(a, b):
    (ah, al), (bh, bl) = split(a), split(b)
    return jnp.dot(
        jnp.concatenate([ah, ah, al], axis=1),
        jnp.concatenate([bh, bl, bh], axis=0),
        preferred_element_type=f32,
    )


def product_nt(a, b):
    (ah, al), (bh, bl) = split(a), split(b)
    return nt(jnp.concatenate([ah, ah, al], axis=1), jnp.concatenate([bh, bl, bh], axis=1))


def chain_kernel(dps, counts, idx, *refs):
    z, out_half, core = idx[0], idx[1], idx[2]
    quarters, big, small, out, stays, leaves, flat, thin, wide, left, right, spread = (
        refs[:4],
        *refs[4:],
    )
    size, bit = quarters[0].shape[0], z % 2
    for n, ref in enumerate(quarters):
        which = 2 * (core ^ (n // 2)) + (bit ^ (n % 2))
        flat[pl.ds(pl.multiple_of(which * size, 16), size), :] = ref[...]
    per_gram, thin_rows, wide_rows = packed_rows(dps)
    for n in range(2):
        at, split_at = n * 2 * size, n * 2 * size + thin_rows // 2
        thin[n * (thin_rows // 2) : (n + 1) * (thin_rows // 2), :] = flat[at:split_at, :]
        wide[n * (wide_rows // 2) : (n + 1) * (wide_rows // 2), :] = flat[split_at : at + 2 * size, :]
    r = lax.broadcasted_iota(jnp.int32, (BLK, BLK), 0)
    c = lax.broadcasted_iota(jnp.int32, (BLK, BLK), 1)
    rows = jnp.concatenate(
        [wide[per_gram + i * RANK : per_gram + (i + 1) * RANK, :] for i in range(dps)], axis=1
    ).astype(f32)
    wide_diag = wide[per_gram + dps * RANK : per_gram + dps * RANK + 16, :].astype(f32)
    thin_diag = thin[per_gram : per_gram + 16, :].astype(f32)
    is_out = out_half == 1
    for gram, is_wide in ((left, out_half == 0), (right, is_out)):

        def block(n):
            part = slice(n * BLK, (n + 1) * BLK)
            return jnp.where(is_wide, wide[part, :].astype(f32), thin[part, :].astype(f32))

        def put(i, j, value):
            gram[i * BLK : (i + 1) * BLK, j * BLK : (j + 1) * BLK] = value.astype(bf16)

        n = 0
        for i in range(dps):
            for j in range(i):
                value = block(n)
                put(i, j, value)
                put(j, i, value.T)
                n += 1
        diag = jnp.where(is_wide, wide_diag, thin_diag)
        for i in range(0, dps, 2):
            value = block(n)
            turned = value.T
            put(i, i, jnp.where(r > c, value, jnp.where(r == c, diag[i : i + 1, :], turned)))
            put(
                i + 1,
                i + 1,
                jnp.where(r < c, value, jnp.where(r == c, diag[i + 1 : i + 2, :], turned)),
            )
            n += 1
    ahead = times(rows, left[...])
    gram = product_nt(ahead, rows)
    for step in range(2 * POWER):
        following = (right if step % 2 == 0 else left)[...]
        beyond = times(ahead, following)
        inner = product_nt(beyond, ahead)
        low_inv = inverse_factor(gram, spread)
        rows = product(low_inv, ahead)
        if step < 2 * POWER - 1:
            gram = product_nt(product(low_inv, inner), low_inv)
            ahead = product(low_inv, beyond)
        else:
            ahead = times(rows, following)
            gram = product_nt(ahead, rows)
    low_inv = inverse_factor(gram, spread)
    basis = product(low_inv, rows)
    rows = product(low_inv, ahead)
    energy = jnp.sum(times(rows, right[...]) * rows)
    count = jnp.where(out_half == 1, counts[0], counts[1]).astype(f32)
    scale = lax.rsqrt(jnp.full((1, 1), energy, f32) / count + 1e-06)
    coef_b, coef_a = basis.astype(bf16), rows.astype(bf16)
    for_big = jnp.where(is_out, coef_a, coef_b)
    for_small = jnp.where(is_out, coef_b, coef_a)
    scale_big = jnp.where(is_out, scale, 16.0)
    scale_small = jnp.where(is_out, 16.0, scale)
    big_w, small_w = big.shape[1] // 2, small.shape[1] // 2
    made_big = (jnp.dot(for_big, big[...], preferred_element_type=f32) * scale_big).astype(bf16)
    made_small = (jnp.dot(for_small, small[...], preferred_element_type=f32) * scale_small).astype(
        bf16
    )
    for n, half in enumerate((stays, leaves)):
        half[:, :big_w] = made_big[:, n * big_w : (n + 1) * big_w]
        half[:, big_w:] = made_small[:, n * small_w : (n + 1) * small_w]
        out[n * RANK : (n + 1) * RANK, :] = half[...]


def place_kernel(dps, idx, *refs):
    z, kind = idx[0], idx[3]
    mine, theirs = refs[:dps], refs[dps : 2 * dps]
    b_q, a_q, b_o, a_o = refs[2 * dps :]
    big_w, small_w = b_q.shape[1] // dps, a_q.shape[1] // dps
    for d in range(dps):
        bigs = pl.ds(pl.multiple_of((z ^ d) * big_w, big_w), big_w)
        smalls = pl.ds(pl.multiple_of((z ^ d) * small_w, small_w), small_w)
        here, there = mine[d].at[:RANK], theirs[d].at[theirs[d].shape[0] - RANK :]
        for which, query, output in ((0, here, there), (1, there, here)):

            @pl.when(kind == which)
            def _():
                b_q[:, bigs] = query[:, :big_w]
                a_q[:, smalls] = query[:, big_w:].astype(f32)
                a_o[:, bigs] = output[:, :big_w].astype(f32)
                b_o[:, smalls] = output[:, big_w:]


def call(kernel, out_shapes, args, scratch=(), spaces=()):
    spaces = [SMEM] + [VMEM] * (len(args) - 1) if not spaces else spaces
    return pl.pallas_call(
        kernel,
        out_shape=out_shapes,
        in_specs=spaces,
        out_specs=jax.tree.map(lambda _: VMEM, out_shapes),
        scratch_shapes=list(scratch),
        compiler_params=pltpu.CompilerParams(vmem_limit_bytes=48 * 2**20),
    )(*args)


def token_space(sizes, norm_in, query_grad, attn_out, handed, sketch_q, sketch_o):
    _, dps, tensors = sizes
    side = tensors // 2

    def shape(*dims, dtype=bf16):
        return jax.ShapeDtypeStruct(dims, dtype)

    z, t = lax.axis_index("dp"), lax.axis_index("tensor")
    half, core = t // side, t % side
    idx = jnp.stack([z, half, core, half ^ core]).astype(jnp.int32)
    wide, narrow = norm_in.shape[2], query_grad.shape[2]
    big_w, small_w = wide // dps, narrow // dps
    tokens = dps * BLK
    hbm = pl.BlockSpec(memory_space=pltpu.HBM)
    norm, grad, attn, hand, sk_q, sk_o = (
        pltpu.with_memory_space_constraint(v[0], pltpu.HBM)
        for v in (norm_in, query_grad, attn_out, handed, sketch_q, sketch_o)
    )

    give = call(
        functools.partial(give_kernel, dps),
        shape(BLK + RANK // dps, wide + narrow),
        (idx, norm, grad, attn, hand, sk_q, sk_o),
        [pltpu.SemaphoreType.DMA((2 + dps,))],
        [SMEM] + [hbm] * 6,
    )
    got = swap(give, "tensor", 1)
    smalls = call(
        functools.partial(merge_thin_kernel, dps),
        [shape(BLK, 2 * small_w)] * dps,
        (idx, grad, attn, got),
        [pltpu.SemaphoreType.DMA((dps,))],
        [SMEM, hbm, hbm, VMEM],
    )
    packed = call(
        functools.partial(merge_wide_kernel, dps),
        [shape(BLK, 2 * big_w)] * dps + [shape(3 * RANK, 2 * small_w)],
        (idx, norm, hand, sk_q, sk_o, got),
        [pltpu.SemaphoreType.DMA((dps + 1,))],
        [SMEM, hbm, hbm, hbm, hbm, VMEM],
    )
    smalls = [routed(smalls[d], sizes, d, False) for d in THIN_ORDER]
    sketch = routed(packed[dps], sizes, 0, False)
    bigs = [routed(packed[d], sizes, d, True) for d in WIDE_ORDER]

    _, thin_rows, wide_rows = packed_rows(dps)

    def gram(kernel, m, rows, operands):
        m, keep, send = call(
            functools.partial(kernel, dps),
            [m, shape(rows // 2, BLK), shape(rows // 2, BLK)],
            (idx, *operands),
            [pltpu.VMEM((rows, BLK), bf16)],
        )
        return m, keep, swap(send, "tensor", 1)

    small, *thin = gram(thin_gram_kernel, shape(tokens, 2 * small_w), thin_rows, smalls)
    big, *rest = gram(
        wide_gram_kernel, shape(tokens, 2 * big_w), wide_rows, (sketch, *bigs, small)
    )
    total = thin_rows + wide_rows
    quarter = shape(total // 4, BLK)
    keep, send = call(
        add_halves_kernel,
        [quarter] * 2,
        (idx, *thin, *rest),
        [pltpu.VMEM((total // 2, BLK), bf16)],
    )
    for bit, value in ((1, send), (2, None)):
        value = swap(keep if value is None else value, "dp", bit)
        keep = call(add_kernel, quarter, (keep, value), (), [VMEM] * 2)
    beside = swap(keep, "dp", 1)
    quarters = (keep, beside, swap(keep, "tensor", 1), swap(beside, "tensor", 1))

    counts = (RANK * wide * tensors, RANK * narrow * tensors)
    whole, stays, leaves = call(
        functools.partial(chain_kernel, dps, counts),
        [shape(2 * RANK, big_w + small_w)] + [shape(RANK, big_w + small_w)] * 2,
        (idx, *quarters, big, small),
        [
            pltpu.VMEM((total, BLK), bf16),
            pltpu.VMEM((thin_rows, BLK), bf16),
            pltpu.VMEM((wide_rows, BLK), bf16),
            pltpu.VMEM((tokens, tokens), bf16),
            pltpu.VMEM((tokens, tokens), bf16),
            pltpu.VMEM((9 * RANK, 2 * RANK), f32),
        ],
    )
    leaves, stays = routed(leaves, sizes, 2, False), routed(stays, sizes, 2, False)
    near, here = routed(whole, sizes, 1, False), routed(whole, sizes, 0, False)
    leaves_on, stays_on = swap(leaves, "dp", 1), swap(stays, "dp", 1)
    mine = (here, near, stays, stays_on)
    theirs = [swap(v, "tensor", 1) for v in (here, near, leaves, leaves_on)]
    outs = call(
        functools.partial(place_kernel, dps),
        [
            shape(RANK, wide),
            shape(RANK, narrow, dtype=f32),
            shape(RANK, narrow),
            shape(RANK, wide, dtype=f32),
        ],
        (idx, *mine, *theirs),
    )
    return tuple(o[None] for o in outs)


def solution(mesh):
    sizes = tuple(mesh.shape[axis] for axis in ("section", "dp", "tensor"))
    _, dps, tensors = sizes

    def body(norm_in, query_grad, attn_out, handed, sketch_q, sketch_o):
        args = (norm_in, query_grad, attn_out, handed, sketch_q, sketch_o)
        fits = (
            dps == 4
            and tensors == 4
            and norm_in.shape[1] == BLK
            and sketch_q.shape[1] == RANK
            and norm_in.shape[2] == handed.shape[2]
            and query_grad.shape[2] == attn_out.shape[2]
            and norm_in.shape[2] == 2 * query_grad.shape[2]
            and query_grad.shape[2] % (dps * 128) == 0
        )
        return token_space(sizes, *args) if fits else feature_space(*args)

    return jax.shard_map(
        body,
        mesh=mesh,
        in_specs=(P("section", "dp", "tensor"),) * 4 + (P("section", None, "tensor"),) * 2,
        out_specs=(P("section", None, "tensor"),) * 4,
        check_vma=False,
    )
```

```python
import functools

import jax
import jax.numpy as jnp
from jax import lax
from jax.experimental import pallas as pl
from jax.experimental.pallas import tpu as pltpu
from jax.sharding import PartitionSpec as P

RANK = 64
POWER = 2
BLK = 128
THIN_ORDER = (2, 1, 0, 3)
WIDE_ORDER = (2, 3, 1, 0)

precise = lax.Precision.HIGHEST
f32 = jnp.float32
bf16 = jnp.bfloat16
VMEM = pl.BlockSpec(memory_space=pltpu.VMEM)
SMEM = pl.BlockSpec(memory_space=pltpu.SMEM)


def from_behind(value, axis, steps):
    count = lax.axis_size(axis)
    pairs = [(source, (source + steps) % count) for source in range(count)]
    return lax.ppermute(value, axis, pairs)


def gram_of(row_block):
    return jnp.dot(row_block, row_block.T, precision=precise, preferred_element_type=f32)


def solve_rows(gram_rows, row_block):
    low_factor = jnp.linalg.cholesky(gram_rows)
    solved = lax.linalg.triangular_solve(low_factor, row_block, left_side=True, lower=True)
    return solved.astype(bf16)


def tokens_of(sketches, matrices):
    parts = [
        jnp.einsum("km,tm->kt", s, m, preferred_element_type=f32)
        for s, m in zip(sketches, matrices)
    ]
    return tuple(lax.psum(p.astype(bf16), "tensor").astype(bf16) for p in parts)


def partials(token_rows, matrices):
    return tuple(
        jnp.dot(r, m, preferred_element_type=f32) for r, m in zip(token_rows, matrices)
    )


def orthonormal(parts):
    rows = [lax.psum(p.astype(bf16), "dp").astype(f32) for p in parts]
    grams = [lax.psum(gram_of(r).astype(bf16), "tensor").astype(f32) for r in rows]
    return tuple(solve_rows(g, r) for g, r in zip(grams, rows))


def feature_space(norm_in, query_grad, attn_out, handed, sketch_q, sketch_o):
    upstream = from_behind(handed, "section", -1)
    lefts = (norm_in[0], attn_out[0])
    rights = (query_grad[0], upstream[0])
    basis = orthonormal(partials(tokens_of((sketch_q[0], sketch_o[0]), rights), lefts))
    for _ in range(POWER):
        other = orthonormal(partials(tokens_of(basis, lefts), rights))
        basis = orthonormal(partials(tokens_of(other, rights), lefts))
    final = partials(tokens_of(basis, lefts), rights)
    raws = [lax.psum(p.astype(bf16), "dp").astype(f32) for p in final]
    energies = lax.psum(tuple(jnp.sum(r * r) for r in raws), "tensor")
    count = lax.axis_size("tensor")
    adapters = [
        r / jnp.sqrt(e / (r.size * count) + 1e-06) for r, e in zip(raws, energies)
    ]
    return (
        (basis[0] * 16.0)[None],
        adapters[0][None],
        (basis[1] * 16.0)[None],
        adapters[1][None],
    )


def swap(value, axis, bit):
    count = lax.axis_size(axis)
    return lax.ppermute(value, axis, [(i, i ^ bit) for i in range(count)])


def routed(value, sizes, token_bit, shifted):
    sections, dps, tensors = sizes
    side = tensors // 2
    pairs = []
    for s in range(sections):
        for z in range(dps):
            for t in range(tensors):
                to_t = t ^ side if t % side else t
                to_s = (s - 1) % sections if shifted and to_t >= side else s
                to = (to_s * dps + (z ^ token_bit)) * tensors + to_t
                pairs.append(((s * dps + z) * tensors + t, to))
    return lax.ppermute(value, ("section", "dp", "tensor"), pairs)


def window(ref, width, at):
    return ref.at[:, pl.ds(pl.multiple_of(at * width, width), width)]


def move(pairs, sems):
    copies = [pltpu.make_async_copy(src, dst, sems.at[n]) for n, (src, dst) in enumerate(pairs)]
    for c in copies:
        c.start()
    for c in copies:
        c.wait()


def give_kernel(dps, idx, norm, grad, attn, hand, sk_q, sk_o, give, sems):
    z, kind = idx[0], idx[3]
    wide, narrow = norm.shape[1], grad.shape[1]
    big_w, small_w = wide // dps, narrow // dps
    rows = RANK // dps

    def sketch(ref, width, start):
        part = ref.at[:, pl.ds(pl.multiple_of(z * width, width), width)]
        return [
            (
                part.at[i * rows : (i + 1) * rows],
                give.at[BLK:, i * (big_w + small_w) + start : i * (big_w + small_w) + start + width],
            )
            for i in range(dps)
        ]

    give[BLK:, :] = jnp.zeros((rows, wide + narrow), bf16)

    @pl.when(kind == 0)
    def _():
        pairs = [(hand, give.at[:BLK, :wide]), (attn, give.at[:BLK, wide:])]
        move(pairs + sketch(sk_o, big_w, 0), sems)

    @pl.when(kind == 1)
    def _():
        pairs = [(norm, give.at[:BLK, :wide]), (grad, give.at[:BLK, wide:])]
        move(pairs + sketch(sk_q, small_w, big_w), sems)


def merge_kernel(dps, kind, fill, pairs, sems):
    for which in (0, 1):

        @pl.when(kind == which)
        def _():
            copies = [
                pltpu.make_async_copy(src, dst, sems.at[n])
                for n, (src, dst) in enumerate(pairs[which])
            ]
            for c in copies:
                c.start()
            fill(which)
            for c in copies:
                c.wait()


def merge_thin_kernel(dps, idx, grad, attn, got, *refs):
    z, kind, smalls, sems = idx[0], idx[3], refs[:dps], refs[-1]
    small_w = smalls[0].shape[1] // 2
    wide = got.shape[1] - grad.shape[1]

    def fill(_):
        for d in range(dps):
            at = pl.multiple_of(wide + (z ^ d) * small_w, small_w)
            smalls[d][:, small_w:] = got[:BLK, pl.ds(at, small_w)]

    def keep(ref):
        return [
            (window(ref, small_w, z ^ d), smalls[d].at[:, :small_w]) for d in range(dps)
        ]

    merge_kernel(dps, kind, fill, (keep(grad), keep(attn)), sems)


def merge_wide_kernel(dps, idx, norm, hand, sk_q, sk_o, got, *refs):
    z, kind, bigs, sk, sems = idx[0], idx[3], refs[:dps], refs[dps], refs[-1]
    big_w, small_w = bigs[0].shape[1] // 2, sk.shape[1] // 2
    rows = RANK // dps

    def fill(which):
        for d in range(dps):
            at = pl.multiple_of((z ^ d) * big_w, big_w)
            bigs[d][:, big_w:] = got[:BLK, pl.ds(at, big_w)]
        for i in range(dps):
            at = i * (big_w + small_w)
            sk[RANK + i * rows : RANK + (i + 1) * rows, :] = got[BLK:, at : at + big_w]
            below = slice(2 * RANK + i * rows, 2 * RANK + (i + 1) * rows)
            sk[below, small_w:] = got[BLK:, at + big_w : at + big_w + small_w]
        if which == 0:
            sk[:RANK, :] = jnp.zeros((RANK, big_w), bf16)
        else:
            sk[2 * RANK :, :small_w] = jnp.zeros((RANK, small_w), bf16)

    def keep(ref, sketch):
        return [sketch] + [
            (window(ref, big_w, z ^ d), bigs[d].at[:, :big_w]) for d in range(dps)
        ]

    pairs = (
        keep(norm, (window(sk_q, small_w, z), sk.at[2 * RANK :, :small_w])),
        keep(hand, (window(sk_o, big_w, z), sk.at[:RANK, :])),
    )
    merge_kernel(dps, kind, fill, pairs, sems)


def nt(a, b, precision=None):
    return lax.dot_general(
        a, b, (((1,), (1,)), ((), ())), precision=precision, preferred_element_type=f32
    )


def packed_rows(dps):
    per_gram = (dps * (dps - 1) // 2 + dps // 2) * BLK
    thin = pl.cdiv(per_gram + 16, 32) * 32
    rest = per_gram + dps * RANK + 16
    wide = pl.cdiv(thin + rest, 64) * 64 - thin
    return per_gram, thin, wide


def pack_gram(m, flat, dps):
    r = lax.broadcasted_iota(jnp.int32, (BLK, BLK), 0)
    c = lax.broadcasted_iota(jnp.int32, (BLK, BLK), 1)
    at, on = 0, []
    for i in range(dps):
        row = nt(m[i * BLK : (i + 1) * BLK, :], m[: (i + 1) * BLK, :])
        for j in range(i):
            flat[at : at + BLK, :] = row[:, j * BLK : (j + 1) * BLK].astype(bf16)
            at += BLK
        on.append(row[:, i * BLK :])
    for i in range(0, dps, 2):
        flat[at : at + BLK, :] = jnp.where(r > c, on[i], on[i + 1]).astype(bf16)
        at += BLK
    diagonals = [jnp.sum(jnp.where(r == c, v, 0.0), axis=0, keepdims=True) for v in on]
    diagonals.append(jnp.zeros((16 - dps, BLK), f32))
    return at, jnp.concatenate(diagonals, axis=0).astype(bf16)


def hand_out(core, flat, keep, send):
    half = flat.shape[0] // 2
    keep[...] = flat[pl.ds(pl.multiple_of(core * half, 16), half), :]
    send[...] = flat[pl.ds(pl.multiple_of((1 - core) * half, 16), half), :]


def thin_gram_kernel(dps, idx, *refs):
    z, core = idx[0], idx[2]
    smalls, small, keep, send, flat = refs[:dps], *refs[dps:]
    for d, ref in zip(THIN_ORDER, smalls):
        small[pl.ds(pl.multiple_of((z ^ d) * BLK, BLK), BLK), :] = ref[...]
    at, diagonals = pack_gram(small, flat, dps)
    flat[at:, :] = jnp.zeros((flat.shape[0] - at, BLK), bf16)
    flat[at : at + 16, :] = diagonals
    hand_out(core, flat, keep, send)


def wide_gram_kernel(dps, idx, *refs):
    z, core = idx[0], idx[2]
    sk, bigs, small, big, keep, send, flat = refs[0], refs[1 : dps + 1], *refs[dps + 1 :]
    half_w = big.shape[1] // 2
    for d, ref in zip(WIDE_ORDER, bigs):
        big[pl.ds(pl.multiple_of((z ^ d) * BLK, BLK), BLK), :] = ref[...]
    at, diagonals = pack_gram(big, flat, dps)
    first = (
        nt(sk[:RANK, :], big[:, :half_w])
        + nt(sk[RANK : 2 * RANK, :], big[:, half_w:])
        + nt(sk[2 * RANK :, :], small[...])
    ).astype(bf16)
    for i in range(dps):
        flat[at : at + RANK, :] = first[:, i * BLK : (i + 1) * BLK]
        at += RANK
    flat[at:, :] = jnp.zeros((flat.shape[0] - at, BLK), bf16)
    flat[at : at + 16, :] = diagonals
    hand_out(core, flat, keep, send)


def add_halves_kernel(idx, thin_mine, thin_got, wide_mine, wide_got, keep, send, both):
    size, bit, split_at = keep.shape[0], idx[0] % 2, thin_mine.shape[0]
    both[:split_at, :] = (thin_mine[...].astype(f32) + thin_got[...].astype(f32)).astype(bf16)
    both[split_at:, :] = (wide_mine[...].astype(f32) + wide_got[...].astype(f32)).astype(bf16)
    for out, which in ((keep, bit), (send, 1 - bit)):
        out[...] = both[pl.ds(pl.multiple_of(which * size, 16), size), :]


def add_kernel(mine, got, out):
    out[...] = (mine[...].astype(f32) + got[...].astype(f32)).astype(bf16)


def inverse_factor(gram, spread):
    n, nb = gram.shape[0], 8
    rows = lax.broadcasted_iota(jnp.int32, (n, n), 0)
    cols = lax.broadcasted_iota(jnp.int32, (n, n), 1)
    work = jnp.concatenate([(rows == cols).astype(f32), gram], axis=1)
    count = n // nb
    slabs = [work[nb * s : nb * s + nb, :] for s in range(count)]
    sub = lax.broadcasted_iota(jnp.int32, (nb, 2 * n), 0)

    def lane(x, k):
        return jnp.broadcast_to(x[:, n + k : n + k + 1], (nb, 2 * n))

    def row(at):
        return jnp.broadcast_to(spread[at : at + 1, :], (nb, 2 * n))

    done = []
    for b in range(count):
        base = b * nb * (nb + 1)
        spread[base : base + nb, :] = slabs[b]
        for j in range(nb):
            at = base + nb * (j + 1)
            spread[at : at + nb, :] = lane(slabs[b], nb * b + j)
        pivot_rows = [row(base + i) for i in range(nb)]
        splat = [[row(base + nb * (j + 1) + i) for j in range(i + 1)] for i in range(nb)]
        below = {s: [lane(slabs[s], nb * b + j) for j in range(nb)] for s in range(b + 1, count)}
        out = None
        for k in range(nb):
            inv = 1.0 / splat[k][k]
            at = pivot_rows[k]
            final = at * lax.rsqrt(splat[k][k])
            out = final if out is None else jnp.where(sub == k, final, out)
            for i in range(k + 1, nb):
                mult = splat[i][k] * inv
                for j in range(k + 1, i + 1):
                    splat[i][j] = splat[i][j] - mult * splat[j][k]
                pivot_rows[i] = pivot_rows[i] - mult * at
            for s in range(b + 1, count):
                mult = below[s][k] * inv
                for j in range(k + 1, nb):
                    below[s][j] = below[s][j] - mult * splat[j][k]
                slabs[s] = slabs[s] - mult * at
        done.append(out)
    return jnp.concatenate(done, axis=0)[:, :n]


def split(x):
    high = x.astype(bf16)
    return high, (x - high.astype(f32)).astype(bf16)


def times(rows, gram):
    n = rows.shape[0]
    both = jnp.dot(jnp.concatenate(split(rows), axis=0), gram, preferred_element_type=f32)
    return both[:n] + both[n:]


def product(a, b):
    (ah, al), (bh, bl) = split(a), split(b)
    return jnp.dot(
        jnp.concatenate([ah, ah, al], axis=1),
        jnp.concatenate([bh, bl, bh], axis=0),
        preferred_element_type=f32,
    )


def product_nt(a, b):
    (ah, al), (bh, bl) = split(a), split(b)
    return nt(jnp.concatenate([ah, ah, al], axis=1), jnp.concatenate([bh, bl, bh], axis=1))


def chain_kernel(dps, counts, idx, *refs):
    z, out_half, core = idx[0], idx[1], idx[2]
    quarters, big, small, out, stays, leaves, flat, thin, wide, left, right, spread = (
        refs[:4],
        *refs[4:],
    )
    size, bit = quarters[0].shape[0], z % 2
    for n, ref in enumerate(quarters):
        which = 2 * (core ^ (n // 2)) + (bit ^ (n % 2))
        flat[pl.ds(pl.multiple_of(which * size, 16), size), :] = ref[...]
    per_gram, thin_rows, wide_rows = packed_rows(dps)
    for n in range(2):
        at, split_at = n * 2 * size, n * 2 * size + thin_rows // 2
        thin[n * (thin_rows // 2) : (n + 1) * (thin_rows // 2), :] = flat[at:split_at, :]
        wide[n * (wide_rows // 2) : (n + 1) * (wide_rows // 2), :] = flat[split_at : at + 2 * size, :]
    r = lax.broadcasted_iota(jnp.int32, (BLK, BLK), 0)
    c = lax.broadcasted_iota(jnp.int32, (BLK, BLK), 1)
    rows = jnp.concatenate(
        [wide[per_gram + i * RANK : per_gram + (i + 1) * RANK, :] for i in range(dps)], axis=1
    ).astype(f32)
    wide_diag = wide[per_gram + dps * RANK : per_gram + dps * RANK + 16, :].astype(f32)
    thin_diag = thin[per_gram : per_gram + 16, :].astype(f32)
    is_out = out_half == 1
    for gram, is_wide in ((left, out_half == 0), (right, is_out)):

        def block(n):
            part = slice(n * BLK, (n + 1) * BLK)
            return jnp.where(is_wide, wide[part, :].astype(f32), thin[part, :].astype(f32))

        def put(i, j, value):
            gram[i * BLK : (i + 1) * BLK, j * BLK : (j + 1) * BLK] = value.astype(bf16)

        n = 0
        for i in range(dps):
            for j in range(i):
                value = block(n)
                put(i, j, value)
                put(j, i, value.T)
                n += 1
        diag = jnp.where(is_wide, wide_diag, thin_diag)
        for i in range(0, dps, 2):
            value = block(n)
            turned = value.T
            put(i, i, jnp.where(r > c, value, jnp.where(r == c, diag[i : i + 1, :], turned)))
            put(
                i + 1,
                i + 1,
                jnp.where(r < c, value, jnp.where(r == c, diag[i + 1 : i + 2, :], turned)),
            )
            n += 1
    ahead = times(rows, left[...])
    gram = product_nt(ahead, rows)
    for step in range(2 * POWER):
        following = (right if step % 2 == 0 else left)[...]
        beyond = times(ahead, following)
        inner = product_nt(beyond, ahead)
        low_inv = inverse_factor(gram, spread)
        rows = product(low_inv, ahead)
        if step < 2 * POWER - 1:
            gram = product_nt(product(low_inv, inner), low_inv)
            ahead = product(low_inv, beyond)
        else:
            ahead = times(rows, following)
            gram = product_nt(ahead, rows)
    low_inv = inverse_factor(gram, spread)
    basis = product(low_inv, rows)
    rows = product(low_inv, ahead)
    energy = jnp.sum(times(rows, right[...]) * rows)
    count = jnp.where(out_half == 1, counts[0], counts[1]).astype(f32)
    scale = lax.rsqrt(jnp.full((1, 1), energy, f32) / count + 1e-06)
    coef_b, coef_a = basis.astype(bf16), rows.astype(bf16)
    for_big = jnp.where(is_out, coef_a, coef_b)
    for_small = jnp.where(is_out, coef_b, coef_a)
    scale_big = jnp.where(is_out, scale, 16.0)
    scale_small = jnp.where(is_out, 16.0, scale)
    big_w, small_w = big.shape[1] // 2, small.shape[1] // 2
    made_big = (jnp.dot(for_big, big[...], preferred_element_type=f32) * scale_big).astype(bf16)
    made_small = (jnp.dot(for_small, small[...], preferred_element_type=f32) * scale_small).astype(
        bf16
    )
    for n, half in enumerate((stays, leaves)):
        half[:, :big_w] = made_big[:, n * big_w : (n + 1) * big_w]
        half[:, big_w:] = made_small[:, n * small_w : (n + 1) * small_w]
        out[n * RANK : (n + 1) * RANK, :] = half[...]


def place_kernel(dps, idx, *refs):
    z, kind = idx[0], idx[3]
    mine, theirs = refs[:dps], refs[dps : 2 * dps]
    b_q, a_q, b_o, a_o = refs[2 * dps :]
    big_w, small_w = b_q.shape[1] // dps, a_q.shape[1] // dps
    for d in range(dps):
        bigs = pl.ds(pl.multiple_of((z ^ d) * big_w, big_w), big_w)
        smalls = pl.ds(pl.multiple_of((z ^ d) * small_w, small_w), small_w)
        here, there = mine[d].at[:RANK], theirs[d].at[theirs[d].shape[0] - RANK :]
        for which, query, output in ((0, here, there), (1, there, here)):

            @pl.when(kind == which)
            def _():
                b_q[:, bigs] = query[:, :big_w]
                a_q[:, smalls] = query[:, big_w:].astype(f32)
                a_o[:, bigs] = output[:, :big_w].astype(f32)
                b_o[:, smalls] = output[:, big_w:]


def call(kernel, out_shapes, args, scratch=(), spaces=()):
    spaces = [SMEM] + [VMEM] * (len(args) - 1) if not spaces else spaces
    return pl.pallas_call(
        kernel,
        out_shape=out_shapes,
        in_specs=spaces,
        out_specs=jax.tree.map(lambda _: VMEM, out_shapes),
        scratch_shapes=list(scratch),
        compiler_params=pltpu.CompilerParams(vmem_limit_bytes=48 * 2**20),
    )(*args)


def token_space(sizes, norm_in, query_grad, attn_out, handed, sketch_q, sketch_o):
    _, dps, tensors = sizes
    side = tensors // 2

    def shape(*dims, dtype=bf16):
        return jax.ShapeDtypeStruct(dims, dtype)

    z, t = lax.axis_index("dp"), lax.axis_index("tensor")
    half, core = t // side, t % side
    idx = jnp.stack([z, half, core, half ^ core]).astype(jnp.int32)
    wide, narrow = norm_in.shape[2], query_grad.shape[2]
    big_w, small_w = wide // dps, narrow // dps
    tokens = dps * BLK
    hbm = pl.BlockSpec(memory_space=pltpu.HBM)
    norm, grad, attn, hand, sk_q, sk_o = (
        pltpu.with_memory_space_constraint(v[0], pltpu.HBM)
        for v in (norm_in, query_grad, attn_out, handed, sketch_q, sketch_o)
    )

    give = call(
        functools.partial(give_kernel, dps),
        shape(BLK + RANK // dps, wide + narrow),
        (idx, norm, grad, attn, hand, sk_q, sk_o),
        [pltpu.SemaphoreType.DMA((2 + dps,))],
        [SMEM] + [hbm] * 6,
    )
    got = swap(give, "tensor", 1)
    smalls = call(
        functools.partial(merge_thin_kernel, dps),
        [shape(BLK, 2 * small_w)] * dps,
        (idx, grad, attn, got),
        [pltpu.SemaphoreType.DMA((dps,))],
        [SMEM, hbm, hbm, VMEM],
    )
    packed = call(
        functools.partial(merge_wide_kernel, dps),
        [shape(BLK, 2 * big_w)] * dps + [shape(3 * RANK, 2 * small_w)],
        (idx, norm, hand, sk_q, sk_o, got),
        [pltpu.SemaphoreType.DMA((dps + 1,))],
        [SMEM, hbm, hbm, hbm, hbm, VMEM],
    )
    smalls = [routed(smalls[d], sizes, d, False) for d in THIN_ORDER]
    sketch = routed(packed[dps], sizes, 0, False)
    bigs = [routed(packed[d], sizes, d, True) for d in WIDE_ORDER]

    _, thin_rows, wide_rows = packed_rows(dps)

    def gram(kernel, m, rows, operands):
        m, keep, send = call(
            functools.partial(kernel, dps),
            [m, shape(rows // 2, BLK), shape(rows // 2, BLK)],
            (idx, *operands),
            [pltpu.VMEM((rows, BLK), bf16)],
        )
        return m, keep, swap(send, "tensor", 1)

    small, *thin = gram(thin_gram_kernel, shape(tokens, 2 * small_w), thin_rows, smalls)
    big, *rest = gram(
        wide_gram_kernel, shape(tokens, 2 * big_w), wide_rows, (sketch, *bigs, small)
    )
    total = thin_rows + wide_rows
    quarter = shape(total // 4, BLK)
    keep, send = call(
        add_halves_kernel,
        [quarter] * 2,
        (idx, *thin, *rest),
        [pltpu.VMEM((total // 2, BLK), bf16)],
    )
    for bit, value in ((1, send), (2, None)):
        value = swap(keep if value is None else value, "dp", bit)
        keep = call(add_kernel, quarter, (keep, value), (), [VMEM] * 2)
    beside = swap(keep, "dp", 1)
    quarters = (keep, beside, swap(keep, "tensor", 1), swap(beside, "tensor", 1))

    counts = (RANK * wide * tensors, RANK * narrow * tensors)
    whole, stays, leaves = call(
        functools.partial(chain_kernel, dps, counts),
        [shape(2 * RANK, big_w + small_w)] + [shape(RANK, big_w + small_w)] * 2,
        (idx, *quarters, big, small),
        [
            pltpu.VMEM((total, BLK), bf16),
            pltpu.VMEM((thin_rows, BLK), bf16),
            pltpu.VMEM((wide_rows, BLK), bf16),
            pltpu.VMEM((tokens, tokens), bf16),
            pltpu.VMEM((tokens, tokens), bf16),
            pltpu.VMEM((9 * RANK, 2 * RANK), f32),
        ],
    )
    leaves, stays = routed(leaves, sizes, 2, False), routed(stays, sizes, 2, False)
    near, here = routed(whole, sizes, 1, False), routed(whole, sizes, 0, False)
    leaves_on, stays_on = swap(leaves, "dp", 1), swap(stays, "dp", 1)
    mine = (here, near, stays, stays_on)
    theirs = [swap(v, "tensor", 1) for v in (here, near, leaves, leaves_on)]
    outs = call(
        functools.partial(place_kernel, dps),
        [
            shape(RANK, wide),
            shape(RANK, narrow, dtype=f32),
            shape(RANK, narrow),
            shape(RANK, wide, dtype=f32),
        ],
        (idx, *mine, *theirs),
    )
    return tuple(o[None] for o in outs)


def solution(mesh):
    sizes = tuple(mesh.shape[axis] for axis in ("section", "dp", "tensor"))
    _, dps, tensors = sizes

    def body(norm_in, query_grad, attn_out, handed, sketch_q, sketch_o):
        args = (norm_in, query_grad, attn_out, handed, sketch_q, sketch_o)
        fits = (
            dps == 4
            and tensors == 4
            and norm_in.shape[1] == BLK
            and sketch_q.shape[1] == RANK
            and norm_in.shape[2] == handed.shape[2]
            and query_grad.shape[2] == attn_out.shape[2]
            and norm_in.shape[2] == 2 * query_grad.shape[2]
            and query_grad.shape[2] % (dps * 128) == 0
        )
        return token_space(sizes, *args) if fits else feature_space(*args)

    return jax.shard_map(
        body,
        mesh=mesh,
        in_specs=(P("section", "dp", "tensor"),) * 4 + (P("section", None, "tensor"),) * 2,
        out_specs=(P("section", None, "tensor"),) * 4,
        check_vma=False,
    )
```

```python
import functools

import jax
import jax.numpy as jnp
from jax import lax
from jax.experimental import pallas as pl
from jax.experimental.pallas import tpu as pltpu
from jax.sharding import PartitionSpec as P

RANK = 64
POWER = 2
BLK = 128
THIN_ORDER = (2, 1, 0, 3)
WIDE_ORDER = (2, 3, 1, 0)

precise = lax.Precision.HIGHEST
f32 = jnp.float32
bf16 = jnp.bfloat16
VMEM = pl.BlockSpec(memory_space=pltpu.VMEM)
SMEM = pl.BlockSpec(memory_space=pltpu.SMEM)


def from_behind(value, axis, steps):
    count = lax.axis_size(axis)
    pairs = [(source, (source + steps) % count) for source in range(count)]
    return lax.ppermute(value, axis, pairs)


def gram_of(row_block):
    return jnp.dot(row_block, row_block.T, precision=precise, preferred_element_type=f32)


def solve_rows(gram_rows, row_block):
    low_factor = jnp.linalg.cholesky(gram_rows)
    solved = lax.linalg.triangular_solve(low_factor, row_block, left_side=True, lower=True)
    return solved.astype(bf16)


def tokens_of(sketches, matrices):
    parts = [
        jnp.einsum("km,tm->kt", s, m, preferred_element_type=f32)
        for s, m in zip(sketches, matrices)
    ]
    return tuple(lax.psum(p.astype(bf16), "tensor").astype(bf16) for p in parts)


def partials(token_rows, matrices):
    return tuple(
        jnp.dot(r, m, preferred_element_type=f32) for r, m in zip(token_rows, matrices)
    )


def orthonormal(parts):
    rows = [lax.psum(p.astype(bf16), "dp").astype(f32) for p in parts]
    grams = [lax.psum(gram_of(r).astype(bf16), "tensor").astype(f32) for r in rows]
    return tuple(solve_rows(g, r) for g, r in zip(grams, rows))


def feature_space(norm_in, query_grad, attn_out, handed, sketch_q, sketch_o):
    upstream = from_behind(handed, "section", -1)
    lefts = (norm_in[0], attn_out[0])
    rights = (query_grad[0], upstream[0])
    basis = orthonormal(partials(tokens_of((sketch_q[0], sketch_o[0]), rights), lefts))
    for _ in range(POWER):
        other = orthonormal(partials(tokens_of(basis, lefts), rights))
        basis = orthonormal(partials(tokens_of(other, rights), lefts))
    final = partials(tokens_of(basis, lefts), rights)
    raws = [lax.psum(p.astype(bf16), "dp").astype(f32) for p in final]
    energies = lax.psum(tuple(jnp.sum(r * r) for r in raws), "tensor")
    count = lax.axis_size("tensor")
    adapters = [
        r / jnp.sqrt(e / (r.size * count) + 1e-06) for r, e in zip(raws, energies)
    ]
    return (
        (basis[0] * 16.0)[None],
        adapters[0][None],
        (basis[1] * 16.0)[None],
        adapters[1][None],
    )


def swap(value, axis, bit):
    count = lax.axis_size(axis)
    return lax.ppermute(value, axis, [(i, i ^ bit) for i in range(count)])


def routed(value, sizes, token_bit, shifted):
    sections, dps, tensors = sizes
    side = tensors // 2
    pairs = []
    for s in range(sections):
        for z in range(dps):
            for t in range(tensors):
                to_t = t ^ side if t % side else t
                to_s = (s - 1) % sections if shifted and to_t >= side else s
                to = (to_s * dps + (z ^ token_bit)) * tensors + to_t
                pairs.append(((s * dps + z) * tensors + t, to))
    return lax.ppermute(value, ("section", "dp", "tensor"), pairs)


def window(ref, width, at):
    return ref.at[:, pl.ds(pl.multiple_of(at * width, width), width)]


def move(pairs, sems):
    copies = [pltpu.make_async_copy(src, dst, sems.at[n]) for n, (src, dst) in enumerate(pairs)]
    for c in copies:
        c.start()
    for c in copies:
        c.wait()


def give_thin_kernel(idx, grad, attn, give, sems):
    for which, ref in ((0, attn), (1, grad)):

        @pl.when(idx[3] == which)
        def _():
            move([(ref, give)], sems)


def give_wide_kernel(dps, idx, norm, hand, sk_q, sk_o, give, sems):
    z, kind = idx[0], idx[3]
    rows, fold = RANK // dps, give.shape[1] // dps
    small_w = sk_q.shape[1] // dps

    def sketch(ref, width):
        part = ref.at[:, pl.ds(pl.multiple_of(z * width, width), width)]
        return [
            (part.at[i * rows : (i + 1) * rows], give.at[BLK:, i * fold : i * fold + width])
            for i in range(dps)
        ]

    @pl.when(kind == 0)
    def _():
        move([(hand, give.at[:BLK])] + sketch(sk_o, fold), sems)

    @pl.when(kind == 1)
    def _():
        give[BLK:, :] = jnp.zeros((rows, give.shape[1]), bf16)
        move([(norm, give.at[:BLK])] + sketch(sk_q, small_w), sems)


def merge_kernel(dps, kind, fill, pairs, sems):
    for which in (0, 1):

        @pl.when(kind == which)
        def _():
            copies = [
                pltpu.make_async_copy(src, dst, sems.at[n])
                for n, (src, dst) in enumerate(pairs[which])
            ]
            for c in copies:
                c.start()
            fill(which)
            for c in copies:
                c.wait()


def merge_thin_kernel(dps, idx, grad, attn, got, *refs):
    z, kind, smalls, sems = idx[0], idx[3], refs[:dps], refs[-1]
    small_w = smalls[0].shape[1] // 2

    def fill(_):
        for d in range(dps):
            at = pl.multiple_of((z ^ d) * small_w, small_w)
            smalls[d][:, small_w:] = got[:, pl.ds(at, small_w)]

    def keep(ref):
        return [
            (window(ref, small_w, z ^ d), smalls[d].at[:, :small_w]) for d in range(dps)
        ]

    merge_kernel(dps, kind, fill, (keep(grad), keep(attn)), sems)


def merge_wide_kernel(dps, idx, norm, hand, sk_q, sk_o, got, *refs):
    z, kind, bigs, sk, sems = idx[0], idx[3], refs[:dps], refs[dps], refs[-1]
    big_w, small_w = bigs[0].shape[1] // 2, sk.shape[1] // 2
    rows = RANK // dps

    def fill(which):
        for d in range(dps):
            at = pl.multiple_of((z ^ d) * big_w, big_w)
            bigs[d][:, big_w:] = got[:BLK, pl.ds(at, big_w)]
        for i in range(dps):
            part = got[BLK:, i * big_w : (i + 1) * big_w]
            one, two = RANK + i * rows, 2 * RANK + i * rows
            if which == 0:
                sk[one : one + rows, :] = jnp.zeros_like(part)
                sk[two : two + rows, small_w:] = part[:, :small_w]
            else:
                sk[one : one + rows, :] = part
                sk[two : two + rows, small_w:] = jnp.zeros_like(part[:, :small_w])
        if which == 0:
            sk[:RANK, :] = jnp.zeros((RANK, big_w), bf16)
        else:
            sk[2 * RANK :, :small_w] = jnp.zeros((RANK, small_w), bf16)

    def keep(ref, sketch):
        return [sketch] + [
            (window(ref, big_w, z ^ d), bigs[d].at[:, :big_w]) for d in range(dps)
        ]

    pairs = (
        keep(norm, (window(sk_q, small_w, z), sk.at[2 * RANK :, :small_w])),
        keep(hand, (window(sk_o, big_w, z), sk.at[:RANK, :])),
    )
    merge_kernel(dps, kind, fill, pairs, sems)


def nt(a, b, precision=None):
    return lax.dot_general(
        a, b, (((1,), (1,)), ((), ())), precision=precision, preferred_element_type=f32
    )


def packed_rows(dps):
    per_gram = (dps * (dps - 1) // 2 + dps // 2) * BLK
    thin = pl.cdiv(per_gram + 16, 32) * 32
    rest = per_gram + dps * RANK + 16
    wide = pl.cdiv(thin + rest, 64) * 64 - thin
    return per_gram, thin, wide


def pack_gram(m, flat, dps):
    r = lax.broadcasted_iota(jnp.int32, (BLK, BLK), 0)
    c = lax.broadcasted_iota(jnp.int32, (BLK, BLK), 1)
    at, on = 0, []
    for i in range(dps):
        row = nt(m[i * BLK : (i + 1) * BLK, :], m[: (i + 1) * BLK, :])
        for j in range(i):
            flat[at : at + BLK, :] = row[:, j * BLK : (j + 1) * BLK].astype(bf16)
            at += BLK
        on.append(row[:, i * BLK :])
    for i in range(0, dps, 2):
        flat[at : at + BLK, :] = jnp.where(r > c, on[i], on[i + 1]).astype(bf16)
        at += BLK
    diagonals = [jnp.sum(jnp.where(r == c, v, 0.0), axis=0, keepdims=True) for v in on]
    diagonals.append(jnp.zeros((16 - dps, BLK), f32))
    return at, jnp.concatenate(diagonals, axis=0).astype(bf16)


def hand_out(core, flat, keep, send):
    half = flat.shape[0] // 2
    keep[...] = flat[pl.ds(pl.multiple_of(core * half, 16), half), :]
    send[...] = flat[pl.ds(pl.multiple_of((1 - core) * half, 16), half), :]


def thin_gram_kernel(dps, idx, *refs):
    z, core = idx[0], idx[2]
    smalls, small, keep, send, flat = refs[:dps], *refs[dps:]
    for d, ref in zip(THIN_ORDER, smalls):
        small[pl.ds(pl.multiple_of((z ^ d) * BLK, BLK), BLK), :] = ref[...]
    at, diagonals = pack_gram(small, flat, dps)
    flat[at:, :] = jnp.zeros((flat.shape[0] - at, BLK), bf16)
    flat[at : at + 16, :] = diagonals
    hand_out(core, flat, keep, send)


def wide_gram_kernel(dps, idx, *refs):
    z, core = idx[0], idx[2]
    sk, bigs, small, big, keep, send, flat = refs[0], refs[1 : dps + 1], *refs[dps + 1 :]
    half_w = big.shape[1] // 2
    for d, ref in zip(WIDE_ORDER, bigs):
        big[pl.ds(pl.multiple_of((z ^ d) * BLK, BLK), BLK), :] = ref[...]
    at, diagonals = pack_gram(big, flat, dps)
    first = (
        nt(sk[:RANK, :], big[:, :half_w])
        + nt(sk[RANK : 2 * RANK, :], big[:, half_w:])
        + nt(sk[2 * RANK :, :], small[...])
    ).astype(bf16)
    for i in range(dps):
        flat[at : at + RANK, :] = first[:, i * BLK : (i + 1) * BLK]
        at += RANK
    flat[at:, :] = jnp.zeros((flat.shape[0] - at, BLK), bf16)
    flat[at : at + 16, :] = diagonals
    hand_out(core, flat, keep, send)


def add_halves_kernel(idx, thin_mine, thin_got, wide_mine, wide_got, keep, send, both):
    size, bit, split_at = keep.shape[0], idx[0] % 2, thin_mine.shape[0]
    both[:split_at, :] = (thin_mine[...].astype(f32) + thin_got[...].astype(f32)).astype(bf16)
    both[split_at:, :] = (wide_mine[...].astype(f32) + wide_got[...].astype(f32)).astype(bf16)
    for out, which in ((keep, bit), (send, 1 - bit)):
        out[...] = both[pl.ds(pl.multiple_of(which * size, 16), size), :]


def add_kernel(mine, got, out):
    out[...] = (mine[...].astype(f32) + got[...].astype(f32)).astype(bf16)


def inverse_factor(gram, spread):
    n, nb = gram.shape[0], 8
    rows = lax.broadcasted_iota(jnp.int32, (n, n), 0)
    cols = lax.broadcasted_iota(jnp.int32, (n, n), 1)
    work = jnp.concatenate([(rows == cols).astype(f32), gram], axis=1)
    count = n // nb
    slabs = [work[nb * s : nb * s + nb, :] for s in range(count)]
    sub = lax.broadcasted_iota(jnp.int32, (nb, 2 * n), 0)

    def lane(x, k):
        return jnp.broadcast_to(x[:, n + k : n + k + 1], (nb, 2 * n))

    def row(at):
        return jnp.broadcast_to(spread[at : at + 1, :], (nb, 2 * n))

    done = []
    for b in range(count):
        base = b * nb * (nb + 1)
        spread[base : base + nb, :] = slabs[b]
        for j in range(nb):
            at = base + nb * (j + 1)
            spread[at : at + nb, :] = lane(slabs[b], nb * b + j)
        pivot_rows = [row(base + i) for i in range(nb)]
        splat = [[row(base + nb * (j + 1) + i) for j in range(i + 1)] for i in range(nb)]
        below = {s: [lane(slabs[s], nb * b + j) for j in range(nb)] for s in range(b + 1, count)}
        out = None
        for k in range(nb):
            inv = 1.0 / splat[k][k]
            at = pivot_rows[k]
            final = at * lax.rsqrt(splat[k][k])
            out = final if out is None else jnp.where(sub == k, final, out)
            for i in range(k + 1, nb):
                mult = splat[i][k] * inv
                for j in range(k + 1, i + 1):
                    splat[i][j] = splat[i][j] - mult * splat[j][k]
                pivot_rows[i] = pivot_rows[i] - mult * at
            for s in range(b + 1, count):
                mult = below[s][k] * inv
                for j in range(k + 1, nb):
                    below[s][j] = below[s][j] - mult * splat[j][k]
                slabs[s] = slabs[s] - mult * at
        done.append(out)
    return jnp.concatenate(done, axis=0)[:, :n]


def split(x):
    high = x.astype(bf16)
    return high, (x - high.astype(f32)).astype(bf16)


def times(rows, gram):
    n = rows.shape[0]
    both = jnp.dot(jnp.concatenate(split(rows), axis=0), gram, preferred_element_type=f32)
    return both[:n] + both[n:]


def product(a, b):
    (ah, al), (bh, bl) = split(a), split(b)
    return jnp.dot(
        jnp.concatenate([ah, ah, al], axis=1),
        jnp.concatenate([bh, bl, bh], axis=0),
        preferred_element_type=f32,
    )


def product_nt(a, b):
    (ah, al), (bh, bl) = split(a), split(b)
    return nt(jnp.concatenate([ah, ah, al], axis=1), jnp.concatenate([bh, bl, bh], axis=1))


def chain_kernel(dps, counts, idx, *refs):
    z, out_half, core = idx[0], idx[1], idx[2]
    quarters, big, small, out, stays, leaves, flat, thin, wide, left, right, spread = (
        refs[:4],
        *refs[4:],
    )
    size, bit = quarters[0].shape[0], z % 2
    for n, ref in enumerate(quarters):
        which = 2 * (core ^ (n // 2)) + (bit ^ (n % 2))
        flat[pl.ds(pl.multiple_of(which * size, 16), size), :] = ref[...]
    per_gram, thin_rows, wide_rows = packed_rows(dps)
    for n in range(2):
        at, split_at = n * 2 * size, n * 2 * size + thin_rows // 2
        thin[n * (thin_rows // 2) : (n + 1) * (thin_rows // 2), :] = flat[at:split_at, :]
        wide[n * (wide_rows // 2) : (n + 1) * (wide_rows // 2), :] = flat[split_at : at + 2 * size, :]
    r = lax.broadcasted_iota(jnp.int32, (BLK, BLK), 0)
    c = lax.broadcasted_iota(jnp.int32, (BLK, BLK), 1)
    rows = jnp.concatenate(
        [wide[per_gram + i * RANK : per_gram + (i + 1) * RANK, :] for i in range(dps)], axis=1
    ).astype(f32)
    wide_diag = wide[per_gram + dps * RANK : per_gram + dps * RANK + 16, :].astype(f32)
    thin_diag = thin[per_gram : per_gram + 16, :].astype(f32)
    is_out = out_half == 1
    for gram, is_wide in ((left, out_half == 0), (right, is_out)):

        def block(n):
            part = slice(n * BLK, (n + 1) * BLK)
            return jnp.where(is_wide, wide[part, :].astype(f32), thin[part, :].astype(f32))

        def put(i, j, value):
            gram[i * BLK : (i + 1) * BLK, j * BLK : (j + 1) * BLK] = value.astype(bf16)

        n = 0
        for i in range(dps):
            for j in range(i):
                value = block(n)
                put(i, j, value)
                put(j, i, value.T)
                n += 1
        diag = jnp.where(is_wide, wide_diag, thin_diag)
        for i in range(0, dps, 2):
            value = block(n)
            turned = value.T
            put(i, i, jnp.where(r > c, value, jnp.where(r == c, diag[i : i + 1, :], turned)))
            put(
                i + 1,
                i + 1,
                jnp.where(r < c, value, jnp.where(r == c, diag[i + 1 : i + 2, :], turned)),
            )
            n += 1
    ahead = times(rows, left[...])
    gram = product_nt(ahead, rows)
    for step in range(2 * POWER):
        following = (right if step % 2 == 0 else left)[...]
        beyond = times(ahead, following)
        inner = product_nt(beyond, ahead)
        low_inv = inverse_factor(gram, spread)
        rows = product(low_inv, ahead)
        if step < 2 * POWER - 1:
            gram = product_nt(product(low_inv, inner), low_inv)
            ahead = product(low_inv, beyond)
        else:
            ahead = times(rows, following)
            gram = product_nt(ahead, rows)
    low_inv = inverse_factor(gram, spread)
    basis = product(low_inv, rows)
    rows = product(low_inv, ahead)
    energy = jnp.sum(times(rows, right[...]) * rows)
    count = jnp.where(out_half == 1, counts[0], counts[1]).astype(f32)
    scale = lax.rsqrt(jnp.full((1, 1), energy, f32) / count + 1e-06)
    coef_b, coef_a = basis.astype(bf16), rows.astype(bf16)
    for_big = jnp.where(is_out, coef_a, coef_b)
    for_small = jnp.where(is_out, coef_b, coef_a)
    scale_big = jnp.where(is_out, scale, 16.0)
    scale_small = jnp.where(is_out, 16.0, scale)
    big_w, small_w = big.shape[1] // 2, small.shape[1] // 2
    made_big = (jnp.dot(for_big, big[...], preferred_element_type=f32) * scale_big).astype(bf16)
    made_small = (jnp.dot(for_small, small[...], preferred_element_type=f32) * scale_small).astype(
        bf16
    )
    for n, half in enumerate((stays, leaves)):
        half[:, :big_w] = made_big[:, n * big_w : (n + 1) * big_w]
        half[:, big_w:] = made_small[:, n * small_w : (n + 1) * small_w]
        out[n * RANK : (n + 1) * RANK, :] = half[...]


def place_kernel(dps, idx, *refs):
    z, kind = idx[0], idx[3]
    mine, theirs = refs[:dps], refs[dps : 2 * dps]
    b_q, a_q, b_o, a_o = refs[2 * dps :]
    big_w, small_w = b_q.shape[1] // dps, a_q.shape[1] // dps
    for d in range(dps):
        bigs = pl.ds(pl.multiple_of((z ^ d) * big_w, big_w), big_w)
        smalls = pl.ds(pl.multiple_of((z ^ d) * small_w, small_w), small_w)
        here, there = mine[d].at[:RANK], theirs[d].at[theirs[d].shape[0] - RANK :]
        for which, query, output in ((0, here, there), (1, there, here)):

            @pl.when(kind == which)
            def _():
                b_q[:, bigs] = query[:, :big_w]
                a_q[:, smalls] = query[:, big_w:].astype(f32)
                a_o[:, bigs] = output[:, :big_w].astype(f32)
                b_o[:, smalls] = output[:, big_w:]


def call(kernel, out_shapes, args, scratch=(), spaces=()):
    spaces = [SMEM] + [VMEM] * (len(args) - 1) if not spaces else spaces
    return pl.pallas_call(
        kernel,
        out_shape=out_shapes,
        in_specs=spaces,
        out_specs=jax.tree.map(lambda _: VMEM, out_shapes),
        scratch_shapes=list(scratch),
        compiler_params=pltpu.CompilerParams(vmem_limit_bytes=48 * 2**20),
    )(*args)


def token_space(sizes, norm_in, query_grad, attn_out, handed, sketch_q, sketch_o):
    _, dps, tensors = sizes
    side = tensors // 2

    def shape(*dims, dtype=bf16):
        return jax.ShapeDtypeStruct(dims, dtype)

    z, t = lax.axis_index("dp"), lax.axis_index("tensor")
    half, core = t // side, t % side
    idx = jnp.stack([z, half, core, half ^ core]).astype(jnp.int32)
    wide, narrow = norm_in.shape[2], query_grad.shape[2]
    big_w, small_w = wide // dps, narrow // dps
    tokens = dps * BLK
    hbm = pl.BlockSpec(memory_space=pltpu.HBM)
    norm, grad, attn, hand, sk_q, sk_o = (
        pltpu.with_memory_space_constraint(v[0], pltpu.HBM)
        for v in (norm_in, query_grad, attn_out, handed, sketch_q, sketch_o)
    )

    give_thin = call(
        give_thin_kernel,
        shape(BLK, narrow),
        (idx, grad, attn),
        [pltpu.SemaphoreType.DMA((1,))],
        [SMEM] + [hbm] * 2,
    )
    after, give_thin = lax.optimization_barrier((idx, give_thin))
    got_thin = swap(give_thin, "tensor", 1)
    give = call(
        functools.partial(give_wide_kernel, dps),
        shape(BLK + RANK // dps, wide),
        (after, norm, hand, sk_q, sk_o),
        [pltpu.SemaphoreType.DMA((1 + dps,))],
        [SMEM] + [hbm] * 4,
    )
    give, got_thin = lax.optimization_barrier((give, got_thin))
    smalls = call(
        functools.partial(merge_thin_kernel, dps),
        [shape(BLK, 2 * small_w)] * dps,
        (idx, grad, attn, got_thin),
        [pltpu.SemaphoreType.DMA((dps,))],
        [SMEM, hbm, hbm, VMEM],
    )
    got = swap(give, "tensor", 1)
    packed = call(
        functools.partial(merge_wide_kernel, dps),
        [shape(BLK, 2 * big_w)] * dps + [shape(3 * RANK, 2 * small_w)],
        (idx, norm, hand, sk_q, sk_o, got),
        [pltpu.SemaphoreType.DMA((dps + 1,))],
        [SMEM, hbm, hbm, hbm, hbm, VMEM],
    )
    smalls = [routed(smalls[d], sizes, d, False) for d in THIN_ORDER]
    sketch = routed(packed[dps], sizes, 0, False)
    bigs = [routed(packed[d], sizes, d, True) for d in WIDE_ORDER]

    _, thin_rows, wide_rows = packed_rows(dps)

    def gram(kernel, m, rows, operands):
        m, keep, send = call(
            functools.partial(kernel, dps),
            [m, shape(rows // 2, BLK), shape(rows // 2, BLK)],
            (idx, *operands),
            [pltpu.VMEM((rows, BLK), bf16)],
        )
        return m, keep, swap(send, "tensor", 1)

    small, *thin = gram(thin_gram_kernel, shape(tokens, 2 * small_w), thin_rows, smalls)
    big, *rest = gram(
        wide_gram_kernel, shape(tokens, 2 * big_w), wide_rows, (sketch, *bigs, small)
    )
    total = thin_rows + wide_rows
    quarter = shape(total // 4, BLK)
    keep, send = call(
        add_halves_kernel,
        [quarter] * 2,
        (idx, *thin, *rest),
        [pltpu.VMEM((total // 2, BLK), bf16)],
    )
    for bit, value in ((1, send), (2, None)):
        value = swap(keep if value is None else value, "dp", bit)
        keep = call(add_kernel, quarter, (keep, value), (), [VMEM] * 2)
    beside = swap(keep, "dp", 1)
    quarters = (keep, beside, swap(keep, "tensor", 1), swap(beside, "tensor", 1))

    counts = (RANK * wide * tensors, RANK * narrow * tensors)
    whole, stays, leaves = call(
        functools.partial(chain_kernel, dps, counts),
        [shape(2 * RANK, big_w + small_w)] + [shape(RANK, big_w + small_w)] * 2,
        (idx, *quarters, big, small),
        [
            pltpu.VMEM((total, BLK), bf16),
            pltpu.VMEM((thin_rows, BLK), bf16),
            pltpu.VMEM((wide_rows, BLK), bf16),
            pltpu.VMEM((tokens, tokens), bf16),
            pltpu.VMEM((tokens, tokens), bf16),
            pltpu.VMEM((9 * RANK, 2 * RANK), f32),
        ],
    )
    leaves, stays = routed(leaves, sizes, 2, False), routed(stays, sizes, 2, False)
    near, here = routed(whole, sizes, 1, False), routed(whole, sizes, 0, False)
    leaves_on, stays_on = swap(leaves, "dp", 1), swap(stays, "dp", 1)
    here, near, stays = lax.optimization_barrier((here, near, stays))
    mine = (here, near, stays, stays_on)
    theirs = [swap(v, "tensor", 1) for v in (here, near, leaves, leaves_on)]
    outs = call(
        functools.partial(place_kernel, dps),
        [
            shape(RANK, wide),
            shape(RANK, narrow, dtype=f32),
            shape(RANK, narrow),
            shape(RANK, wide, dtype=f32),
        ],
        (idx, *mine, *theirs),
    )
    return tuple(o[None] for o in outs)


def solution(mesh):
    sizes = tuple(mesh.shape[axis] for axis in ("section", "dp", "tensor"))
    _, dps, tensors = sizes

    def body(norm_in, query_grad, attn_out, handed, sketch_q, sketch_o):
        args = (norm_in, query_grad, attn_out, handed, sketch_q, sketch_o)
        fits = (
            dps == 4
            and tensors == 4
            and norm_in.shape[1] == BLK
            and sketch_q.shape[1] == RANK
            and norm_in.shape[2] == handed.shape[2]
            and query_grad.shape[2] == attn_out.shape[2]
            and norm_in.shape[2] == 2 * query_grad.shape[2]
            and query_grad.shape[2] % (dps * 128) == 0
        )
        return token_space(sizes, *args) if fits else feature_space(*args)

    return jax.shard_map(
        body,
        mesh=mesh,
        in_specs=(P("section", "dp", "tensor"),) * 4 + (P("section", None, "tensor"),) * 2,
        out_specs=(P("section", None, "tensor"),) * 4,
        check_vma=False,
    )
```

```python
import functools

import jax
import jax.numpy as jnp
from jax import lax
from jax.experimental import pallas as pl
from jax.experimental.pallas import tpu as pltpu
from jax.sharding import PartitionSpec as P

RANK = 64
POWER = 2
BLK = 128
THIN_ORDER = (2, 1, 0, 3)
WIDE_ORDER = (2, 3, 1, 0)

precise = lax.Precision.HIGHEST
f32 = jnp.float32
bf16 = jnp.bfloat16
VMEM = pl.BlockSpec(memory_space=pltpu.VMEM)
SMEM = pl.BlockSpec(memory_space=pltpu.SMEM)


def from_behind(value, axis, steps):
    count = lax.axis_size(axis)
    pairs = [(source, (source + steps) % count) for source in range(count)]
    return lax.ppermute(value, axis, pairs)


def gram_of(row_block):
    return jnp.dot(row_block, row_block.T, precision=precise, preferred_element_type=f32)


def solve_rows(gram_rows, row_block):
    low_factor = jnp.linalg.cholesky(gram_rows)
    solved = lax.linalg.triangular_solve(low_factor, row_block, left_side=True, lower=True)
    return solved.astype(bf16)


def tokens_of(sketches, matrices):
    parts = [
        jnp.einsum("km,tm->kt", s, m, preferred_element_type=f32)
        for s, m in zip(sketches, matrices)
    ]
    return tuple(lax.psum(p.astype(bf16), "tensor").astype(bf16) for p in parts)


def partials(token_rows, matrices):
    return tuple(
        jnp.dot(r, m, preferred_element_type=f32) for r, m in zip(token_rows, matrices)
    )


def orthonormal(parts):
    rows = [lax.psum(p.astype(bf16), "dp").astype(f32) for p in parts]
    grams = [lax.psum(gram_of(r).astype(bf16), "tensor").astype(f32) for r in rows]
    return tuple(solve_rows(g, r) for g, r in zip(grams, rows))


def feature_space(norm_in, query_grad, attn_out, handed, sketch_q, sketch_o):
    upstream = from_behind(handed, "section", -1)
    lefts = (norm_in[0], attn_out[0])
    rights = (query_grad[0], upstream[0])
    basis = orthonormal(partials(tokens_of((sketch_q[0], sketch_o[0]), rights), lefts))
    for _ in range(POWER):
        other = orthonormal(partials(tokens_of(basis, lefts), rights))
        basis = orthonormal(partials(tokens_of(other, rights), lefts))
    final = partials(tokens_of(basis, lefts), rights)
    raws = [lax.psum(p.astype(bf16), "dp").astype(f32) for p in final]
    energies = lax.psum(tuple(jnp.sum(r * r) for r in raws), "tensor")
    count = lax.axis_size("tensor")
    adapters = [
        r / jnp.sqrt(e / (r.size * count) + 1e-06) for r, e in zip(raws, energies)
    ]
    return (
        (basis[0] * 16.0)[None],
        adapters[0][None],
        (basis[1] * 16.0)[None],
        adapters[1][None],
    )


def swap(value, axis, bit):
    count = lax.axis_size(axis)
    return lax.ppermute(value, axis, [(i, i ^ bit) for i in range(count)])


def routed(value, sizes, token_bit, shifted):
    sections, dps, tensors = sizes
    side = tensors // 2
    pairs = []
    for s in range(sections):
        for z in range(dps):
            for t in range(tensors):
                to_t = t ^ side if t % side else t
                to_s = (s - 1) % sections if shifted and to_t >= side else s
                to = (to_s * dps + (z ^ token_bit)) * tensors + to_t
                pairs.append(((s * dps + z) * tensors + t, to))
    return lax.ppermute(value, ("section", "dp", "tensor"), pairs)


def window(ref, width, at):
    return ref.at[:, pl.ds(pl.multiple_of(at * width, width), width)]


def move(pairs, sems):
    copies = [pltpu.make_async_copy(src, dst, sems.at[n]) for n, (src, dst) in enumerate(pairs)]
    for c in copies:
        c.start()
    for c in copies:
        c.wait()


def give_kernel(dps, idx, norm, grad, attn, hand, sk_q, sk_o, give, sems):
    z, kind = idx[0], idx[3]
    wide, narrow = norm.shape[1], grad.shape[1]
    big_w, small_w = wide // dps, narrow // dps
    rows = RANK // dps

    def sketch(ref, width, start):
        part = ref.at[:, pl.ds(pl.multiple_of(z * width, width), width)]
        return [
            (
                part.at[i * rows : (i + 1) * rows],
                give.at[BLK:, i * (big_w + small_w) + start : i * (big_w + small_w) + start + width],
            )
            for i in range(dps)
        ]

    give[BLK:, :] = jnp.zeros((rows, wide + narrow), bf16)

    @pl.when(kind == 0)
    def _():
        pairs = [(hand, give.at[:BLK, :wide]), (attn, give.at[:BLK, wide:])]
        move(pairs + sketch(sk_o, big_w, 0), sems)

    @pl.when(kind == 1)
    def _():
        pairs = [(norm, give.at[:BLK, :wide]), (grad, give.at[:BLK, wide:])]
        move(pairs + sketch(sk_q, small_w, big_w), sems)


def merge_kernel(dps, kind, fill, pairs, sems):
    for which in (0, 1):

        @pl.when(kind == which)
        def _():
            copies = [
                pltpu.make_async_copy(src, dst, sems.at[n])
                for n, (src, dst) in enumerate(pairs[which])
            ]
            for c in copies:
                c.start()
            fill(which)
            for c in copies:
                c.wait()


def merge_thin_kernel(dps, idx, grad, attn, got, *refs):
    z, kind, smalls, sems = idx[0], idx[3], refs[:dps], refs[-1]
    small_w = smalls[0].shape[1] // 2
    wide = got.shape[1] - grad.shape[1]

    def fill(_):
        for d in range(dps):
            at = pl.multiple_of(wide + (z ^ d) * small_w, small_w)
            smalls[d][:, small_w:] = got[:BLK, pl.ds(at, small_w)]

    def keep(ref):
        return [
            (window(ref, small_w, z ^ d), smalls[d].at[:, :small_w]) for d in range(dps)
        ]

    merge_kernel(dps, kind, fill, (keep(grad), keep(attn)), sems)


def merge_wide_kernel(dps, idx, norm, hand, sk_q, sk_o, got, *refs):
    z, kind, bigs, sk, sems = idx[0], idx[3], refs[:dps], refs[dps], refs[-1]
    big_w, small_w = bigs[0].shape[1] // 2, sk.shape[1] // 2
    rows = RANK // dps

    def fill(which):
        for d in range(dps):
            at = pl.multiple_of((z ^ d) * big_w, big_w)
            bigs[d][:, big_w:] = got[:BLK, pl.ds(at, big_w)]
        for i in range(dps):
            at = i * (big_w + small_w)
            sk[RANK + i * rows : RANK + (i + 1) * rows, :] = got[BLK:, at : at + big_w]
            below = slice(2 * RANK + i * rows, 2 * RANK + (i + 1) * rows)
            sk[below, small_w:] = got[BLK:, at + big_w : at + big_w + small_w]
        if which == 0:
            sk[:RANK, :] = jnp.zeros((RANK, big_w), bf16)
        else:
            sk[2 * RANK :, :small_w] = jnp.zeros((RANK, small_w), bf16)

    def keep(ref, sketch):
        return [sketch] + [
            (window(ref, big_w, z ^ d), bigs[d].at[:, :big_w]) for d in range(dps)
        ]

    pairs = (
        keep(norm, (window(sk_q, small_w, z), sk.at[2 * RANK :, :small_w])),
        keep(hand, (window(sk_o, big_w, z), sk.at[:RANK, :])),
    )
    merge_kernel(dps, kind, fill, pairs, sems)


def nt(a, b, precision=None):
    return lax.dot_general(
        a, b, (((1,), (1,)), ((), ())), precision=precision, preferred_element_type=f32
    )


def packed_rows(dps):
    per_gram = (dps * (dps - 1) // 2 + dps // 2) * BLK
    thin = pl.cdiv(per_gram + 16, 32) * 32
    rest = per_gram + dps * RANK + 16
    wide = pl.cdiv(thin + rest, 64) * 64 - thin
    return per_gram, thin, wide


def pack_gram(m, flat, dps):
    r = lax.broadcasted_iota(jnp.int32, (BLK, BLK), 0)
    c = lax.broadcasted_iota(jnp.int32, (BLK, BLK), 1)
    at, on = 0, []
    for i in range(dps):
        row = nt(m[i * BLK : (i + 1) * BLK, :], m[: (i + 1) * BLK, :])
        for j in range(i):
            flat[at : at + BLK, :] = row[:, j * BLK : (j + 1) * BLK].astype(bf16)
            at += BLK
        on.append(row[:, i * BLK :])
    for i in range(0, dps, 2):
        flat[at : at + BLK, :] = jnp.where(r > c, on[i], on[i + 1]).astype(bf16)
        at += BLK
    diagonals = [jnp.sum(jnp.where(r == c, v, 0.0), axis=0, keepdims=True) for v in on]
    diagonals.append(jnp.zeros((16 - dps, BLK), f32))
    return at, jnp.concatenate(diagonals, axis=0).astype(bf16)


def hand_out(core, flat, keep, send):
    half = flat.shape[0] // 2
    keep[...] = flat[pl.ds(pl.multiple_of(core * half, 16), half), :]
    send[...] = flat[pl.ds(pl.multiple_of((1 - core) * half, 16), half), :]


def thin_gram_kernel(dps, idx, *refs):
    z, core = idx[0], idx[2]
    smalls, small, keep, send, flat = refs[:dps], *refs[dps:]
    for d, ref in zip(THIN_ORDER, smalls):
        small[pl.ds(pl.multiple_of((z ^ d) * BLK, BLK), BLK), :] = ref[...]
    at, diagonals = pack_gram(small, flat, dps)
    flat[at:, :] = jnp.zeros((flat.shape[0] - at, BLK), bf16)
    flat[at : at + 16, :] = diagonals
    hand_out(core, flat, keep, send)


def wide_gram_kernel(dps, idx, *refs):
    z, core = idx[0], idx[2]
    sk, bigs, small, big, keep, send, flat = refs[0], refs[1 : dps + 1], *refs[dps + 1 :]
    half_w = big.shape[1] // 2
    for d, ref in zip(WIDE_ORDER, bigs):
        big[pl.ds(pl.multiple_of((z ^ d) * BLK, BLK), BLK), :] = ref[...]
    at, diagonals = pack_gram(big, flat, dps)
    first = (
        nt(sk[:RANK, :], big[:, :half_w])
        + nt(sk[RANK : 2 * RANK, :], big[:, half_w:])
        + nt(sk[2 * RANK :, :], small[...])
    ).astype(bf16)
    for i in range(dps):
        flat[at : at + RANK, :] = first[:, i * BLK : (i + 1) * BLK]
        at += RANK
    flat[at:, :] = jnp.zeros((flat.shape[0] - at, BLK), bf16)
    flat[at : at + 16, :] = diagonals
    hand_out(core, flat, keep, send)


def add_halves_kernel(idx, thin_mine, thin_got, wide_mine, wide_got, keep, send, both):
    size, bit, split_at = keep.shape[0], idx[0] % 2, thin_mine.shape[0]
    both[:split_at, :] = (thin_mine[...].astype(f32) + thin_got[...].astype(f32)).astype(bf16)
    both[split_at:, :] = (wide_mine[...].astype(f32) + wide_got[...].astype(f32)).astype(bf16)
    for out, which in ((keep, bit), (send, 1 - bit)):
        out[...] = both[pl.ds(pl.multiple_of(which * size, 16), size), :]


def add_kernel(mine, got, out):
    out[...] = (mine[...].astype(f32) + got[...].astype(f32)).astype(bf16)


def inverse_factor(gram, spread):
    n, nb = gram.shape[0], 8
    rows = lax.broadcasted_iota(jnp.int32, (n, n), 0)
    cols = lax.broadcasted_iota(jnp.int32, (n, n), 1)
    work = jnp.concatenate([(rows == cols).astype(f32), gram], axis=1)
    count = n // nb
    slabs = [work[nb * s : nb * s + nb, :] for s in range(count)]
    sub = lax.broadcasted_iota(jnp.int32, (nb, 2 * n), 0)

    def lane(x, k):
        return jnp.broadcast_to(x[:, n + k : n + k + 1], (nb, 2 * n))

    def row(at):
        return jnp.broadcast_to(spread[at : at + 1, :], (nb, 2 * n))

    done = []
    for b in range(count):
        base = b * nb * (nb + 1)
        spread[base : base + nb, :] = slabs[b]
        for j in range(nb):
            at = base + nb * (j + 1)
            spread[at : at + nb, :] = lane(slabs[b], nb * b + j)
        pivot_rows = [row(base + i) for i in range(nb)]
        splat = [[row(base + nb * (j + 1) + i) for j in range(i + 1)] for i in range(nb)]
        below = {s: [lane(slabs[s], nb * b + j) for j in range(nb)] for s in range(b + 1, count)}
        out = None
        for k in range(nb):
            inv = 1.0 / splat[k][k]
            at = pivot_rows[k]
            final = at * lax.rsqrt(splat[k][k])
            out = final if out is None else jnp.where(sub == k, final, out)
            for i in range(k + 1, nb):
                mult = splat[i][k] * inv
                for j in range(k + 1, i + 1):
                    splat[i][j] = splat[i][j] - mult * splat[j][k]
                pivot_rows[i] = pivot_rows[i] - mult * at
            for s in range(b + 1, count):
                mult = below[s][k] * inv
                for j in range(k + 1, nb):
                    below[s][j] = below[s][j] - mult * splat[j][k]
                slabs[s] = slabs[s] - mult * at
        done.append(out)
    return jnp.concatenate(done, axis=0)[:, :n]


def split(x):
    high = x.astype(bf16)
    return high, (x - high.astype(f32)).astype(bf16)


def times(rows, gram):
    n = rows.shape[0]
    both = jnp.dot(jnp.concatenate(split(rows), axis=0), gram, preferred_element_type=f32)
    return both[:n] + both[n:]


def product(a, b):
    (ah, al), (bh, bl) = split(a), split(b)
    return jnp.dot(
        jnp.concatenate([ah, ah, al], axis=1),
        jnp.concatenate([bh, bl, bh], axis=0),
        preferred_element_type=f32,
    )


def product_nt(a, b):
    (ah, al), (bh, bl) = split(a), split(b)
    return nt(jnp.concatenate([ah, ah, al], axis=1), jnp.concatenate([bh, bl, bh], axis=1))


def chain_kernel(dps, counts, idx, *refs):
    z, out_half, core = idx[0], idx[1], idx[2]
    quarters, big, small, out, stays, leaves, flat, thin, wide, left, right, spread = (
        refs[:4],
        *refs[4:],
    )
    size, bit = quarters[0].shape[0], z % 2
    for n, ref in enumerate(quarters):
        which = 2 * (core ^ (n // 2)) + (bit ^ (n % 2))
        flat[pl.ds(pl.multiple_of(which * size, 16), size), :] = ref[...]
    per_gram, thin_rows, wide_rows = packed_rows(dps)
    for n in range(2):
        at, split_at = n * 2 * size, n * 2 * size + thin_rows // 2
        thin[n * (thin_rows // 2) : (n + 1) * (thin_rows // 2), :] = flat[at:split_at, :]
        wide[n * (wide_rows // 2) : (n + 1) * (wide_rows // 2), :] = flat[split_at : at + 2 * size, :]
    r = lax.broadcasted_iota(jnp.int32, (BLK, BLK), 0)
    c = lax.broadcasted_iota(jnp.int32, (BLK, BLK), 1)
    rows = jnp.concatenate(
        [wide[per_gram + i * RANK : per_gram + (i + 1) * RANK, :] for i in range(dps)], axis=1
    ).astype(f32)
    wide_diag = wide[per_gram + dps * RANK : per_gram + dps * RANK + 16, :].astype(f32)
    thin_diag = thin[per_gram : per_gram + 16, :].astype(f32)
    is_out = out_half == 1
    for gram, is_wide in ((left, out_half == 0), (right, is_out)):

        def block(n):
            part = slice(n * BLK, (n + 1) * BLK)
            return jnp.where(is_wide, wide[part, :].astype(f32), thin[part, :].astype(f32))

        def put(i, j, value):
            gram[i * BLK : (i + 1) * BLK, j * BLK : (j + 1) * BLK] = value.astype(bf16)

        n = 0
        for i in range(dps):
            for j in range(i):
                value = block(n)
                put(i, j, value)
                put(j, i, value.T)
                n += 1
        diag = jnp.where(is_wide, wide_diag, thin_diag)
        for i in range(0, dps, 2):
            value = block(n)
            turned = value.T
            put(i, i, jnp.where(r > c, value, jnp.where(r == c, diag[i : i + 1, :], turned)))
            put(
                i + 1,
                i + 1,
                jnp.where(r < c, value, jnp.where(r == c, diag[i + 1 : i + 2, :], turned)),
            )
            n += 1
    ahead = times(rows, left[...])
    gram = product_nt(ahead, rows)
    for step in range(2 * POWER):
        following = (right if step % 2 == 0 else left)[...]
        beyond = times(ahead, following)
        inner = product_nt(beyond, ahead)
        low_inv = inverse_factor(gram, spread)
        rows = product(low_inv, ahead)
        if step < 2 * POWER - 1:
            gram = product_nt(product(low_inv, inner), low_inv)
            ahead = product(low_inv, beyond)
        else:
            ahead = times(rows, following)
            gram = product_nt(ahead, rows)
    low_inv = inverse_factor(gram, spread)
    basis = product(low_inv, rows)
    rows = product(low_inv, ahead)
    energy = jnp.sum(times(rows, right[...]) * rows)
    count = jnp.where(out_half == 1, counts[0], counts[1]).astype(f32)
    scale = lax.rsqrt(jnp.full((1, 1), energy, f32) / count + 1e-06)
    coef_b, coef_a = basis.astype(bf16), rows.astype(bf16)
    for_big = jnp.where(is_out, coef_a, coef_b)
    for_small = jnp.where(is_out, coef_b, coef_a)
    scale_big = jnp.where(is_out, scale, 16.0)
    scale_small = jnp.where(is_out, 16.0, scale)
    big_w, small_w = big.shape[1] // 2, small.shape[1] // 2
    made_big = (jnp.dot(for_big, big[...], preferred_element_type=f32) * scale_big).astype(bf16)
    made_small = (jnp.dot(for_small, small[...], preferred_element_type=f32) * scale_small).astype(
        bf16
    )
    for n, half in enumerate((stays, leaves)):
        half[:, :big_w] = made_big[:, n * big_w : (n + 1) * big_w]
        half[:, big_w:] = made_small[:, n * small_w : (n + 1) * small_w]
        out[n * RANK : (n + 1) * RANK, :] = half[...]


def place_kernel(dps, idx, *refs):
    z, kind = idx[0], idx[3]
    mine, theirs = refs[:dps], refs[dps : 2 * dps]
    b_q, a_q, b_o, a_o = refs[2 * dps :]
    big_w, small_w = b_q.shape[1] // dps, a_q.shape[1] // dps
    for d in range(dps):
        bigs = pl.ds(pl.multiple_of((z ^ d) * big_w, big_w), big_w)
        smalls = pl.ds(pl.multiple_of((z ^ d) * small_w, small_w), small_w)
        here, there = mine[d].at[:RANK], theirs[d].at[theirs[d].shape[0] - RANK :]
        for which, query, output in ((0, here, there), (1, there, here)):

            @pl.when(kind == which)
            def _():
                b_q[:, bigs] = query[:, :big_w]
                a_q[:, smalls] = query[:, big_w:].astype(f32)
                a_o[:, bigs] = output[:, :big_w].astype(f32)
                b_o[:, smalls] = output[:, big_w:]


def call(kernel, out_shapes, args, scratch=(), spaces=()):
    spaces = [SMEM] + [VMEM] * (len(args) - 1) if not spaces else spaces
    return pl.pallas_call(
        kernel,
        out_shape=out_shapes,
        in_specs=spaces,
        out_specs=jax.tree.map(lambda _: VMEM, out_shapes),
        scratch_shapes=list(scratch),
        compiler_params=pltpu.CompilerParams(vmem_limit_bytes=48 * 2**20),
    )(*args)


def token_space(sizes, norm_in, query_grad, attn_out, handed, sketch_q, sketch_o):
    _, dps, tensors = sizes
    side = tensors // 2

    def shape(*dims, dtype=bf16):
        return jax.ShapeDtypeStruct(dims, dtype)

    z, t = lax.axis_index("dp"), lax.axis_index("tensor")
    half, core = t // side, t % side
    idx = jnp.stack([z, half, core, half ^ core]).astype(jnp.int32)
    wide, narrow = norm_in.shape[2], query_grad.shape[2]
    big_w, small_w = wide // dps, narrow // dps
    tokens = dps * BLK
    hbm = pl.BlockSpec(memory_space=pltpu.HBM)
    norm, grad, attn, hand, sk_q, sk_o = (
        pltpu.with_memory_space_constraint(v[0], pltpu.HBM)
        for v in (norm_in, query_grad, attn_out, handed, sketch_q, sketch_o)
    )

    give = call(
        functools.partial(give_kernel, dps),
        shape(BLK + RANK // dps, wide + narrow),
        (idx, norm, grad, attn, hand, sk_q, sk_o),
        [pltpu.SemaphoreType.DMA((2 + dps,))],
        [SMEM] + [hbm] * 6,
    )
    got = swap(give, "tensor", 1)
    smalls = call(
        functools.partial(merge_thin_kernel, dps),
        [shape(BLK, 2 * small_w)] * dps,
        (idx, grad, attn, got),
        [pltpu.SemaphoreType.DMA((dps,))],
        [SMEM, hbm, hbm, VMEM],
    )
    packed = call(
        functools.partial(merge_wide_kernel, dps),
        [shape(BLK, 2 * big_w)] * dps + [shape(3 * RANK, 2 * small_w)],
        (idx, norm, hand, sk_q, sk_o, got),
        [pltpu.SemaphoreType.DMA((dps + 1,))],
        [SMEM, hbm, hbm, hbm, hbm, VMEM],
    )
    smalls = [routed(smalls[d], sizes, d, False) for d in THIN_ORDER]
    sketch = routed(packed[dps], sizes, 0, False)
    bigs = [routed(packed[d], sizes, d, True) for d in WIDE_ORDER]

    _, thin_rows, wide_rows = packed_rows(dps)

    def gram(kernel, m, rows, operands):
        m, keep, send = call(
            functools.partial(kernel, dps),
            [m, shape(rows // 2, BLK), shape(rows // 2, BLK)],
            (idx, *operands),
            [pltpu.VMEM((rows, BLK), bf16)],
        )
        return m, keep, swap(send, "tensor", 1)

    small, *thin = gram(thin_gram_kernel, shape(tokens, 2 * small_w), thin_rows, smalls)
    big, *rest = gram(
        wide_gram_kernel, shape(tokens, 2 * big_w), wide_rows, (sketch, *bigs, small)
    )
    total = thin_rows + wide_rows
    quarter = shape(total // 4, BLK)
    keep, send = call(
        add_halves_kernel,
        [quarter] * 2,
        (idx, *thin, *rest),
        [pltpu.VMEM((total // 2, BLK), bf16)],
    )
    for bit, value in ((1, send), (2, None)):
        value = swap(keep if value is None else value, "dp", bit)
        keep = call(add_kernel, quarter, (keep, value), (), [VMEM] * 2)
    beside = swap(keep, "dp", 1)
    quarters = (keep, beside, swap(keep, "tensor", 1), swap(beside, "tensor", 1))

    counts = (RANK * wide * tensors, RANK * narrow * tensors)
    whole, stays, leaves = call(
        functools.partial(chain_kernel, dps, counts),
        [shape(2 * RANK, big_w + small_w)] + [shape(RANK, big_w + small_w)] * 2,
        (idx, *quarters, big, small),
        [
            pltpu.VMEM((total, BLK), bf16),
            pltpu.VMEM((thin_rows, BLK), bf16),
            pltpu.VMEM((wide_rows, BLK), bf16),
            pltpu.VMEM((tokens, tokens), bf16),
            pltpu.VMEM((tokens, tokens), bf16),
            pltpu.VMEM((9 * RANK, 2 * RANK), f32),
        ],
    )
    leaves, stays = routed(leaves, sizes, 2, False), routed(stays, sizes, 2, False)
    near, here = routed(whole, sizes, 1, False), routed(whole, sizes, 0, False)
    leaves_on, stays_on = swap(leaves, "dp", 1), swap(stays, "dp", 1)
    here, near, stays = lax.optimization_barrier((here, near, stays))
    leaves_on, stays_on = lax.optimization_barrier((leaves_on, stays_on))
    mine = (here, near, stays, stays_on)
    theirs = [swap(v, "tensor", 1) for v in (here, near, leaves, leaves_on)]
    outs = call(
        functools.partial(place_kernel, dps),
        [
            shape(RANK, wide),
            shape(RANK, narrow, dtype=f32),
            shape(RANK, narrow),
            shape(RANK, wide, dtype=f32),
        ],
        (idx, *mine, *theirs),
    )
    return tuple(o[None] for o in outs)


def solution(mesh):
    sizes = tuple(mesh.shape[axis] for axis in ("section", "dp", "tensor"))
    _, dps, tensors = sizes

    def body(norm_in, query_grad, attn_out, handed, sketch_q, sketch_o):
        args = (norm_in, query_grad, attn_out, handed, sketch_q, sketch_o)
        fits = (
            dps == 4
            and tensors == 4
            and norm_in.shape[1] == BLK
            and sketch_q.shape[1] == RANK
            and norm_in.shape[2] == handed.shape[2]
            and query_grad.shape[2] == attn_out.shape[2]
            and norm_in.shape[2] == 2 * query_grad.shape[2]
            and query_grad.shape[2] % (dps * 128) == 0
        )
        return token_space(sizes, *args) if fits else feature_space(*args)

    return jax.shard_map(
        body,
        mesh=mesh,
        in_specs=(P("section", "dp", "tensor"),) * 4 + (P("section", None, "tensor"),) * 2,
        out_specs=(P("section", None, "tensor"),) * 4,
        check_vma=False,
    )
```

```python
import functools

import jax
import jax.numpy as jnp
from jax import lax
from jax.experimental import pallas as pl
from jax.experimental.pallas import tpu as pltpu
from jax.sharding import PartitionSpec as P

RANK = 64
POWER = 2
BLK = 128
THIN_ORDER = (2, 1, 0, 3)
WIDE_ORDER = (2, 3, 1, 0)

precise = lax.Precision.HIGHEST
f32 = jnp.float32
bf16 = jnp.bfloat16
VMEM = pl.BlockSpec(memory_space=pltpu.VMEM)
SMEM = pl.BlockSpec(memory_space=pltpu.SMEM)


def from_behind(value, axis, steps):
    count = lax.axis_size(axis)
    pairs = [(source, (source + steps) % count) for source in range(count)]
    return lax.ppermute(value, axis, pairs)


def gram_of(row_block):
    return jnp.dot(row_block, row_block.T, precision=precise, preferred_element_type=f32)


def solve_rows(gram_rows, row_block):
    low_factor = jnp.linalg.cholesky(gram_rows)
    solved = lax.linalg.triangular_solve(low_factor, row_block, left_side=True, lower=True)
    return solved.astype(bf16)


def tokens_of(sketches, matrices):
    parts = [
        jnp.einsum("km,tm->kt", s, m, preferred_element_type=f32)
        for s, m in zip(sketches, matrices)
    ]
    return tuple(lax.psum(p.astype(bf16), "tensor").astype(bf16) for p in parts)


def partials(token_rows, matrices):
    return tuple(
        jnp.dot(r, m, preferred_element_type=f32) for r, m in zip(token_rows, matrices)
    )


def orthonormal(parts):
    rows = [lax.psum(p.astype(bf16), "dp").astype(f32) for p in parts]
    grams = [lax.psum(gram_of(r).astype(bf16), "tensor").astype(f32) for r in rows]
    return tuple(solve_rows(g, r) for g, r in zip(grams, rows))


def feature_space(norm_in, query_grad, attn_out, handed, sketch_q, sketch_o):
    upstream = from_behind(handed, "section", -1)
    lefts = (norm_in[0], attn_out[0])
    rights = (query_grad[0], upstream[0])
    basis = orthonormal(partials(tokens_of((sketch_q[0], sketch_o[0]), rights), lefts))
    for _ in range(POWER):
        other = orthonormal(partials(tokens_of(basis, lefts), rights))
        basis = orthonormal(partials(tokens_of(other, rights), lefts))
    final = partials(tokens_of(basis, lefts), rights)
    raws = [lax.psum(p.astype(bf16), "dp").astype(f32) for p in final]
    energies = lax.psum(tuple(jnp.sum(r * r) for r in raws), "tensor")
    count = lax.axis_size("tensor")
    adapters = [
        r / jnp.sqrt(e / (r.size * count) + 1e-06) for r, e in zip(raws, energies)
    ]
    return (
        (basis[0] * 16.0)[None],
        adapters[0][None],
        (basis[1] * 16.0)[None],
        adapters[1][None],
    )


def swap(value, axis, bit):
    count = lax.axis_size(axis)
    return lax.ppermute(value, axis, [(i, i ^ bit) for i in range(count)])


def routed(value, sizes, token_bit, shifted):
    sections, dps, tensors = sizes
    side = tensors // 2
    pairs = []
    for s in range(sections):
        for z in range(dps):
            for t in range(tensors):
                to_t = t ^ side if t % side else t
                to_s = (s - 1) % sections if shifted and to_t >= side else s
                to = (to_s * dps + (z ^ token_bit)) * tensors + to_t
                pairs.append(((s * dps + z) * tensors + t, to))
    return lax.ppermute(value, ("section", "dp", "tensor"), pairs)


def window(ref, width, at):
    return ref.at[:, pl.ds(pl.multiple_of(at * width, width), width)]


def move(pairs, sems):
    copies = [pltpu.make_async_copy(src, dst, sems.at[n]) for n, (src, dst) in enumerate(pairs)]
    for c in copies:
        c.start()
    for c in copies:
        c.wait()


def give_wide_kernel(dps, idx, norm, hand, sk_q, sk_o, give, sems):
    z, kind = idx[0], idx[3]
    rows, fold = RANK // dps, give.shape[1] // dps
    small_w = sk_q.shape[1] // dps

    def sketch(ref, width):
        part = ref.at[:, pl.ds(pl.multiple_of(z * width, width), width)]
        return [
            (part.at[i * rows : (i + 1) * rows], give.at[BLK:, i * fold : i * fold + width])
            for i in range(dps)
        ]

    @pl.when(kind == 0)
    def _():
        move([(hand, give.at[:BLK])] + sketch(sk_o, fold), sems)

    @pl.when(kind == 1)
    def _():
        give[BLK:, :] = jnp.zeros((rows, give.shape[1]), bf16)
        move([(norm, give.at[:BLK])] + sketch(sk_q, small_w), sems)


def merge_kernel(dps, kind, fill, pairs, sems):
    for which in (0, 1):

        @pl.when(kind == which)
        def _():
            copies = [
                pltpu.make_async_copy(src, dst, sems.at[n])
                for n, (src, dst) in enumerate(pairs[which])
            ]
            for c in copies:
                c.start()
            fill(which)
            for c in copies:
                c.wait()


def merge_thin_kernel(dps, idx, grad, attn, got_grad, got_attn, *smalls):
    z, kind = idx[0], idx[3]
    small_w = smalls[0].shape[1] // 2
    for which, keep, got in ((0, grad, got_grad), (1, attn, got_attn)):

        @pl.when(kind == which)
        def _():
            for d in range(dps):
                part = pl.ds(pl.multiple_of((z ^ d) * small_w, small_w), small_w)
                smalls[d][:, :small_w] = keep[:, part]
                smalls[d][:, small_w:] = got[:, part]


def merge_wide_kernel(dps, idx, norm, hand, sk_q, sk_o, got, *refs):
    z, kind, bigs, sk, sems = idx[0], idx[3], refs[:dps], refs[dps], refs[-1]
    big_w, small_w = bigs[0].shape[1] // 2, sk.shape[1] // 2
    rows = RANK // dps

    def fill(which):
        for d in range(dps):
            at = pl.multiple_of((z ^ d) * big_w, big_w)
            bigs[d][:, big_w:] = got[:BLK, pl.ds(at, big_w)]
        for i in range(dps):
            part = got[BLK:, i * big_w : (i + 1) * big_w]
            one, two = RANK + i * rows, 2 * RANK + i * rows
            if which == 0:
                sk[one : one + rows, :] = jnp.zeros_like(part)
                sk[two : two + rows, small_w:] = part[:, :small_w]
            else:
                sk[one : one + rows, :] = part
                sk[two : two + rows, small_w:] = jnp.zeros_like(part[:, :small_w])
        if which == 0:
            sk[:RANK, :] = jnp.zeros((RANK, big_w), bf16)
        else:
            sk[2 * RANK :, :small_w] = jnp.zeros((RANK, small_w), bf16)

    def keep(ref, sketch):
        return [sketch] + [
            (window(ref, big_w, z ^ d), bigs[d].at[:, :big_w]) for d in range(dps)
        ]

    pairs = (
        keep(norm, (window(sk_q, small_w, z), sk.at[2 * RANK :, :small_w])),
        keep(hand, (window(sk_o, big_w, z), sk.at[:RANK, :])),
    )
    merge_kernel(dps, kind, fill, pairs, sems)


def nt(a, b, precision=None):
    return lax.dot_general(
        a, b, (((1,), (1,)), ((), ())), precision=precision, preferred_element_type=f32
    )


def packed_rows(dps):
    per_gram = (dps * (dps - 1) // 2 + dps // 2) * BLK
    thin = pl.cdiv(per_gram + 16, 32) * 32
    rest = per_gram + dps * RANK + 16
    wide = pl.cdiv(thin + rest, 64) * 64 - thin
    return per_gram, thin, wide


def pack_gram(m, flat, dps):
    r = lax.broadcasted_iota(jnp.int32, (BLK, BLK), 0)
    c = lax.broadcasted_iota(jnp.int32, (BLK, BLK), 1)
    at, on = 0, []
    for i in range(dps):
        row = nt(m[i * BLK : (i + 1) * BLK, :], m[: (i + 1) * BLK, :])
        for j in range(i):
            flat[at : at + BLK, :] = row[:, j * BLK : (j + 1) * BLK].astype(bf16)
            at += BLK
        on.append(row[:, i * BLK :])
    for i in range(0, dps, 2):
        flat[at : at + BLK, :] = jnp.where(r > c, on[i], on[i + 1]).astype(bf16)
        at += BLK
    diagonals = [jnp.sum(jnp.where(r == c, v, 0.0), axis=0, keepdims=True) for v in on]
    diagonals.append(jnp.zeros((16 - dps, BLK), f32))
    return at, jnp.concatenate(diagonals, axis=0).astype(bf16)


def hand_out(core, flat, keep, send):
    half = flat.shape[0] // 2
    keep[...] = flat[pl.ds(pl.multiple_of(core * half, 16), half), :]
    send[...] = flat[pl.ds(pl.multiple_of((1 - core) * half, 16), half), :]


def thin_gram_kernel(dps, idx, *refs):
    z, core = idx[0], idx[2]
    smalls, small, keep, send, flat = refs[:dps], *refs[dps:]
    for d, ref in zip(THIN_ORDER, smalls):
        small[pl.ds(pl.multiple_of((z ^ d) * BLK, BLK), BLK), :] = ref[...]
    at, diagonals = pack_gram(small, flat, dps)
    flat[at:, :] = jnp.zeros((flat.shape[0] - at, BLK), bf16)
    flat[at : at + 16, :] = diagonals
    hand_out(core, flat, keep, send)


def wide_gram_kernel(dps, idx, *refs):
    z, core = idx[0], idx[2]
    sk, bigs, small, big, keep, send, flat = refs[0], refs[1 : dps + 1], *refs[dps + 1 :]
    half_w = big.shape[1] // 2
    for d, ref in zip(WIDE_ORDER, bigs):
        big[pl.ds(pl.multiple_of((z ^ d) * BLK, BLK), BLK), :] = ref[...]
    at, diagonals = pack_gram(big, flat, dps)
    first = (
        nt(sk[:RANK, :], big[:, :half_w])
        + nt(sk[RANK : 2 * RANK, :], big[:, half_w:])
        + nt(sk[2 * RANK :, :], small[...])
    ).astype(bf16)
    for i in range(dps):
        flat[at : at + RANK, :] = first[:, i * BLK : (i + 1) * BLK]
        at += RANK
    flat[at:, :] = jnp.zeros((flat.shape[0] - at, BLK), bf16)
    flat[at : at + 16, :] = diagonals
    hand_out(core, flat, keep, send)


def add_halves_kernel(idx, thin_mine, thin_got, wide_mine, wide_got, keep, send, both):
    size, bit, split_at = keep.shape[0], idx[0] % 2, thin_mine.shape[0]
    both[:split_at, :] = (thin_mine[...].astype(f32) + thin_got[...].astype(f32)).astype(bf16)
    both[split_at:, :] = (wide_mine[...].astype(f32) + wide_got[...].astype(f32)).astype(bf16)
    for out, which in ((keep, bit), (send, 1 - bit)):
        out[...] = both[pl.ds(pl.multiple_of(which * size, 16), size), :]


def add_kernel(mine, got, out):
    out[...] = (mine[...].astype(f32) + got[...].astype(f32)).astype(bf16)


def inverse_factor(gram, spread):
    n, nb = gram.shape[0], 8
    rows = lax.broadcasted_iota(jnp.int32, (n, n), 0)
    cols = lax.broadcasted_iota(jnp.int32, (n, n), 1)
    work = jnp.concatenate([(rows == cols).astype(f32), gram], axis=1)
    count = n // nb
    slabs = [work[nb * s : nb * s + nb, :] for s in range(count)]
    sub = lax.broadcasted_iota(jnp.int32, (nb, 2 * n), 0)

    def lane(x, k):
        return jnp.broadcast_to(x[:, n + k : n + k + 1], (nb, 2 * n))

    def row(at):
        return jnp.broadcast_to(spread[at : at + 1, :], (nb, 2 * n))

    done = []
    for b in range(count):
        base = b * nb * (nb + 1)
        spread[base : base + nb, :] = slabs[b]
        for j in range(nb):
            at = base + nb * (j + 1)
            spread[at : at + nb, :] = lane(slabs[b], nb * b + j)
        pivot_rows = [row(base + i) for i in range(nb)]
        splat = [[row(base + nb * (j + 1) + i) for j in range(i + 1)] for i in range(nb)]
        below = {s: [lane(slabs[s], nb * b + j) for j in range(nb)] for s in range(b + 1, count)}
        out = None
        for k in range(nb):
            inv = 1.0 / splat[k][k]
            at = pivot_rows[k]
            final = at * lax.rsqrt(splat[k][k])
            out = final if out is None else jnp.where(sub == k, final, out)
            for i in range(k + 1, nb):
                mult = splat[i][k] * inv
                for j in range(k + 1, i + 1):
                    splat[i][j] = splat[i][j] - mult * splat[j][k]
                pivot_rows[i] = pivot_rows[i] - mult * at
            for s in range(b + 1, count):
                mult = below[s][k] * inv
                for j in range(k + 1, nb):
                    below[s][j] = below[s][j] - mult * splat[j][k]
                slabs[s] = slabs[s] - mult * at
        done.append(out)
    return jnp.concatenate(done, axis=0)[:, :n]


def split(x):
    high = x.astype(bf16)
    return high, (x - high.astype(f32)).astype(bf16)


def times(rows, gram):
    n = rows.shape[0]
    both = jnp.dot(jnp.concatenate(split(rows), axis=0), gram, preferred_element_type=f32)
    return both[:n] + both[n:]


def product(a, b):
    (ah, al), (bh, bl) = split(a), split(b)
    return jnp.dot(
        jnp.concatenate([ah, ah, al], axis=1),
        jnp.concatenate([bh, bl, bh], axis=0),
        preferred_element_type=f32,
    )


def product_nt(a, b):
    (ah, al), (bh, bl) = split(a), split(b)
    return nt(jnp.concatenate([ah, ah, al], axis=1), jnp.concatenate([bh, bl, bh], axis=1))


def chain_kernel(dps, counts, idx, *refs):
    z, out_half, core = idx[0], idx[1], idx[2]
    quarters, big, small, out, stays, leaves, flat, thin, wide, left, right, spread = (
        refs[:4],
        *refs[4:],
    )
    size, bit = quarters[0].shape[0], z % 2
    for n, ref in enumerate(quarters):
        which = 2 * (core ^ (n // 2)) + (bit ^ (n % 2))
        flat[pl.ds(pl.multiple_of(which * size, 16), size), :] = ref[...]
    per_gram, thin_rows, wide_rows = packed_rows(dps)
    for n in range(2):
        at, split_at = n * 2 * size, n * 2 * size + thin_rows // 2
        thin[n * (thin_rows // 2) : (n + 1) * (thin_rows // 2), :] = flat[at:split_at, :]
        wide[n * (wide_rows // 2) : (n + 1) * (wide_rows // 2), :] = flat[split_at : at + 2 * size, :]
    r = lax.broadcasted_iota(jnp.int32, (BLK, BLK), 0)
    c = lax.broadcasted_iota(jnp.int32, (BLK, BLK), 1)
    rows = jnp.concatenate(
        [wide[per_gram + i * RANK : per_gram + (i + 1) * RANK, :] for i in range(dps)], axis=1
    ).astype(f32)
    wide_diag = wide[per_gram + dps * RANK : per_gram + dps * RANK + 16, :].astype(f32)
    thin_diag = thin[per_gram : per_gram + 16, :].astype(f32)
    is_out = out_half == 1
    for gram, is_wide in ((left, out_half == 0), (right, is_out)):

        def block(n):
            part = slice(n * BLK, (n + 1) * BLK)
            return jnp.where(is_wide, wide[part, :].astype(f32), thin[part, :].astype(f32))

        def put(i, j, value):
            gram[i * BLK : (i + 1) * BLK, j * BLK : (j + 1) * BLK] = value.astype(bf16)

        n = 0
        for i in range(dps):
            for j in range(i):
                value = block(n)
                put(i, j, value)
                put(j, i, value.T)
                n += 1
        diag = jnp.where(is_wide, wide_diag, thin_diag)
        for i in range(0, dps, 2):
            value = block(n)
            turned = value.T
            put(i, i, jnp.where(r > c, value, jnp.where(r == c, diag[i : i + 1, :], turned)))
            put(
                i + 1,
                i + 1,
                jnp.where(r < c, value, jnp.where(r == c, diag[i + 1 : i + 2, :], turned)),
            )
            n += 1
    ahead = times(rows, left[...])
    gram = product_nt(ahead, rows)
    for step in range(2 * POWER):
        following = (right if step % 2 == 0 else left)[...]
        beyond = times(ahead, following)
        inner = product_nt(beyond, ahead)
        low_inv = inverse_factor(gram, spread)
        rows = product(low_inv, ahead)
        if step < 2 * POWER - 1:
            gram = product_nt(product(low_inv, inner), low_inv)
            ahead = product(low_inv, beyond)
        else:
            ahead = times(rows, following)
            gram = product_nt(ahead, rows)
    low_inv = inverse_factor(gram, spread)
    basis = product(low_inv, rows)
    rows = product(low_inv, ahead)
    energy = jnp.sum(times(rows, right[...]) * rows)
    count = jnp.where(out_half == 1, counts[0], counts[1]).astype(f32)
    scale = lax.rsqrt(jnp.full((1, 1), energy, f32) / count + 1e-06)
    coef_b, coef_a = basis.astype(bf16), rows.astype(bf16)
    for_big = jnp.where(is_out, coef_a, coef_b)
    for_small = jnp.where(is_out, coef_b, coef_a)
    scale_big = jnp.where(is_out, scale, 16.0)
    scale_small = jnp.where(is_out, 16.0, scale)
    big_w, small_w = big.shape[1] // 2, small.shape[1] // 2
    made_big = (jnp.dot(for_big, big[...], preferred_element_type=f32) * scale_big).astype(bf16)
    made_small = (jnp.dot(for_small, small[...], preferred_element_type=f32) * scale_small).astype(
        bf16
    )
    for n, half in enumerate((stays, leaves)):
        half[:, :big_w] = made_big[:, n * big_w : (n + 1) * big_w]
        half[:, big_w:] = made_small[:, n * small_w : (n + 1) * small_w]
        out[n * RANK : (n + 1) * RANK, :] = half[...]


def place_kernel(dps, idx, *refs):
    z, kind = idx[0], idx[3]
    mine, theirs = refs[:dps], refs[dps : 2 * dps]
    b_q, a_q, b_o, a_o = refs[2 * dps :]
    big_w, small_w = b_q.shape[1] // dps, a_q.shape[1] // dps
    for d in range(dps):
        bigs = pl.ds(pl.multiple_of((z ^ d) * big_w, big_w), big_w)
        smalls = pl.ds(pl.multiple_of((z ^ d) * small_w, small_w), small_w)
        here, there = mine[d].at[:RANK], theirs[d].at[theirs[d].shape[0] - RANK :]
        for which, query, output in ((0, here, there), (1, there, here)):

            @pl.when(kind == which)
            def _():
                b_q[:, bigs] = query[:, :big_w]
                a_q[:, smalls] = query[:, big_w:].astype(f32)
                a_o[:, bigs] = output[:, :big_w].astype(f32)
                b_o[:, smalls] = output[:, big_w:]


def call(kernel, out_shapes, args, scratch=(), spaces=()):
    spaces = [SMEM] + [VMEM] * (len(args) - 1) if not spaces else spaces
    return pl.pallas_call(
        kernel,
        out_shape=out_shapes,
        in_specs=spaces,
        out_specs=jax.tree.map(lambda _: VMEM, out_shapes),
        scratch_shapes=list(scratch),
        compiler_params=pltpu.CompilerParams(vmem_limit_bytes=48 * 2**20),
    )(*args)


def token_space(sizes, norm_in, query_grad, attn_out, handed, sketch_q, sketch_o):
    _, dps, tensors = sizes
    side = tensors // 2

    def shape(*dims, dtype=bf16):
        return jax.ShapeDtypeStruct(dims, dtype)

    z, t = lax.axis_index("dp"), lax.axis_index("tensor")
    half, core = t // side, t % side
    idx = jnp.stack([z, half, core, half ^ core]).astype(jnp.int32)
    wide, narrow = norm_in.shape[2], query_grad.shape[2]
    big_w, small_w = wide // dps, narrow // dps
    tokens = dps * BLK
    hbm = pl.BlockSpec(memory_space=pltpu.HBM)
    norm, hand, sk_q, sk_o = (
        pltpu.with_memory_space_constraint(v[0], pltpu.HBM)
        for v in (norm_in, handed, sketch_q, sketch_o)
    )

    got_grad, got_attn = swap(query_grad[0], "tensor", 1), swap(attn_out[0], "tensor", 1)
    give = call(
        functools.partial(give_wide_kernel, dps),
        shape(BLK + RANK // dps, wide),
        (idx, norm, hand, sk_q, sk_o),
        [pltpu.SemaphoreType.DMA((1 + dps,))],
        [SMEM] + [hbm] * 4,
    )
    give, got_grad, got_attn = lax.optimization_barrier((give, got_grad, got_attn))
    smalls = call(
        functools.partial(merge_thin_kernel, dps),
        [shape(BLK, 2 * small_w)] * dps,
        (idx, query_grad[0], attn_out[0], got_grad, got_attn),
    )
    smalls = list(smalls)
    got = swap(give, "tensor", 1)
    packed = call(
        functools.partial(merge_wide_kernel, dps),
        [shape(BLK, 2 * big_w)] * dps + [shape(3 * RANK, 2 * small_w)],
        (idx, norm, hand, sk_q, sk_o, got),
        [pltpu.SemaphoreType.DMA((dps + 1,))],
        [SMEM, hbm, hbm, hbm, hbm, VMEM],
    )
    smalls = [routed(smalls[d], sizes, d, False) for d in THIN_ORDER]
    sketch = routed(packed[dps], sizes, 0, False)
    bigs = [routed(packed[d], sizes, d, True) for d in WIDE_ORDER]

    _, thin_rows, wide_rows = packed_rows(dps)

    def gram(kernel, m, rows, operands):
        m, keep, send = call(
            functools.partial(kernel, dps),
            [m, shape(rows // 2, BLK), shape(rows // 2, BLK)],
            (idx, *operands),
            [pltpu.VMEM((rows, BLK), bf16)],
        )
        return m, keep, swap(send, "tensor", 1)

    small, *thin = gram(thin_gram_kernel, shape(tokens, 2 * small_w), thin_rows, smalls)
    big, *rest = gram(
        wide_gram_kernel, shape(tokens, 2 * big_w), wide_rows, (sketch, *bigs, small)
    )
    total = thin_rows + wide_rows
    quarter = shape(total // 4, BLK)
    keep, send = call(
        add_halves_kernel,
        [quarter] * 2,
        (idx, *thin, *rest),
        [pltpu.VMEM((total // 2, BLK), bf16)],
    )
    for bit, value in ((1, send), (2, None)):
        value = swap(keep if value is None else value, "dp", bit)
        keep = call(add_kernel, quarter, (keep, value), (), [VMEM] * 2)
    beside = swap(keep, "dp", 1)
    quarters = (keep, beside, swap(keep, "tensor", 1), swap(beside, "tensor", 1))

    counts = (RANK * wide * tensors, RANK * narrow * tensors)
    whole, stays, leaves = call(
        functools.partial(chain_kernel, dps, counts),
        [shape(2 * RANK, big_w + small_w)] + [shape(RANK, big_w + small_w)] * 2,
        (idx, *quarters, big, small),
        [
            pltpu.VMEM((total, BLK), bf16),
            pltpu.VMEM((thin_rows, BLK), bf16),
            pltpu.VMEM((wide_rows, BLK), bf16),
            pltpu.VMEM((tokens, tokens), bf16),
            pltpu.VMEM((tokens, tokens), bf16),
            pltpu.VMEM((9 * RANK, 2 * RANK), f32),
        ],
    )
    leaves, stays = routed(leaves, sizes, 2, False), routed(stays, sizes, 2, False)
    near, here = routed(whole, sizes, 1, False), routed(whole, sizes, 0, False)
    leaves_on, stays_on = swap(leaves, "dp", 1), swap(stays, "dp", 1)
    mine = (here, near, stays, stays_on)
    theirs = [swap(v, "tensor", 1) for v in (here, near, leaves, leaves_on)]
    outs = call(
        functools.partial(place_kernel, dps),
        [
            shape(RANK, wide),
            shape(RANK, narrow, dtype=f32),
            shape(RANK, narrow),
            shape(RANK, wide, dtype=f32),
        ],
        (idx, *mine, *theirs),
    )
    return tuple(o[None] for o in outs)


def solution(mesh):
    sizes = tuple(mesh.shape[axis] for axis in ("section", "dp", "tensor"))
    _, dps, tensors = sizes

    def body(norm_in, query_grad, attn_out, handed, sketch_q, sketch_o):
        args = (norm_in, query_grad, attn_out, handed, sketch_q, sketch_o)
        fits = (
            dps == 4
            and tensors == 4
            and norm_in.shape[1] == BLK
            and sketch_q.shape[1] == RANK
            and norm_in.shape[2] == handed.shape[2]
            and query_grad.shape[2] == attn_out.shape[2]
            and norm_in.shape[2] == 2 * query_grad.shape[2]
            and query_grad.shape[2] % (dps * 128) == 0
        )
        return token_space(sizes, *args) if fits else feature_space(*args)

    return jax.shard_map(
        body,
        mesh=mesh,
        in_specs=(P("section", "dp", "tensor"),) * 4 + (P("section", None, "tensor"),) * 2,
        out_specs=(P("section", None, "tensor"),) * 4,
        check_vma=False,
    )
```

```python
import functools

import jax
import jax.numpy as jnp
from jax import lax
from jax.experimental import pallas as pl
from jax.experimental.pallas import tpu as pltpu
from jax.sharding import PartitionSpec as P

RANK = 64
POWER = 2
BLK = 128
THIN_ORDER = (2, 1, 0, 3)
WIDE_ORDER = (2, 3, 1, 0)

precise = lax.Precision.HIGHEST
f32 = jnp.float32
bf16 = jnp.bfloat16
VMEM = pl.BlockSpec(memory_space=pltpu.VMEM)
SMEM = pl.BlockSpec(memory_space=pltpu.SMEM)


def from_behind(value, axis, steps):
    count = lax.axis_size(axis)
    pairs = [(source, (source + steps) % count) for source in range(count)]
    return lax.ppermute(value, axis, pairs)


def gram_of(row_block):
    return jnp.dot(row_block, row_block.T, precision=precise, preferred_element_type=f32)


def solve_rows(gram_rows, row_block):
    low_factor = jnp.linalg.cholesky(gram_rows)
    solved = lax.linalg.triangular_solve(low_factor, row_block, left_side=True, lower=True)
    return solved.astype(bf16)


def tokens_of(sketches, matrices):
    parts = [
        jnp.einsum("km,tm->kt", s, m, preferred_element_type=f32)
        for s, m in zip(sketches, matrices)
    ]
    return tuple(lax.psum(p.astype(bf16), "tensor").astype(bf16) for p in parts)


def partials(token_rows, matrices):
    return tuple(
        jnp.dot(r, m, preferred_element_type=f32) for r, m in zip(token_rows, matrices)
    )


def orthonormal(parts):
    rows = [lax.psum(p.astype(bf16), "dp").astype(f32) for p in parts]
    grams = [lax.psum(gram_of(r).astype(bf16), "tensor").astype(f32) for r in rows]
    return tuple(solve_rows(g, r) for g, r in zip(grams, rows))


def feature_space(norm_in, query_grad, attn_out, handed, sketch_q, sketch_o):
    upstream = from_behind(handed, "section", -1)
    lefts = (norm_in[0], attn_out[0])
    rights = (query_grad[0], upstream[0])
    basis = orthonormal(partials(tokens_of((sketch_q[0], sketch_o[0]), rights), lefts))
    for _ in range(POWER):
        other = orthonormal(partials(tokens_of(basis, lefts), rights))
        basis = orthonormal(partials(tokens_of(other, rights), lefts))
    final = partials(tokens_of(basis, lefts), rights)
    raws = [lax.psum(p.astype(bf16), "dp").astype(f32) for p in final]
    energies = lax.psum(tuple(jnp.sum(r * r) for r in raws), "tensor")
    count = lax.axis_size("tensor")
    adapters = [
        r / jnp.sqrt(e / (r.size * count) + 1e-06) for r, e in zip(raws, energies)
    ]
    return (
        (basis[0] * 16.0)[None],
        adapters[0][None],
        (basis[1] * 16.0)[None],
        adapters[1][None],
    )


def swap(value, axis, bit):
    count = lax.axis_size(axis)
    return lax.ppermute(value, axis, [(i, i ^ bit) for i in range(count)])


def routed(value, sizes, token_bit, shifted):
    sections, dps, tensors = sizes
    side = tensors // 2
    pairs = []
    for s in range(sections):
        for z in range(dps):
            for t in range(tensors):
                to_t = t ^ side if t % side else t
                to_s = (s - 1) % sections if shifted and to_t >= side else s
                to = (to_s * dps + (z ^ token_bit)) * tensors + to_t
                pairs.append(((s * dps + z) * tensors + t, to))
    return lax.ppermute(value, ("section", "dp", "tensor"), pairs)


def window(ref, width, at):
    return ref.at[:, pl.ds(pl.multiple_of(at * width, width), width)]


def move(pairs, sems):
    copies = [pltpu.make_async_copy(src, dst, sems.at[n]) for n, (src, dst) in enumerate(pairs)]
    for c in copies:
        c.start()
    for c in copies:
        c.wait()


def give_wide_kernel(dps, idx, norm, hand, sk_q, sk_o, give, sems):
    z, kind = idx[0], idx[3]
    rows, fold = RANK // dps, give.shape[1] // dps
    small_w = sk_q.shape[1] // dps

    def sketch(ref, width):
        part = ref.at[:, pl.ds(pl.multiple_of(z * width, width), width)]
        return [
            (part.at[i * rows : (i + 1) * rows], give.at[BLK:, i * fold : i * fold + width])
            for i in range(dps)
        ]

    @pl.when(kind == 0)
    def _():
        move([(hand, give.at[:BLK])] + sketch(sk_o, fold), sems)

    @pl.when(kind == 1)
    def _():
        give[BLK:, :] = jnp.zeros((rows, give.shape[1]), bf16)
        move([(norm, give.at[:BLK])] + sketch(sk_q, small_w), sems)


def merge_kernel(dps, kind, fill, pairs, sems):
    for which in (0, 1):

        @pl.when(kind == which)
        def _():
            copies = [
                pltpu.make_async_copy(src, dst, sems.at[n])
                for n, (src, dst) in enumerate(pairs[which])
            ]
            for c in copies:
                c.start()
            fill(which)
            for c in copies:
                c.wait()


def merge_thin_kernel(dps, idx, grad, attn, got_grad, got_attn, *smalls):
    z, kind = idx[0], idx[3]
    small_w = smalls[0].shape[1] // 2
    for which, keep, got in ((0, grad, got_grad), (1, attn, got_attn)):

        @pl.when(kind == which)
        def _():
            for d in range(dps):
                part = pl.ds(pl.multiple_of((z ^ d) * small_w, small_w), small_w)
                smalls[d][:, :small_w] = keep[:, part]
                smalls[d][:, small_w:] = got[:, part]


def merge_wide_kernel(dps, idx, norm, hand, sk_q, sk_o, got, *refs):
    z, kind, bigs, sk, sems = idx[0], idx[3], refs[:dps], refs[dps], refs[-1]
    big_w, small_w = bigs[0].shape[1] // 2, sk.shape[1] // 2
    rows = RANK // dps

    def fill(which):
        for d in range(dps):
            at = pl.multiple_of((z ^ d) * big_w, big_w)
            bigs[d][:, big_w:] = got[:BLK, pl.ds(at, big_w)]
        for i in range(dps):
            part = got[BLK:, i * big_w : (i + 1) * big_w]
            one, two = RANK + i * rows, 2 * RANK + i * rows
            if which == 0:
                sk[one : one + rows, :] = jnp.zeros_like(part)
                sk[two : two + rows, small_w:] = part[:, :small_w]
            else:
                sk[one : one + rows, :] = part
                sk[two : two + rows, small_w:] = jnp.zeros_like(part[:, :small_w])
        if which == 0:
            sk[:RANK, :] = jnp.zeros((RANK, big_w), bf16)
        else:
            sk[2 * RANK :, :small_w] = jnp.zeros((RANK, small_w), bf16)

    def keep(ref, sketch):
        return [sketch] + [
            (window(ref, big_w, z ^ d), bigs[d].at[:, :big_w]) for d in range(dps)
        ]

    pairs = (
        keep(norm, (window(sk_q, small_w, z), sk.at[2 * RANK :, :small_w])),
        keep(hand, (window(sk_o, big_w, z), sk.at[:RANK, :])),
    )
    merge_kernel(dps, kind, fill, pairs, sems)


def nt(a, b, precision=None):
    return lax.dot_general(
        a, b, (((1,), (1,)), ((), ())), precision=precision, preferred_element_type=f32
    )


def packed_rows(dps):
    per_gram = (dps * (dps - 1) // 2 + dps // 2) * BLK
    thin = pl.cdiv(per_gram + 16, 32) * 32
    rest = per_gram + dps * RANK + 16
    wide = pl.cdiv(thin + rest, 64) * 64 - thin
    return per_gram, thin, wide


def pack_gram(m, flat, dps):
    r = lax.broadcasted_iota(jnp.int32, (BLK, BLK), 0)
    c = lax.broadcasted_iota(jnp.int32, (BLK, BLK), 1)
    at, on = 0, []
    for i in range(dps):
        row = nt(m[i * BLK : (i + 1) * BLK, :], m[: (i + 1) * BLK, :])
        for j in range(i):
            flat[at : at + BLK, :] = row[:, j * BLK : (j + 1) * BLK].astype(bf16)
            at += BLK
        on.append(row[:, i * BLK :])
    for i in range(0, dps, 2):
        flat[at : at + BLK, :] = jnp.where(r > c, on[i], on[i + 1]).astype(bf16)
        at += BLK
    diagonals = [jnp.sum(jnp.where(r == c, v, 0.0), axis=0, keepdims=True) for v in on]
    diagonals.append(jnp.zeros((16 - dps, BLK), f32))
    return at, jnp.concatenate(diagonals, axis=0).astype(bf16)


def hand_out(core, flat, keep, send):
    half = flat.shape[0] // 2
    keep[...] = flat[pl.ds(pl.multiple_of(core * half, 16), half), :]
    send[...] = flat[pl.ds(pl.multiple_of((1 - core) * half, 16), half), :]


def thin_gram_kernel(dps, idx, *refs):
    z, core = idx[0], idx[2]
    smalls, small, keep, send, flat = refs[:dps], *refs[dps:]
    for d, ref in zip(THIN_ORDER, smalls):
        small[pl.ds(pl.multiple_of((z ^ d) * BLK, BLK), BLK), :] = ref[...]
    at, diagonals = pack_gram(small, flat, dps)
    flat[at:, :] = jnp.zeros((flat.shape[0] - at, BLK), bf16)
    flat[at : at + 16, :] = diagonals
    hand_out(core, flat, keep, send)


def wide_gram_kernel(dps, idx, *refs):
    z, core = idx[0], idx[2]
    sk, bigs, small, big, keep, send, flat = refs[0], refs[1 : dps + 1], *refs[dps + 1 :]
    half_w = big.shape[1] // 2
    for d, ref in zip(WIDE_ORDER, bigs):
        big[pl.ds(pl.multiple_of((z ^ d) * BLK, BLK), BLK), :] = ref[...]
    at, diagonals = pack_gram(big, flat, dps)
    first = (
        nt(sk[:RANK, :], big[:, :half_w])
        + nt(sk[RANK : 2 * RANK, :], big[:, half_w:])
        + nt(sk[2 * RANK :, :], small[...])
    ).astype(bf16)
    for i in range(dps):
        flat[at : at + RANK, :] = first[:, i * BLK : (i + 1) * BLK]
        at += RANK
    flat[at:, :] = jnp.zeros((flat.shape[0] - at, BLK), bf16)
    flat[at : at + 16, :] = diagonals
    hand_out(core, flat, keep, send)


def add_halves_kernel(idx, thin_mine, thin_got, wide_mine, wide_got, keep, send, both):
    size, bit, split_at = keep.shape[0], idx[0] % 2, thin_mine.shape[0]
    both[:split_at, :] = (thin_mine[...].astype(f32) + thin_got[...].astype(f32)).astype(bf16)
    both[split_at:, :] = (wide_mine[...].astype(f32) + wide_got[...].astype(f32)).astype(bf16)
    for out, which in ((keep, bit), (send, 1 - bit)):
        out[...] = both[pl.ds(pl.multiple_of(which * size, 16), size), :]


def add_kernel(mine, got, out):
    out[...] = (mine[...].astype(f32) + got[...].astype(f32)).astype(bf16)


def inverse_factor(gram, spread):
    n, nb = gram.shape[0], 8
    rows = lax.broadcasted_iota(jnp.int32, (n, n), 0)
    cols = lax.broadcasted_iota(jnp.int32, (n, n), 1)
    work = jnp.concatenate([(rows == cols).astype(f32), gram], axis=1)
    count = n // nb
    slabs = [work[nb * s : nb * s + nb, :] for s in range(count)]
    sub = lax.broadcasted_iota(jnp.int32, (nb, 2 * n), 0)

    def lane(x, k):
        return jnp.broadcast_to(x[:, n + k : n + k + 1], (nb, 2 * n))

    def row(at):
        return jnp.broadcast_to(spread[at : at + 1, :], (nb, 2 * n))

    done = []
    for b in range(count):
        base = b * nb * (nb + 1)
        spread[base : base + nb, :] = slabs[b]
        for j in range(nb):
            at = base + nb * (j + 1)
            spread[at : at + nb, :] = lane(slabs[b], nb * b + j)
        pivot_rows = [row(base + i) for i in range(nb)]
        splat = [[row(base + nb * (j + 1) + i) for j in range(i + 1)] for i in range(nb)]
        below = {s: [lane(slabs[s], nb * b + j) for j in range(nb)] for s in range(b + 1, count)}
        out = None
        for k in range(nb):
            inv = 1.0 / splat[k][k]
            at = pivot_rows[k]
            final = at * lax.rsqrt(splat[k][k])
            out = final if out is None else jnp.where(sub == k, final, out)
            for i in range(k + 1, nb):
                mult = splat[i][k] * inv
                for j in range(k + 1, i + 1):
                    splat[i][j] = splat[i][j] - mult * splat[j][k]
                pivot_rows[i] = pivot_rows[i] - mult * at
            for s in range(b + 1, count):
                mult = below[s][k] * inv
                for j in range(k + 1, nb):
                    below[s][j] = below[s][j] - mult * splat[j][k]
                slabs[s] = slabs[s] - mult * at
        done.append(out)
    return jnp.concatenate(done, axis=0)[:, :n]


def split(x):
    high = x.astype(bf16)
    return high, (x - high.astype(f32)).astype(bf16)


def times(rows, gram):
    n = rows.shape[0]
    both = jnp.dot(jnp.concatenate(split(rows), axis=0), gram, preferred_element_type=f32)
    return both[:n] + both[n:]


def product(a, b):
    (ah, al), (bh, bl) = split(a), split(b)
    return jnp.dot(
        jnp.concatenate([ah, ah, al], axis=1),
        jnp.concatenate([bh, bl, bh], axis=0),
        preferred_element_type=f32,
    )


def product_nt(a, b):
    (ah, al), (bh, bl) = split(a), split(b)
    return nt(jnp.concatenate([ah, ah, al], axis=1), jnp.concatenate([bh, bl, bh], axis=1))


def chain_kernel(dps, counts, idx, *refs):
    z, out_half, core = idx[0], idx[1], idx[2]
    quarters, big, small, out, stays, leaves, flat, thin, wide, left, right, spread = (
        refs[:4],
        *refs[4:],
    )
    size, bit = quarters[0].shape[0], z % 2
    for n, ref in enumerate(quarters):
        which = 2 * (core ^ (n // 2)) + (bit ^ (n % 2))
        flat[pl.ds(pl.multiple_of(which * size, 16), size), :] = ref[...]
    per_gram, thin_rows, wide_rows = packed_rows(dps)
    for n in range(2):
        at, split_at = n * 2 * size, n * 2 * size + thin_rows // 2
        thin[n * (thin_rows // 2) : (n + 1) * (thin_rows // 2), :] = flat[at:split_at, :]
        wide[n * (wide_rows // 2) : (n + 1) * (wide_rows // 2), :] = flat[split_at : at + 2 * size, :]
    r = lax.broadcasted_iota(jnp.int32, (BLK, BLK), 0)
    c = lax.broadcasted_iota(jnp.int32, (BLK, BLK), 1)
    rows = jnp.concatenate(
        [wide[per_gram + i * RANK : per_gram + (i + 1) * RANK, :] for i in range(dps)], axis=1
    ).astype(f32)
    wide_diag = wide[per_gram + dps * RANK : per_gram + dps * RANK + 16, :].astype(f32)
    thin_diag = thin[per_gram : per_gram + 16, :].astype(f32)
    is_out = out_half == 1
    for gram, is_wide in ((left, out_half == 0), (right, is_out)):

        def block(n):
            part = slice(n * BLK, (n + 1) * BLK)
            return jnp.where(is_wide, wide[part, :].astype(f32), thin[part, :].astype(f32))

        def put(i, j, value):
            gram[i * BLK : (i + 1) * BLK, j * BLK : (j + 1) * BLK] = value.astype(bf16)

        n = 0
        for i in range(dps):
            for j in range(i):
                value = block(n)
                put(i, j, value)
                put(j, i, value.T)
                n += 1
        diag = jnp.where(is_wide, wide_diag, thin_diag)
        for i in range(0, dps, 2):
            value = block(n)
            turned = value.T
            put(i, i, jnp.where(r > c, value, jnp.where(r == c, diag[i : i + 1, :], turned)))
            put(
                i + 1,
                i + 1,
                jnp.where(r < c, value, jnp.where(r == c, diag[i + 1 : i + 2, :], turned)),
            )
            n += 1
    ahead = times(rows, left[...])
    gram = product_nt(ahead, rows)
    for step in range(2 * POWER):
        following = (right if step % 2 == 0 else left)[...]
        beyond = times(ahead, following)
        inner = product_nt(beyond, ahead)
        low_inv = inverse_factor(gram, spread)
        rows = product(low_inv, ahead)
        if step < 2 * POWER - 1:
            gram = product_nt(product(low_inv, inner), low_inv)
            ahead = product(low_inv, beyond)
        else:
            ahead = times(rows, following)
            gram = product_nt(ahead, rows)
    low_inv = inverse_factor(gram, spread)
    basis = product(low_inv, rows)
    rows = product(low_inv, ahead)
    energy = jnp.sum(times(rows, right[...]) * rows)
    count = jnp.where(out_half == 1, counts[0], counts[1]).astype(f32)
    scale = lax.rsqrt(jnp.full((1, 1), energy, f32) / count + 1e-06)
    coef_b, coef_a = basis.astype(bf16), rows.astype(bf16)
    for_big = jnp.where(is_out, coef_a, coef_b)
    for_small = jnp.where(is_out, coef_b, coef_a)
    scale_big = jnp.where(is_out, scale, 16.0)
    scale_small = jnp.where(is_out, 16.0, scale)
    big_w, small_w = big.shape[1] // 2, small.shape[1] // 2
    made_big = (jnp.dot(for_big, big[...], preferred_element_type=f32) * scale_big).astype(bf16)
    made_small = (jnp.dot(for_small, small[...], preferred_element_type=f32) * scale_small).astype(
        bf16
    )
    for n, half in enumerate((stays, leaves)):
        half[:, :big_w] = made_big[:, n * big_w : (n + 1) * big_w]
        half[:, big_w:] = made_small[:, n * small_w : (n + 1) * small_w]
        out[n * RANK : (n + 1) * RANK, :] = half[...]


def place_kernel(which, idx, *refs):
    z, kind, n = idx[0], idx[3], len(which)
    mine, theirs = refs[:n], refs[n : 2 * n]
    outs, held, sems = refs[-9:-5], refs[-5:-1], refs[-1]
    for i in range(n):
        here, there = mine[i].at[:RANK], theirs[i].at[theirs[i].shape[0] - RANK :]
        b_q, a_q, b_o, a_o = (h.at[i] for h in held)
        big_w = b_q.shape[1]
        for half, query, output in ((0, here, there), (1, there, here)):

            @pl.when(kind == half)
            def _():
                b_q[...] = query[:, :big_w]
                a_q[...] = query[:, big_w:].astype(f32)
                a_o[...] = output[:, :big_w].astype(f32)
                b_o[...] = output[:, big_w:]

    pairs = [
        (h.at[i], window(out, h.shape[2], z ^ d))
        for i, d in enumerate(which)
        for h, out in zip(held, outs)
    ]
    move(pairs, sems)


def place(which, idx, mine, theirs, shapes, widths, outs=()):
    n = len(which)
    hbm = pl.BlockSpec(memory_space=pl.ANY)
    return pl.pallas_call(
        functools.partial(place_kernel, which),
        out_shape=shapes,
        in_specs=[SMEM] + [VMEM] * (2 * n) + [hbm] * len(outs),
        out_specs=[hbm] * len(shapes),
        scratch_shapes=[pltpu.VMEM((n, RANK, w), s.dtype) for w, s in zip(widths, shapes)]
        + [pltpu.SemaphoreType.DMA((n * len(shapes),))],
        input_output_aliases={2 * n + 1 + i: i for i in range(len(outs))},
        compiler_params=pltpu.CompilerParams(vmem_limit_bytes=48 * 2**20),
    )(idx, *mine, *theirs, *outs)


def call(kernel, out_shapes, args, scratch=(), spaces=()):
    spaces = [SMEM] + [VMEM] * (len(args) - 1) if not spaces else spaces
    return pl.pallas_call(
        kernel,
        out_shape=out_shapes,
        in_specs=spaces,
        out_specs=jax.tree.map(lambda _: VMEM, out_shapes),
        scratch_shapes=list(scratch),
        compiler_params=pltpu.CompilerParams(vmem_limit_bytes=48 * 2**20),
    )(*args)


def token_space(sizes, norm_in, query_grad, attn_out, handed, sketch_q, sketch_o):
    _, dps, tensors = sizes
    side = tensors // 2

    def shape(*dims, dtype=bf16):
        return jax.ShapeDtypeStruct(dims, dtype)

    z, t = lax.axis_index("dp"), lax.axis_index("tensor")
    half, core = t // side, t % side
    idx = jnp.stack([z, half, core, half ^ core]).astype(jnp.int32)
    wide, narrow = norm_in.shape[2], query_grad.shape[2]
    big_w, small_w = wide // dps, narrow // dps
    tokens = dps * BLK
    hbm = pl.BlockSpec(memory_space=pltpu.HBM)
    norm, hand, sk_q, sk_o = (
        pltpu.with_memory_space_constraint(v[0], pltpu.HBM)
        for v in (norm_in, handed, sketch_q, sketch_o)
    )

    got_grad, got_attn = swap(query_grad[0], "tensor", 1), swap(attn_out[0], "tensor", 1)
    give = call(
        functools.partial(give_wide_kernel, dps),
        shape(BLK + RANK // dps, wide),
        (idx, norm, hand, sk_q, sk_o),
        [pltpu.SemaphoreType.DMA((1 + dps,))],
        [SMEM] + [hbm] * 4,
    )
    give, got_grad, got_attn = lax.optimization_barrier((give, got_grad, got_attn))
    smalls = call(
        functools.partial(merge_thin_kernel, dps),
        [shape(BLK, 2 * small_w)] * dps,
        (idx, query_grad[0], attn_out[0], got_grad, got_attn),
    )
    smalls = list(smalls)
    got = swap(give, "tensor", 1)
    packed = call(
        functools.partial(merge_wide_kernel, dps),
        [shape(BLK, 2 * big_w)] * dps + [shape(3 * RANK, 2 * small_w)],
        (idx, norm, hand, sk_q, sk_o, got),
        [pltpu.SemaphoreType.DMA((dps + 1,))],
        [SMEM, hbm, hbm, hbm, hbm, VMEM],
    )
    smalls = [routed(smalls[d], sizes, d, False) for d in THIN_ORDER]
    sketch = routed(packed[dps], sizes, 0, False)
    bigs = [routed(packed[d], sizes, d, True) for d in WIDE_ORDER]

    _, thin_rows, wide_rows = packed_rows(dps)

    def gram(kernel, m, rows, operands):
        m, keep, send = call(
            functools.partial(kernel, dps),
            [m, shape(rows // 2, BLK), shape(rows // 2, BLK)],
            (idx, *operands),
            [pltpu.VMEM((rows, BLK), bf16)],
        )
        return m, keep, swap(send, "tensor", 1)

    small, *thin = gram(thin_gram_kernel, shape(tokens, 2 * small_w), thin_rows, smalls)
    big, *rest = gram(
        wide_gram_kernel, shape(tokens, 2 * big_w), wide_rows, (sketch, *bigs, small)
    )
    total = thin_rows + wide_rows
    quarter = shape(total // 4, BLK)
    keep, send = call(
        add_halves_kernel,
        [quarter] * 2,
        (idx, *thin, *rest),
        [pltpu.VMEM((total // 2, BLK), bf16)],
    )
    for bit, value in ((1, send), (2, None)):
        value = swap(keep if value is None else value, "dp", bit)
        keep = call(add_kernel, quarter, (keep, value), (), [VMEM] * 2)
    beside = swap(keep, "dp", 1)
    quarters = (keep, beside, swap(keep, "tensor", 1), swap(beside, "tensor", 1))

    counts = (RANK * wide * tensors, RANK * narrow * tensors)
    whole, stays, leaves = call(
        functools.partial(chain_kernel, dps, counts),
        [shape(2 * RANK, big_w + small_w)] + [shape(RANK, big_w + small_w)] * 2,
        (idx, *quarters, big, small),
        [
            pltpu.VMEM((total, BLK), bf16),
            pltpu.VMEM((thin_rows, BLK), bf16),
            pltpu.VMEM((wide_rows, BLK), bf16),
            pltpu.VMEM((tokens, tokens), bf16),
            pltpu.VMEM((tokens, tokens), bf16),
            pltpu.VMEM((9 * RANK, 2 * RANK), f32),
        ],
    )
    leaves, stays = routed(leaves, sizes, 2, False), routed(stays, sizes, 2, False)
    near, here = routed(whole, sizes, 1, False), routed(whole, sizes, 0, False)
    leaves_on, stays_on = swap(leaves, "dp", 1), swap(stays, "dp", 1)
    mine = (here, near, stays, stays_on)
    theirs = [swap(v, "tensor", 1) for v in (here, near, leaves, leaves_on)]
    shapes = [
        shape(RANK, wide),
        shape(RANK, narrow, dtype=f32),
        shape(RANK, narrow),
        shape(RANK, wide, dtype=f32),
    ]
    widths = (big_w, small_w, small_w, big_w)
    outs = place((0, 1, 2), idx, mine[:3], theirs[:3], shapes, widths)
    outs = place((3,), idx, mine[3:], theirs[3:], shapes, widths, outs)
    return tuple(o[None] for o in outs)


def solution(mesh):
    sizes = tuple(mesh.shape[axis] for axis in ("section", "dp", "tensor"))
    _, dps, tensors = sizes

    def body(norm_in, query_grad, attn_out, handed, sketch_q, sketch_o):
        args = (norm_in, query_grad, attn_out, handed, sketch_q, sketch_o)
        fits = (
            dps == 4
            and tensors == 4
            and norm_in.shape[1] == BLK
            and sketch_q.shape[1] == RANK
            and norm_in.shape[2] == handed.shape[2]
            and query_grad.shape[2] == attn_out.shape[2]
            and norm_in.shape[2] == 2 * query_grad.shape[2]
            and query_grad.shape[2] % (dps * 128) == 0
        )
        return token_space(sizes, *args) if fits else feature_space(*args)

    return jax.shard_map(
        body,
        mesh=mesh,
        in_specs=(P("section", "dp", "tensor"),) * 4 + (P("section", None, "tensor"),) * 2,
        out_specs=(P("section", None, "tensor"),) * 4,
        check_vma=False,
    )
```

```python
import functools

import jax
import jax.numpy as jnp
from jax import lax
from jax.experimental import pallas as pl
from jax.experimental.pallas import tpu as pltpu
from jax.sharding import PartitionSpec as P

RANK = 64
POWER = 2
BLK = 128
THIN_ORDER = (2, 1, 0, 3)
WIDE_ORDER = (2, 3, 1, 0)

precise = lax.Precision.HIGHEST
f32 = jnp.float32
bf16 = jnp.bfloat16
VMEM = pl.BlockSpec(memory_space=pltpu.VMEM)
SMEM = pl.BlockSpec(memory_space=pltpu.SMEM)


def from_behind(value, axis, steps):
    count = lax.axis_size(axis)
    pairs = [(source, (source + steps) % count) for source in range(count)]
    return lax.ppermute(value, axis, pairs)


def gram_of(row_block):
    return jnp.dot(row_block, row_block.T, precision=precise, preferred_element_type=f32)


def solve_rows(gram_rows, row_block):
    low_factor = jnp.linalg.cholesky(gram_rows)
    solved = lax.linalg.triangular_solve(low_factor, row_block, left_side=True, lower=True)
    return solved.astype(bf16)


def tokens_of(sketches, matrices):
    parts = [
        jnp.einsum("km,tm->kt", s, m, preferred_element_type=f32)
        for s, m in zip(sketches, matrices)
    ]
    return tuple(lax.psum(p.astype(bf16), "tensor").astype(bf16) for p in parts)


def partials(token_rows, matrices):
    return tuple(
        jnp.dot(r, m, preferred_element_type=f32) for r, m in zip(token_rows, matrices)
    )


def orthonormal(parts):
    rows = [lax.psum(p.astype(bf16), "dp").astype(f32) for p in parts]
    grams = [lax.psum(gram_of(r).astype(bf16), "tensor").astype(f32) for r in rows]
    return tuple(solve_rows(g, r) for g, r in zip(grams, rows))


def feature_space(norm_in, query_grad, attn_out, handed, sketch_q, sketch_o):
    upstream = from_behind(handed, "section", -1)
    lefts = (norm_in[0], attn_out[0])
    rights = (query_grad[0], upstream[0])
    basis = orthonormal(partials(tokens_of((sketch_q[0], sketch_o[0]), rights), lefts))
    for _ in range(POWER):
        other = orthonormal(partials(tokens_of(basis, lefts), rights))
        basis = orthonormal(partials(tokens_of(other, rights), lefts))
    final = partials(tokens_of(basis, lefts), rights)
    raws = [lax.psum(p.astype(bf16), "dp").astype(f32) for p in final]
    energies = lax.psum(tuple(jnp.sum(r * r) for r in raws), "tensor")
    count = lax.axis_size("tensor")
    adapters = [
        r / jnp.sqrt(e / (r.size * count) + 1e-06) for r, e in zip(raws, energies)
    ]
    return (
        (basis[0] * 16.0)[None],
        adapters[0][None],
        (basis[1] * 16.0)[None],
        adapters[1][None],
    )


def swap(value, axis, bit):
    count = lax.axis_size(axis)
    return lax.ppermute(value, axis, [(i, i ^ bit) for i in range(count)])


def routed(value, sizes, token_bit, shifted):
    sections, dps, tensors = sizes
    side = tensors // 2
    pairs = []
    for s in range(sections):
        for z in range(dps):
            for t in range(tensors):
                to_t = t ^ side if t % side else t
                to_s = (s - 1) % sections if shifted and to_t >= side else s
                to = (to_s * dps + (z ^ token_bit)) * tensors + to_t
                pairs.append(((s * dps + z) * tensors + t, to))
    return lax.ppermute(value, ("section", "dp", "tensor"), pairs)


def window(ref, width, at):
    return ref.at[:, pl.ds(pl.multiple_of(at * width, width), width)]


def move(pairs, sems):
    copies = [pltpu.make_async_copy(src, dst, sems.at[n]) for n, (src, dst) in enumerate(pairs)]
    for c in copies:
        c.start()
    for c in copies:
        c.wait()


def give_wide_kernel(dps, idx, norm, hand, sk_q, sk_o, give, sems):
    z, kind = idx[0], idx[3]
    rows, fold = RANK // dps, give.shape[1] // dps
    small_w = sk_q.shape[1] // dps

    def sketch(ref, width):
        part = ref.at[:, pl.ds(pl.multiple_of(z * width, width), width)]
        return [
            (part.at[i * rows : (i + 1) * rows], give.at[BLK:, i * fold : i * fold + width])
            for i in range(dps)
        ]

    @pl.when(kind == 0)
    def _():
        move([(hand, give.at[:BLK])] + sketch(sk_o, fold), sems)

    @pl.when(kind == 1)
    def _():
        give[BLK:, :] = jnp.zeros((rows, give.shape[1]), bf16)
        move([(norm, give.at[:BLK])] + sketch(sk_q, small_w), sems)


def merge_kernel(dps, kind, fill, pairs, sems):
    for which in (0, 1):

        @pl.when(kind == which)
        def _():
            copies = [
                pltpu.make_async_copy(src, dst, sems.at[n])
                for n, (src, dst) in enumerate(pairs[which])
            ]
            for c in copies:
                c.start()
            fill(which)
            for c in copies:
                c.wait()


def merge_thin_kernel(dps, idx, grad, attn, got_grad, got_attn, *smalls):
    z, kind = idx[0], idx[3]
    small_w = smalls[0].shape[1] // 2
    for which, keep, got in ((0, grad, got_grad), (1, attn, got_attn)):

        @pl.when(kind == which)
        def _():
            for d in range(dps):
                part = pl.ds(pl.multiple_of((z ^ d) * small_w, small_w), small_w)
                smalls[d][:, :small_w] = keep[:, part]
                smalls[d][:, small_w:] = got[:, part]


def merge_wide_kernel(dps, idx, norm, hand, sk_q, sk_o, got, *refs):
    z, kind, bigs, sk, sems = idx[0], idx[3], refs[:dps], refs[dps], refs[-1]
    big_w, small_w = bigs[0].shape[1] // 2, sk.shape[1] // 2
    rows = RANK // dps

    def fill(which):
        own = hand if which else norm
        for d in range(dps):
            part = pl.ds(pl.multiple_of((z ^ d) * big_w, big_w), big_w)
            bigs[d][:, :big_w] = own[:, part]
            bigs[d][:, big_w:] = got[:BLK, part]
        for i in range(dps):
            part = got[BLK:, i * big_w : (i + 1) * big_w]
            one, two = RANK + i * rows, 2 * RANK + i * rows
            if which == 0:
                sk[one : one + rows, :] = jnp.zeros_like(part)
                sk[two : two + rows, small_w:] = part[:, :small_w]
            else:
                sk[one : one + rows, :] = part
                sk[two : two + rows, small_w:] = jnp.zeros_like(part[:, :small_w])
        if which == 0:
            sk[:RANK, :] = jnp.zeros((RANK, big_w), bf16)
        else:
            sk[2 * RANK :, :small_w] = jnp.zeros((RANK, small_w), bf16)

    pairs = (
        [(window(sk_q, small_w, z), sk.at[2 * RANK :, :small_w])],
        [(window(sk_o, big_w, z), sk.at[:RANK, :])],
    )
    merge_kernel(dps, kind, fill, pairs, sems)


def nt(a, b, precision=None):
    return lax.dot_general(
        a, b, (((1,), (1,)), ((), ())), precision=precision, preferred_element_type=f32
    )


def packed_rows(dps):
    per_gram = (dps * (dps - 1) // 2 + dps // 2) * BLK
    thin = pl.cdiv(per_gram + 16, 32) * 32
    rest = per_gram + dps * RANK + 16
    wide = pl.cdiv(thin + rest, 64) * 64 - thin
    return per_gram, thin, wide


def pack_gram(m, flat, dps):
    r = lax.broadcasted_iota(jnp.int32, (BLK, BLK), 0)
    c = lax.broadcasted_iota(jnp.int32, (BLK, BLK), 1)
    at, on = 0, []
    for i in range(dps):
        row = nt(m[i * BLK : (i + 1) * BLK, :], m[: (i + 1) * BLK, :])
        for j in range(i):
            flat[at : at + BLK, :] = row[:, j * BLK : (j + 1) * BLK].astype(bf16)
            at += BLK
        on.append(row[:, i * BLK :])
    for i in range(0, dps, 2):
        flat[at : at + BLK, :] = jnp.where(r > c, on[i], on[i + 1]).astype(bf16)
        at += BLK
    diagonals = [jnp.sum(jnp.where(r == c, v, 0.0), axis=0, keepdims=True) for v in on]
    diagonals.append(jnp.zeros((16 - dps, BLK), f32))
    return at, jnp.concatenate(diagonals, axis=0).astype(bf16)


def hand_out(core, flat, keep, send):
    half = flat.shape[0] // 2
    keep[...] = flat[pl.ds(pl.multiple_of(core * half, 16), half), :]
    send[...] = flat[pl.ds(pl.multiple_of((1 - core) * half, 16), half), :]


def thin_gram_kernel(dps, idx, *refs):
    z, core = idx[0], idx[2]
    smalls, small, keep, send, flat = refs[:dps], *refs[dps:]
    for d, ref in zip(THIN_ORDER, smalls):
        small[pl.ds(pl.multiple_of((z ^ d) * BLK, BLK), BLK), :] = ref[...]
    at, diagonals = pack_gram(small, flat, dps)
    flat[at:, :] = jnp.zeros((flat.shape[0] - at, BLK), bf16)
    flat[at : at + 16, :] = diagonals
    hand_out(core, flat, keep, send)


def wide_gram_kernel(dps, idx, *refs):
    z, core = idx[0], idx[2]
    sk, bigs, small, big, keep, send, flat = refs[0], refs[1 : dps + 1], *refs[dps + 1 :]
    half_w = big.shape[1] // 2
    for d, ref in zip(WIDE_ORDER, bigs):
        big[pl.ds(pl.multiple_of((z ^ d) * BLK, BLK), BLK), :] = ref[...]
    at, diagonals = pack_gram(big, flat, dps)
    first = (
        nt(sk[:RANK, :], big[:, :half_w])
        + nt(sk[RANK : 2 * RANK, :], big[:, half_w:])
        + nt(sk[2 * RANK :, :], small[...])
    ).astype(bf16)
    for i in range(dps):
        flat[at : at + RANK, :] = first[:, i * BLK : (i + 1) * BLK]
        at += RANK
    flat[at:, :] = jnp.zeros((flat.shape[0] - at, BLK), bf16)
    flat[at : at + 16, :] = diagonals
    hand_out(core, flat, keep, send)


def add_halves_kernel(idx, thin_mine, thin_got, wide_mine, wide_got, keep, send, both):
    size, bit, split_at = keep.shape[0], idx[0] % 2, thin_mine.shape[0]
    both[:split_at, :] = (thin_mine[...].astype(f32) + thin_got[...].astype(f32)).astype(bf16)
    both[split_at:, :] = (wide_mine[...].astype(f32) + wide_got[...].astype(f32)).astype(bf16)
    for out, which in ((keep, bit), (send, 1 - bit)):
        out[...] = both[pl.ds(pl.multiple_of(which * size, 16), size), :]


def add_kernel(mine, got, out):
    out[...] = (mine[...].astype(f32) + got[...].astype(f32)).astype(bf16)


def inverse_factor(gram, spread):
    n, nb = gram.shape[0], 8
    rows = lax.broadcasted_iota(jnp.int32, (n, n), 0)
    cols = lax.broadcasted_iota(jnp.int32, (n, n), 1)
    work = jnp.concatenate([(rows == cols).astype(f32), gram], axis=1)
    count = n // nb
    slabs = [work[nb * s : nb * s + nb, :] for s in range(count)]
    sub = lax.broadcasted_iota(jnp.int32, (nb, 2 * n), 0)

    def lane(x, k):
        return jnp.broadcast_to(x[:, n + k : n + k + 1], (nb, 2 * n))

    def row(at):
        return jnp.broadcast_to(spread[at : at + 1, :], (nb, 2 * n))

    done = []
    for b in range(count):
        base = b * nb * (nb + 1)
        spread[base : base + nb, :] = slabs[b]
        for j in range(nb):
            at = base + nb * (j + 1)
            spread[at : at + nb, :] = lane(slabs[b], nb * b + j)
        pivot_rows = [row(base + i) for i in range(nb)]
        splat = [[row(base + nb * (j + 1) + i) for j in range(i + 1)] for i in range(nb)]
        below = {s: [lane(slabs[s], nb * b + j) for j in range(nb)] for s in range(b + 1, count)}
        out = None
        for k in range(nb):
            inv = 1.0 / splat[k][k]
            at = pivot_rows[k]
            final = at * lax.rsqrt(splat[k][k])
            out = final if out is None else jnp.where(sub == k, final, out)
            for i in range(k + 1, nb):
                mult = splat[i][k] * inv
                for j in range(k + 1, i + 1):
                    splat[i][j] = splat[i][j] - mult * splat[j][k]
                pivot_rows[i] = pivot_rows[i] - mult * at
            for s in range(b + 1, count):
                mult = below[s][k] * inv
                for j in range(k + 1, nb):
                    below[s][j] = below[s][j] - mult * splat[j][k]
                slabs[s] = slabs[s] - mult * at
        done.append(out)
    return jnp.concatenate(done, axis=0)[:, :n]


def split(x):
    high = x.astype(bf16)
    return high, (x - high.astype(f32)).astype(bf16)


def times(rows, gram):
    n = rows.shape[0]
    both = jnp.dot(jnp.concatenate(split(rows), axis=0), gram, preferred_element_type=f32)
    return both[:n] + both[n:]


def product(a, b):
    (ah, al), (bh, bl) = split(a), split(b)
    return jnp.dot(
        jnp.concatenate([ah, ah, al], axis=1),
        jnp.concatenate([bh, bl, bh], axis=0),
        preferred_element_type=f32,
    )


def product_nt(a, b):
    (ah, al), (bh, bl) = split(a), split(b)
    return nt(jnp.concatenate([ah, ah, al], axis=1), jnp.concatenate([bh, bl, bh], axis=1))


def chain_kernel(dps, counts, idx, *refs):
    z, out_half, core = idx[0], idx[1], idx[2]
    quarters, big, small, out, stays, leaves, flat, thin, wide, left, right, spread = (
        refs[:4],
        *refs[4:],
    )
    size, bit = quarters[0].shape[0], z % 2
    for n, ref in enumerate(quarters):
        which = 2 * (core ^ (n // 2)) + (bit ^ (n % 2))
        flat[pl.ds(pl.multiple_of(which * size, 16), size), :] = ref[...]
    per_gram, thin_rows, wide_rows = packed_rows(dps)
    for n in range(2):
        at, split_at = n * 2 * size, n * 2 * size + thin_rows // 2
        thin[n * (thin_rows // 2) : (n + 1) * (thin_rows // 2), :] = flat[at:split_at, :]
        wide[n * (wide_rows // 2) : (n + 1) * (wide_rows // 2), :] = flat[split_at : at + 2 * size, :]
    r = lax.broadcasted_iota(jnp.int32, (BLK, BLK), 0)
    c = lax.broadcasted_iota(jnp.int32, (BLK, BLK), 1)
    rows = jnp.concatenate(
        [wide[per_gram + i * RANK : per_gram + (i + 1) * RANK, :] for i in range(dps)], axis=1
    ).astype(f32)
    wide_diag = wide[per_gram + dps * RANK : per_gram + dps * RANK + 16, :].astype(f32)
    thin_diag = thin[per_gram : per_gram + 16, :].astype(f32)
    is_out = out_half == 1
    for gram, is_wide in ((left, out_half == 0), (right, is_out)):

        def block(n):
            part = slice(n * BLK, (n + 1) * BLK)
            return jnp.where(is_wide, wide[part, :].astype(f32), thin[part, :].astype(f32))

        def put(i, j, value):
            gram[i * BLK : (i + 1) * BLK, j * BLK : (j + 1) * BLK] = value.astype(bf16)

        n = 0
        for i in range(dps):
            for j in range(i):
                value = block(n)
                put(i, j, value)
                put(j, i, value.T)
                n += 1
        diag = jnp.where(is_wide, wide_diag, thin_diag)
        for i in range(0, dps, 2):
            value = block(n)
            turned = value.T
            put(i, i, jnp.where(r > c, value, jnp.where(r == c, diag[i : i + 1, :], turned)))
            put(
                i + 1,
                i + 1,
                jnp.where(r < c, value, jnp.where(r == c, diag[i + 1 : i + 2, :], turned)),
            )
            n += 1
    ahead = times(rows, left[...])
    gram = product_nt(ahead, rows)
    for step in range(2 * POWER):
        following = (right if step % 2 == 0 else left)[...]
        beyond = times(ahead, following)
        inner = product_nt(beyond, ahead)
        low_inv = inverse_factor(gram, spread)
        rows = product(low_inv, ahead)
        gram = product_nt(product(low_inv, inner), low_inv)
        ahead = product(low_inv, beyond)
    low_inv = inverse_factor(gram, spread)
    basis = product(low_inv, rows)
    rows = product(low_inv, ahead)
    energy = jnp.sum(times(rows, right[...]) * rows)
    count = jnp.where(out_half == 1, counts[0], counts[1]).astype(f32)
    scale = lax.rsqrt(jnp.full((1, 1), energy, f32) / count + 1e-06)
    coef_b, coef_a = basis.astype(bf16), rows.astype(bf16)
    for_big = jnp.where(is_out, coef_a, coef_b)
    for_small = jnp.where(is_out, coef_b, coef_a)
    scale_big = jnp.where(is_out, scale, 16.0)
    scale_small = jnp.where(is_out, 16.0, scale)
    big_w, small_w = big.shape[1] // 2, small.shape[1] // 2
    made_big = (jnp.dot(for_big, big[...], preferred_element_type=f32) * scale_big).astype(bf16)
    made_small = (jnp.dot(for_small, small[...], preferred_element_type=f32) * scale_small).astype(
        bf16
    )
    for n, half in enumerate((stays, leaves)):
        half[:, :big_w] = made_big[:, n * big_w : (n + 1) * big_w]
        half[:, big_w:] = made_small[:, n * small_w : (n + 1) * small_w]
        out[n * RANK : (n + 1) * RANK, :] = half[...]


def place_kernel(which, idx, *refs):
    z, kind, n = idx[0], idx[3], len(which)
    mine, theirs = refs[:n], refs[n : 2 * n]
    outs, held, sems = refs[-9:-5], refs[-5:-1], refs[-1]
    for i in range(n):
        here, there = mine[i].at[:RANK], theirs[i].at[theirs[i].shape[0] - RANK :]
        b_q, a_q, b_o, a_o = (h.at[i] for h in held)
        big_w = b_q.shape[1]
        for half, query, output in ((0, here, there), (1, there, here)):

            @pl.when(kind == half)
            def _():
                b_q[...] = query[:, :big_w]
                a_q[...] = query[:, big_w:].astype(f32)
                a_o[...] = output[:, :big_w].astype(f32)
                b_o[...] = output[:, big_w:]

    pairs = [
        (h.at[i], window(out, h.shape[2], z ^ d))
        for i, d in enumerate(which)
        for h, out in zip(held, outs)
    ]
    move(pairs, sems)


def place(which, idx, mine, theirs, shapes, widths, outs=()):
    n = len(which)
    hbm = pl.BlockSpec(memory_space=pl.ANY)
    return pl.pallas_call(
        functools.partial(place_kernel, which),
        out_shape=shapes,
        in_specs=[SMEM] + [VMEM] * (2 * n) + [hbm] * len(outs),
        out_specs=[hbm] * len(shapes),
        scratch_shapes=[pltpu.VMEM((n, RANK, w), s.dtype) for w, s in zip(widths, shapes)]
        + [pltpu.SemaphoreType.DMA((n * len(shapes),))],
        input_output_aliases={2 * n + 1 + i: i for i in range(len(outs))},
        compiler_params=pltpu.CompilerParams(vmem_limit_bytes=48 * 2**20),
    )(idx, *mine, *theirs, *outs)


def call(kernel, out_shapes, args, scratch=(), spaces=()):
    spaces = [SMEM] + [VMEM] * (len(args) - 1) if not spaces else spaces
    return pl.pallas_call(
        kernel,
        out_shape=out_shapes,
        in_specs=spaces,
        out_specs=jax.tree.map(lambda _: VMEM, out_shapes),
        scratch_shapes=list(scratch),
        compiler_params=pltpu.CompilerParams(vmem_limit_bytes=48 * 2**20),
    )(*args)


def token_space(sizes, norm_in, query_grad, attn_out, handed, sketch_q, sketch_o):
    _, dps, tensors = sizes
    side = tensors // 2

    def shape(*dims, dtype=bf16):
        return jax.ShapeDtypeStruct(dims, dtype)

    z, t = lax.axis_index("dp"), lax.axis_index("tensor")
    half, core = t // side, t % side
    idx = jnp.stack([z, half, core, half ^ core]).astype(jnp.int32)
    wide, narrow = norm_in.shape[2], query_grad.shape[2]
    big_w, small_w = wide // dps, narrow // dps
    tokens = dps * BLK
    hbm = pl.BlockSpec(memory_space=pltpu.HBM)
    norm, hand, sk_q, sk_o = (
        pltpu.with_memory_space_constraint(v[0], pltpu.HBM)
        for v in (norm_in, handed, sketch_q, sketch_o)
    )

    got_grad, got_attn = swap(query_grad[0], "tensor", 1), swap(attn_out[0], "tensor", 1)
    give = call(
        functools.partial(give_wide_kernel, dps),
        shape(BLK + RANK // dps, wide),
        (idx, norm, hand, sk_q, sk_o),
        [pltpu.SemaphoreType.DMA((1 + dps,))],
        [SMEM] + [hbm] * 4,
    )
    give, got_grad, got_attn = lax.optimization_barrier((give, got_grad, got_attn))
    smalls = call(
        functools.partial(merge_thin_kernel, dps),
        [shape(BLK, 2 * small_w)] * dps,
        (idx, query_grad[0], attn_out[0], got_grad, got_attn),
    )
    smalls = list(smalls)
    got = swap(give, "tensor", 1)
    packed = call(
        functools.partial(merge_wide_kernel, dps),
        [shape(BLK, 2 * big_w)] * dps + [shape(3 * RANK, 2 * small_w)],
        (idx, norm_in[0], handed[0], sk_q, sk_o, got),
        [pltpu.SemaphoreType.DMA((1,))],
        [SMEM, VMEM, VMEM, hbm, hbm, VMEM],
    )
    smalls = [routed(smalls[d], sizes, d, False) for d in THIN_ORDER]
    sketch = routed(packed[dps], sizes, 0, False)
    bigs = [routed(packed[d], sizes, d, True) for d in WIDE_ORDER]

    _, thin_rows, wide_rows = packed_rows(dps)

    def gram(kernel, m, rows, operands):
        m, keep, send = call(
            functools.partial(kernel, dps),
            [m, shape(rows // 2, BLK), shape(rows // 2, BLK)],
            (idx, *operands),
            [pltpu.VMEM((rows, BLK), bf16)],
        )
        return m, keep, swap(send, "tensor", 1)

    small, *thin = gram(thin_gram_kernel, shape(tokens, 2 * small_w), thin_rows, smalls)
    big, *rest = gram(
        wide_gram_kernel, shape(tokens, 2 * big_w), wide_rows, (sketch, *bigs, small)
    )
    total = thin_rows + wide_rows
    quarter = shape(total // 4, BLK)
    keep, send = call(
        add_halves_kernel,
        [quarter] * 2,
        (idx, *thin, *rest),
        [pltpu.VMEM((total // 2, BLK), bf16)],
    )
    for bit, value in ((1, send), (2, None)):
        value = swap(keep if value is None else value, "dp", bit)
        keep = call(add_kernel, quarter, (keep, value), (), [VMEM] * 2)
    beside = swap(keep, "dp", 1)
    quarters = (keep, beside, swap(keep, "tensor", 1), swap(beside, "tensor", 1))

    counts = (RANK * wide * tensors, RANK * narrow * tensors)
    whole, stays, leaves = call(
        functools.partial(chain_kernel, dps, counts),
        [shape(2 * RANK, big_w + small_w)] + [shape(RANK, big_w + small_w)] * 2,
        (idx, *quarters, big, small),
        [
            pltpu.VMEM((total, BLK), bf16),
            pltpu.VMEM((thin_rows, BLK), bf16),
            pltpu.VMEM((wide_rows, BLK), bf16),
            pltpu.VMEM((tokens, tokens), bf16),
            pltpu.VMEM((tokens, tokens), bf16),
            pltpu.VMEM((9 * RANK, 2 * RANK), f32),
        ],
    )
    leaves, stays = routed(leaves, sizes, 2, False), routed(stays, sizes, 2, False)
    near, here = routed(whole, sizes, 1, False), routed(whole, sizes, 0, False)
    leaves_on, stays_on = swap(leaves, "dp", 1), swap(stays, "dp", 1)
    mine = (here, near, stays, stays_on)
    theirs = [swap(v, "tensor", 1) for v in (here, near, leaves, leaves_on)]
    shapes = [
        shape(RANK, wide),
        shape(RANK, narrow, dtype=f32),
        shape(RANK, narrow),
        shape(RANK, wide, dtype=f32),
    ]
    widths = (big_w, small_w, small_w, big_w)
    outs = place((0, 1, 2), idx, mine[:3], theirs[:3], shapes, widths)
    outs = place((3,), idx, mine[3:], theirs[3:], shapes, widths, outs)
    return tuple(o[None] for o in outs)


def solution(mesh):
    sizes = tuple(mesh.shape[axis] for axis in ("section", "dp", "tensor"))
    _, dps, tensors = sizes

    def body(norm_in, query_grad, attn_out, handed, sketch_q, sketch_o):
        args = (norm_in, query_grad, attn_out, handed, sketch_q, sketch_o)
        fits = (
            dps == 4
            and tensors == 4
            and norm_in.shape[1] == BLK
            and sketch_q.shape[1] == RANK
            and norm_in.shape[2] == handed.shape[2]
            and query_grad.shape[2] == attn_out.shape[2]
            and norm_in.shape[2] == 2 * query_grad.shape[2]
            and query_grad.shape[2] % (dps * 128) == 0
        )
        return token_space(sizes, *args) if fits else feature_space(*args)

    return jax.shard_map(
        body,
        mesh=mesh,
        in_specs=(P("section", "dp", "tensor"),) * 4 + (P("section", None, "tensor"),) * 2,
        out_specs=(P("section", None, "tensor"),) * 4,
        check_vma=False,
    )
```
